256 devices in a mesh: blk: 16 (over x, y_hi, core), pair: 16 (over y_lo, z).
Axes of the slice: x: 4, y: 4 (y_hi: 2, y_lo: 2; y = y_hi * 2 + y_lo), z: 8, core: 2. Of those that a mesh axis runs over, the one named last changes fastest.
Arguments:
- users: float32 [131072, 256], P(('blk', 'pair')), may hold values from -1.5 to 1.5
- user_moments: float32 [131072, 256], P(('blk', 'pair')), may hold values from 0.0001 to 0.01
- ads: float32 [131072, 256], P(('blk', 'pair')), may hold values from -1.5 to 1.5
- ad_moments: float32 [131072, 256], P(('blk', 'pair')), may hold values from 0.0001 to 0.01
- pos_user: int32 [16, 16, 4, 512], P('blk'), may hold values from 0 to 511
- pos_ad: int32 [16, 16, 4, 512], P('blk'), may hold values from 0 to 511
- neg_ad: int32 [16, 16, 4, 2, 512], P('blk'), may hold values from 0 to 511
Outputs:
- users_out: float32 [131072, 256], P(('blk', 'pair'))
- user_moments_out: float32 [131072, 256], P(('blk', 'pair'))
- ads_out: float32 [131072, 256], P(('blk', 'pair'))
- ad_moments_out: float32 [131072, 256], P(('blk', 'pair'))
The draws below stay inside these ranges and needn't reach their ends.
Inputs may be any that keep to these rules, and one draw needn't show every extreme that they name: `pos_user`: a row of the user partition. `pos_ad`: a row of the ad partition met. `neg_ad`: a row of the ad partition met; repeats allowed.
All inputs are finite; a program needn't handle non-finite values.
Results may differ from the reference program's by a relative error of at most 0.00017.
Values sent between devices are 32-bit elements; how exact they have to be, the bound alone decides.
No kernel may reach another device: no remote copies, remote signals or barrier semaphores. Data moves between devices by JAX's collectives and lax.ppermute only.
A program may use at most 64 MiB of HBM per device.

```python
import math
import jax
import jax.numpy as jnp
from jax import lax

D = 256
UPART = 512
APART = 512
EDGES = 256
NEG = 512
GROUPS = 2
ROUNDS = 4
BLOCKS = 16
CYCLES = 16
PARTS_SIZE = 256


def with_ends(drawn, key, smallest, high):
    place = [jax.random.randint(jax.random.fold_in(key, axis), (), 0, length) for axis, length in enumerate(drawn.shape)]
    main_axis = drawn.shape.index(max(drawn.shape))
    neighbour = place[:main_axis] + [(place[main_axis] + 1) % drawn.shape[main_axis]] + place[main_axis + 1:]
    return drawn.at[tuple(place)].set(smallest).at[tuple(neighbour)].set(high)


def block_scale(own_key, shape, pieces, smallest, largest):
    factor_of = 1.0
    for axis_at, blocks in pieces:
        heights = jax.random.uniform(jax.random.fold_in(jax.random.fold_in(own_key, 6), axis_at), (blocks,), jnp.float32, smallest / len(pieces), largest / len(pieces))
        factor_of = factor_of * jnp.repeat(jnp.exp(heights), shape[axis_at] // blocks).reshape((-1,) + (1,) * (len(shape) - 1 - axis_at))
    return factor_of


def bell_draw(stream_key, shape, spread, reach, split=(), kind=jnp.bfloat16):
    loudness = block_scale(stream_key, shape, split, -0.22, 0.18) if split else 1.0
    drawn = jax.random.normal(stream_key, shape, jnp.float32) * spread * loudness
    return jnp.minimum(jnp.maximum(drawn, -reach), reach).astype(kind)


def setup_inputs(seed: int = 0) -> dict:
    keys = jax.random.split(jax.random.key(seed), 8)
    return {
        "users": bell_draw(keys[0], (PARTS_SIZE * UPART, D), 0.25, 1.5, ((0, 256),), jnp.float32),
        "user_moments": jnp.clip(jnp.exp(math.log(0.01) - 4.6051702 * jax.random.uniform(keys[1], (PARTS_SIZE * UPART, D), jnp.float32) ** block_scale(keys[1], (PARTS_SIZE * UPART, D), ((0, 256),), -0.2, 0.2)), 0.0001, 0.01),
        "ads": bell_draw(keys[2], (PARTS_SIZE * APART, D), 0.25, 1.5, ((0, 256),), jnp.float32),
        "ad_moments": jnp.clip(jnp.exp(math.log(0.01) - 4.6051702 * jax.random.uniform(keys[3], (PARTS_SIZE * APART, D), jnp.float32) ** block_scale(keys[3], (PARTS_SIZE * APART, D), ((0, 256),), -0.2, 0.2)), 0.0001, 0.01),
        "pos_user": with_ends(jax.random.randint(keys[4], (BLOCKS, CYCLES, ROUNDS, GROUPS * EDGES), 0, UPART), jax.random.fold_in(keys[4], 1), 0, UPART - 1).astype(jnp.int32),
        "pos_ad": with_ends(jax.random.randint(keys[5], (BLOCKS, CYCLES, ROUNDS, GROUPS * EDGES), 0, APART), jax.random.fold_in(keys[5], 1), 0, APART - 1).astype(jnp.int32),
        "neg_ad": with_ends(jax.random.randint(keys[6], (BLOCKS, CYCLES, ROUNDS, GROUPS, NEG), 0, APART), jax.random.fold_in(keys[6], 1), 0, APART - 1).astype(jnp.int32),
    }


learn_rate = 0.1
adagrad_eps = 1e-08

def group_update(users, user_moms, ads, ad_moms, pos_u, pos_a, negs):
    hi = lax.Precision.HIGHEST
    neg_scale = 1.0 / jnp.sqrt(jnp.float32(negs.shape[0]))
    u_rows = users[pos_u]
    a_rows = ads[pos_a]
    n_rows = ads[negs]
    s_pos = lax.optimization_barrier(jnp.sum(u_rows * a_rows, axis=1))
    s_neg = jnp.dot(u_rows, n_rows.T, precision=hi, preferred_element_type=jnp.float32)
    g_pos = -jax.nn.sigmoid(-s_pos)
    g_neg = jax.nn.sigmoid(s_neg) * neg_scale
    user_terms = g_pos[:, None] * a_rows + jnp.dot(g_neg, n_rows, precision=hi, preferred_element_type=jnp.float32)
    pos_terms = g_pos[:, None] * u_rows
    neg_terms = jnp.dot(g_neg.T, u_rows, precision=hi, preferred_element_type=jnp.float32)
    grad_user = jnp.zeros_like(users).at[pos_u].add(user_terms)
    grad_ad = jnp.zeros_like(ads).at[pos_a].add(pos_terms).at[negs].add(neg_terms)
    user_moms = user_moms + grad_user * grad_user
    users = users - learn_rate * grad_user / (jnp.sqrt(user_moms) + adagrad_eps)
    ad_moms = ad_moms + grad_ad * grad_ad
    ads = ads - learn_rate * grad_ad / (jnp.sqrt(ad_moms) + adagrad_eps)
    return (users, user_moms, ads, ad_moms)

def meeting(packed):
    users, user_moms, ads, ad_moms, pos_u, pos_a, negs = packed
    edges_group = pos_u.shape[0] // GROUPS
    for group in range(GROUPS):
        users, user_moms, ads, ad_moms = group_update(users, user_moms, ads, ad_moms, pos_u[group * edges_group:(group + 1) * edges_group], pos_a[group * edges_group:(group + 1) * edges_group], negs[group])
    return (users, user_moms, ads, ad_moms)

def reference(users, user_moments, ads, ad_moments, pos_user, pos_ad, neg_ad):
    half_cycle = CYCLES // 2
    user_grid = users.reshape(BLOCKS, CYCLES, UPART, D)
    umom_grid = user_moments.reshape(BLOCKS, CYCLES, UPART, D)
    ad_grid = ads.reshape(BLOCKS, CYCLES, APART, D)
    amom_grid = ad_moments.reshape(BLOCKS, CYCLES, APART, D)
    for rnd in range(ROUNDS):
        offset = half_cycle if rnd >= ROUNDS // 2 else 0
        user_view = jnp.roll(user_grid, -offset, axis=1).reshape(PARTS_SIZE, UPART, D)
        umom_view = jnp.roll(umom_grid, -offset, axis=1).reshape(PARTS_SIZE, UPART, D)
        ad_view = jnp.roll(ad_grid, rnd, axis=0).reshape(PARTS_SIZE, APART, D)
        amom_view = jnp.roll(amom_grid, rnd, axis=0).reshape(PARTS_SIZE, APART, D)
        pos_u = jnp.roll(pos_user[:, :, rnd], -offset, axis=1).reshape(PARTS_SIZE, GROUPS * EDGES)
        pos_a = jnp.roll(pos_ad[:, :, rnd], -offset, axis=1).reshape(PARTS_SIZE, GROUPS * EDGES)
        negs = jnp.roll(neg_ad[:, :, rnd], -offset, axis=1).reshape(PARTS_SIZE, GROUPS, NEG)
        user_view, umom_view, ad_view, amom_view = lax.map(meeting, (user_view, umom_view, ad_view, amom_view, pos_u, pos_a, negs))
        user_grid = jnp.roll(user_view.reshape(BLOCKS, CYCLES, UPART, D), offset, axis=1)
        umom_grid = jnp.roll(umom_view.reshape(BLOCKS, CYCLES, UPART, D), offset, axis=1)
        ad_grid = jnp.roll(ad_view.reshape(BLOCKS, CYCLES, APART, D), -rnd, axis=0)
        amom_grid = jnp.roll(amom_view.reshape(BLOCKS, CYCLES, APART, D), -rnd, axis=0)
    return (user_grid.reshape(PARTS_SIZE * UPART, D), umom_grid.reshape(PARTS_SIZE * UPART, D), ad_grid.reshape(PARTS_SIZE * APART, D), amom_grid.reshape(PARTS_SIZE * APART, D))
```

```python
import functools

import jax
import jax.numpy as jnp
from jax import lax
from jax.experimental import pallas as pl
from jax.experimental.pallas import tpu as pltpu
from jax.sharding import PartitionSpec as P

LEARN_RATE = 0.1
EPS = 1e-08
F32 = jnp.float32
BF16 = jnp.bfloat16
AXES = ("blk", "pair")
VMEM_LIMIT = 28 * 1024 * 1024


def dot(a, b, ca, cb):
    return lax.dot_general(a, b, (((ca,), (cb,)), ((), ())), preferred_element_type=F32)


def split(x):
    hi = x.astype(BF16)
    return hi, (x - hi.astype(F32)).astype(BF16)


def dot3(a, b, ca, cb):
    (ah, al), (bh, bl) = a, b
    return dot(ah, bh, ca, cb) + (dot(ah, bl, ca, cb) + dot(al, bh, ca, cb))


def adagrad(row, mom, grad):
    mom = mom + grad * grad
    return row - LEARN_RATE * grad / (jnp.sqrt(mom) + EPS), mom


def onehot(idx, count):
    rows = lax.broadcasted_iota(jnp.int32, (count, idx.shape[1]), 0)
    return jnp.where(rows == idx, F32(1), F32(0)).astype(BF16)


def prepare(group, pu, pa, ng, users, ads, mh_ref, cu_ref, cn_ref):
    n = ng.shape[1]
    hot_u = onehot(pu, users)
    hot_a = onehot(pa, ads)
    mh_ref[group] = (0.5 * dot(hot_u, hot_a, 1, 1)).astype(BF16)
    ones = jnp.ones((pu.shape[1], 128), BF16)
    cu_ref[group] = dot(hot_u, ones, 1, 0) * F32(0.5 / n**0.5)
    cn_ref[group] = dot(jnp.ones((8, n), BF16), onehot(ng, ads), 1, 1)


def gradient_matrix(u_hl, at_hl, mh, cu, cn):
    s = dot3(u_hl, at_hl, 1, 0)
    t = jnp.tanh(0.5 * s)
    w = jnp.concatenate([cu] * (s.shape[1] // 128), axis=1) * cn
    m = mh.astype(F32)
    return split((w + m) * t + (w - m))


BLOCK = 256


def group_pass(group, u_ref, at_hl, prep, gu_out, g_out=None):
    mh_ref, cu_ref, cn_ref = prep
    cn = cn_ref[group, 0:1, :]
    ga = None
    for r in range(0, u_ref.shape[0], BLOCK):
        rows = pl.ds(r, BLOCK)
        u_hl = split(u_ref[rows, :])
        g_hl = gradient_matrix(u_hl, at_hl, mh_ref[group, rows, :], cu_ref[group, rows, :], cn)
        part = dot3(u_hl, g_hl, 0, 0)
        ga = part if ga is None else ga + part
        if g_out is None:
            gu_out(rows, dot3(g_hl, at_hl, 1, 1))
        else:
            g_out[0][rows, :], g_out[1][rows, :] = g_hl
    return ga


def update_users(u_ref, um_ref, uo_ref, umo_ref):
    def put(rows, grad):
        uo_ref[rows, :], umo_ref[rows, :] = adagrad(u_ref[rows, :], um_ref[rows, :], grad)

    return put


def fetch_indices(pu_hbm, pa_hbm, ng_hbm, pu, pa, ng, sems):
    cycle = lax.axis_index("pair")
    copies = [
        pltpu.make_async_copy(src.at[0, cycle], dst, sems.at[k])
        for k, (src, dst) in enumerate(((pu_hbm, pu), (pa_hbm, pa), (ng_hbm, ng)))
    ]
    for c in copies:
        c.start()
    return copies


def prepare_round(rnd, pu, pa, ng, users, ads, prep):
    groups = ng.shape[1]
    edges = pu.shape[1] // groups
    for g in range(groups):
        cols = pl.ds(g * edges, edges)
        prepare(g, pu[rnd : rnd + 1, cols], pa[rnd : rnd + 1, cols], ng[rnd, g : g + 1, :], users, ads, *prep)


def second_group(u_ref, at1, amt1, ato_ref, amto_ref, prep, gh_ref, gl_ref, ah_ref, al_ref):
    at_hl = split(at1)
    ah_ref[...], al_ref[...] = at_hl
    ga = group_pass(1, u_ref, at_hl, prep, None, (gh_ref, gl_ref))
    ato_ref[...], amto_ref[...] = adagrad(at1, amt1, ga)


def first_round_kernel(
    u_ref, um_ref, a_ref, am_ref, pu_hbm, pa_hbm, ng_hbm,
    uo_ref, umo_ref, ato_ref, amto_ref, gh_ref, gl_ref, ah_ref, al_ref,
    pu, pa, ng, mh, cu, cn, sems,
):
    copies = fetch_indices(pu_hbm, pa_hbm, ng_hbm, pu, pa, ng, sems)
    at = a_ref[...].T
    amt = am_ref[...].T
    for c in copies:
        c.wait()
    prep = (mh, cu, cn)
    prepare_round(0, pu, pa, ng, u_ref.shape[0], a_ref.shape[0], prep)
    ga = group_pass(0, u_ref, split(at), prep, update_users(u_ref, um_ref, uo_ref, umo_ref))
    at1, amt1 = adagrad(at, amt, ga)
    second_group(uo_ref, at1, amt1, ato_ref, amto_ref, prep, gh_ref, gl_ref, ah_ref, al_ref)


def embedding_kernel(u_ref, um_ref, at_ref, mh, cu, cn, uo_ref, umo_ref, ga_ref):
    put = update_users(u_ref, um_ref, uo_ref, umo_ref)
    ga_ref[...] = group_pass(0, u_ref, split(at_ref[...]), (mh, cu, cn), put)


def moment_kernel(
    u_ref, at_ref, amt_ref, ga_ref, mh, cu, cn,
    ato_ref, amto_ref, gh_ref, gl_ref, ah_ref, al_ref,
):
    at1, amt1 = adagrad(at_ref[...], amt_ref[...], ga_ref[...])
    second_group(u_ref, at1, amt1, ato_ref, amto_ref, (mh, cu, cn), gh_ref, gl_ref, ah_ref, al_ref)


def users_body(u_ref, um_ref, gh_ref, gl_ref, ah_ref, al_ref, uo_ref, umo_ref):
    put = update_users(u_ref, um_ref, uo_ref, umo_ref)
    at_hl = ah_ref[...], al_ref[...]
    for r in range(0, u_ref.shape[0], BLOCK):
        rows = pl.ds(r, BLOCK)
        put(rows, dot3((gh_ref[rows, :], gl_ref[rows, :]), at_hl, 1, 1))


def users_kernel(
    rnd, u_ref, um_ref, gh_ref, gl_ref, ah_ref, al_ref, pu_hbm, pa_hbm, ng_hbm,
    uo_ref, umo_ref, mh, cu, cn, pu, pa, ng, sems,
):
    copies = fetch_indices(pu_hbm, pa_hbm, ng_hbm, pu, pa, ng, sems)
    users_body(u_ref, um_ref, gh_ref, gl_ref, ah_ref, al_ref, uo_ref, umo_ref)
    for c in copies:
        c.wait()
    prepare_round(rnd, pu, pa, ng, u_ref.shape[0], ah_ref.shape[1], (mh, cu, cn))


def last_users_kernel(u_ref, um_ref, gh_ref, gl_ref, ah_ref, al_ref, uo_ref, umo_ref):
    users_body(u_ref, um_ref, gh_ref, gl_ref, ah_ref, al_ref, uo_ref, umo_ref)


def call(kernel, ins, outs, scratch=(), hbm=0, macs=0, name=None):
    vmem = pl.BlockSpec(memory_space=pltpu.VMEM)
    places = [vmem] * (len(ins) - hbm) + [pl.BlockSpec(memory_space=pl.ANY)] * hbm
    size = sum(x.size * x.dtype.itemsize for x in [*ins[: len(ins) - hbm], *outs])
    return pl.pallas_call(
        kernel,
        out_shape=outs,
        in_specs=places,
        out_specs=[vmem] * len(outs),
        scratch_shapes=list(scratch),
        compiler_params=pltpu.CompilerParams(vmem_limit_bytes=VMEM_LIMIT),
        cost_estimate=pl.CostEstimate(flops=2 * macs, bytes_accessed=size, transcendentals=0),
        name=name,
    )(*ins)


def move(x, steps, flip):
    blocks, cycles = lax.axis_size("blk"), lax.axis_size("pair")
    route = []
    for b in range(blocks):
        for p in range(cycles):
            to = (b + steps) % blocks, p ^ (cycles // 2 if flip else 0)
            route.append((b * cycles + p, to[0] * cycles + to[1]))
    return lax.ppermute(x, AXES, route)


def local(users, user_moms, ads, ad_moms, pos_user, pos_ad, neg_ad):
    nu, d = users.shape
    na = ads.shape[0]
    rounds, groups, n = neg_ad.shape[2:]
    edges = pos_user.shape[3]
    indices = (pos_user, pos_ad, neg_ad)

    def shape(*dims, dtype=F32):
        return jax.ShapeDtypeStruct(dims, dtype)

    table_u, table_a = shape(nu, d), shape(d, na)
    part_g, part_a = shape(nu, na, dtype=BF16), shape(d, na, dtype=BF16)
    index_scratch = [
        pltpu.VMEM((rounds, edges), jnp.int32),
        pltpu.VMEM((rounds, edges), jnp.int32),
        pltpu.VMEM((rounds, groups, n), jnp.int32),
    ]
    sems = pltpu.SemaphoreType.DMA((3,))
    prep_shapes = [shape(groups, nu, na, dtype=BF16), shape(groups, nu, 128), shape(groups, 8, na)]
    prep_scratch = [pltpu.VMEM(s.shape, s.dtype) for s in prep_shapes]
    product = 3 * nu * na * d

    u, um, at, amt, *g = call(
        first_round_kernel,
        (users, user_moms, ads, ad_moms, *indices),
        [table_u, table_u, table_a, table_a, part_g, part_g, part_a, part_a],
        [*index_scratch, *prep_scratch, sems], hbm=3, macs=5 * product, name="round_first",
    )
    for rnd in range(1, rounds):
        flip = rnd == rounds // 2
        at = move(at, 1, flip)
        amt = move(amt, 1, flip)
        u, um, *prep = call(
            functools.partial(users_kernel, rnd),
            (u, um, *g, *indices),
            [table_u, table_u, *prep_shapes],
            [*index_scratch, sems], hbm=3, macs=product, name="users_prepare",
        )
        u, um, ga = call(
            embedding_kernel, (u, um, at, *prep), [table_u, table_u, table_a], macs=3 * product, name="group_first",
        )
        at, amt, *g = call(
            moment_kernel, (u, at, amt, ga, *prep), [table_a, table_a, part_g, part_g, part_a, part_a],
            macs=2 * product, name="group_second",
        )
    a = move(at, 1 - rounds, True)
    am = move(amt, 1 - rounds, True)
    u, um = call(last_users_kernel, (u, um, *g), [table_u, table_u], macs=product, name="users_last")
    return u, um, a.T, am.T


def solution(mesh):
    rows = P(AXES, None)
    return jax.shard_map(
        local,
        mesh=mesh,
        in_specs=(rows, rows, rows, rows, P("blk", None, None, None), P("blk", None, None, None), P("blk", None, None, None, None)),
        out_specs=(rows, rows, rows, rows),
        check_vma=False,
    )
```

```python
import functools
import math

import jax
import jax.numpy as jnp
from jax import lax
from jax.experimental import pallas as pl
from jax.experimental.pallas import tpu as pltpu
from jax.sharding import PartitionSpec as P

LEARN_RATE = 0.1
EPS = 1e-08
F32 = jnp.float32
BF16 = jnp.bfloat16
AXES = ("blk", "pair")
VMEM_LIMIT = 28 * 1024 * 1024


def dot(a, b, ca, cb):
    return lax.dot_general(a, b, (((ca,), (cb,)), ((), ())), preferred_element_type=F32)


def split(x):
    hi = x.astype(BF16)
    return hi, (x - hi.astype(F32)).astype(BF16)


def dot3(a, b, ca, cb):
    (ah, al), (bh, bl) = a, b
    return dot(ah, bh, ca, cb) + (dot(ah, bl, ca, cb) + dot(al, bh, ca, cb))


def adagrad(row, mom, grad):
    mom = mom + grad * grad
    return row - LEARN_RATE * grad / (jnp.sqrt(mom) + EPS), mom


def onehot(idx, count):
    rows = lax.broadcasted_iota(jnp.int32, (count, idx.shape[1]), 0)
    return jnp.where(rows == idx, F32(1), F32(0)).astype(BF16)


def prepare(group, pu, pa, ng, users, ads, mh_ref, cu_ref, cn_ref):
    n = ng.shape[1]
    hot_u = onehot(pu, users)
    hot_a = onehot(pa, ads)
    mh_ref[group] = (0.5 * dot(hot_u, hot_a, 1, 1)).astype(BF16)
    ones = jnp.ones((pu.shape[1], 128), BF16)
    cu_ref[group] = dot(hot_u, ones, 1, 0) * F32(0.5 / n**0.5)
    cn_ref[group] = dot(jnp.ones((8, n), BF16), onehot(ng, ads), 1, 1)


def gradient_matrix(u_hl, at_hl, mh, cu, cn):
    s = dot3(u_hl, at_hl, 1, 0)
    t = jnp.tanh(0.5 * s)
    w = jnp.concatenate([cu] * (s.shape[1] // 128), axis=1) * cn
    m = mh.astype(F32)
    return split((w + m) * t + (w - m))


BLOCK = 256


def group_pass(group, u_ref, at_hl, prep, gu_out, g_out=None):
    mh_ref, cu_ref, cn_ref = prep
    cn = cn_ref[group, 0:1, :]
    ga = None
    for r in range(0, u_ref.shape[0], BLOCK):
        rows = pl.ds(r, BLOCK)
        u_hl = split(u_ref[rows, :])
        g_hl = gradient_matrix(u_hl, at_hl, mh_ref[group, rows, :], cu_ref[group, rows, :], cn)
        part = dot3(u_hl, g_hl, 0, 0)
        ga = part if ga is None else ga + part
        if g_out is None:
            gu_out(rows, dot3(g_hl, at_hl, 1, 1))
        else:
            g_out[0][rows, :], g_out[1][rows, :] = g_hl
    return ga


def update_users(u_ref, um_ref, uo_ref, umo_ref):
    def put(rows, grad):
        uo_ref[rows, :], umo_ref[rows, :] = adagrad(u_ref[rows, :], um_ref[rows, :], grad)

    return put


def fetch_indices(pu_hbm, pa_hbm, ng_hbm, pu, pa, ng, sems):
    cycle = lax.axis_index("pair")
    copies = [
        pltpu.make_async_copy(src.at[0, cycle], dst, sems.at[k])
        for k, (src, dst) in enumerate(((pu_hbm, pu), (pa_hbm, pa), (ng_hbm, ng)))
    ]
    for c in copies:
        c.start()
    return copies


def prepare_round(rnd, pu, pa, ng, users, ads, prep):
    groups = ng.shape[1]
    edges = pu.shape[1] // groups
    for g in range(groups):
        cols = pl.ds(g * edges, edges)
        prepare(g, pu[rnd : rnd + 1, cols], pa[rnd : rnd + 1, cols], ng[rnd, g : g + 1, :], users, ads, *prep)


def second_group(u_ref, at1, amt1, ato_ref, amto_ref, prep, gh_ref, gl_ref, ah_ref, al_ref):
    at_hl = split(at1)
    ah_ref[...], al_ref[...] = at_hl
    ga = group_pass(1, u_ref, at_hl, prep, None, (gh_ref, gl_ref))
    ato_ref[...], amto_ref[...] = adagrad(at1, amt1, ga)


def first_round_kernel(
    pu_hbm, pa_hbm, ng_hbm, u_hbm, a_hbm, um_hbm, am_hbm,
    uo_ref, umo_ref, ato_ref, amto_ref, gh_ref, gl_ref, ah_ref, al_ref,
    pu, pa, ng, mh, cu, cn, u_ref, um_ref, a_ref, am_ref, sems, table_sems,
):
    copies = fetch_indices(pu_hbm, pa_hbm, ng_hbm, pu, pa, ng, sems)
    tables = [
        pltpu.make_async_copy(src, dst, table_sems.at[k])
        for k, (src, dst) in enumerate(
            ((u_hbm, u_ref), (a_hbm, a_ref), (um_hbm, um_ref), (am_hbm, am_ref))
        )
    ]
    for c in tables:
        c.start()
    for c in copies:
        c.wait()
    prep = (mh, cu, cn)
    prepare_round(0, pu, pa, ng, u_ref.shape[0], a_ref.shape[0], prep)
    for c in tables:
        c.wait()
    at = a_ref[...].T
    amt = am_ref[...].T
    ga = group_pass(0, u_ref, split(at), prep, update_users(u_ref, um_ref, uo_ref, umo_ref))
    at1, amt1 = adagrad(at, amt, ga)
    second_group(uo_ref, at1, amt1, ato_ref, amto_ref, prep, gh_ref, gl_ref, ah_ref, al_ref)


def embedding_kernel(u_ref, um_ref, at_ref, mh, cu, cn, uo_ref, umo_ref, ga_ref):
    put = update_users(u_ref, um_ref, uo_ref, umo_ref)
    ga_ref[...] = group_pass(0, u_ref, split(at_ref[...]), (mh, cu, cn), put)


def moment_kernel(
    u_ref, at_ref, amt_ref, ga_ref, mh, cu, cn,
    ato_ref, amto_ref, gh_ref, gl_ref, ah_ref, al_ref,
):
    at1, amt1 = adagrad(at_ref[...], amt_ref[...], ga_ref[...])
    second_group(u_ref, at1, amt1, ato_ref, amto_ref, (mh, cu, cn), gh_ref, gl_ref, ah_ref, al_ref)


def users_body(u_ref, um_ref, gh_ref, gl_ref, ah_ref, al_ref, uo_ref, umo_ref):
    put = update_users(u_ref, um_ref, uo_ref, umo_ref)
    at_hl = ah_ref[...], al_ref[...]
    for r in range(0, u_ref.shape[0], BLOCK):
        rows = pl.ds(r, BLOCK)
        put(rows, dot3((gh_ref[rows, :], gl_ref[rows, :]), at_hl, 1, 1))


def users_kernel(
    rnd, u_ref, um_ref, gh_ref, gl_ref, ah_ref, al_ref, pu_hbm, pa_hbm, ng_hbm,
    uo_ref, umo_ref, mh, cu, cn, pu, pa, ng, sems,
):
    copies = fetch_indices(pu_hbm, pa_hbm, ng_hbm, pu, pa, ng, sems)
    users_body(u_ref, um_ref, gh_ref, gl_ref, ah_ref, al_ref, uo_ref, umo_ref)
    for c in copies:
        c.wait()
    prepare_round(rnd, pu, pa, ng, u_ref.shape[0], ah_ref.shape[1], (mh, cu, cn))


def last_users_kernel(u_ref, um_ref, gh_ref, gl_ref, ah_ref, al_ref, uo_hbm, umo_hbm, uo_ref, umo_ref, sems):
    users_body(u_ref, um_ref, gh_ref, gl_ref, ah_ref, al_ref, uo_ref, umo_ref)
    copies = [
        pltpu.make_async_copy(uo_ref, uo_hbm, sems.at[0]),
        pltpu.make_async_copy(umo_ref, umo_hbm, sems.at[1]),
    ]
    for c in copies:
        c.start()
    for c in copies:
        c.wait()


def call(kernel, ins, outs, scratch=(), hbm=0, macs=0, name=None, out_place=pltpu.VMEM):
    vmem = pl.BlockSpec(memory_space=pltpu.VMEM)
    places = [vmem] * (len(ins) - hbm) + [pl.BlockSpec(memory_space=pltpu.HBM)] * hbm
    size = sum(math.prod(x.shape) * x.dtype.itemsize for x in [*ins[: len(ins) - hbm], *outs])
    return pl.pallas_call(
        kernel,
        out_shape=outs,
        in_specs=places,
        out_specs=[pl.BlockSpec(memory_space=out_place)] * len(outs),
        scratch_shapes=list(scratch),
        compiler_params=pltpu.CompilerParams(vmem_limit_bytes=VMEM_LIMIT),
        cost_estimate=pl.CostEstimate(flops=2 * macs, bytes_accessed=size, transcendentals=0),
        name=name,
    )(*ins[: len(ins) - hbm], *(pltpu.with_memory_space_constraint(x, pltpu.HBM) for x in ins[len(ins) - hbm :]))


def finish_kernel(xt_ref, out_hbm, x_ref, sems):
    count = sems.shape[0]
    size = x_ref.shape[0] // count
    copies = []
    for k in range(count):
        rows = pl.ds(k * size, size)
        x_ref[rows, :] = xt_ref[:, rows].T
        copies.append(pltpu.make_async_copy(x_ref.at[rows, :], out_hbm.at[rows, :], sems.at[k]))
        copies[-1].start()
    for c in copies:
        c.wait()


def finish(xt):
    d, rows = xt.shape
    return pl.pallas_call(
        finish_kernel,
        out_shape=pltpu.HBM((rows, d), xt.dtype),
        in_specs=[pl.BlockSpec(memory_space=pltpu.VMEM)],
        out_specs=pl.BlockSpec(memory_space=pltpu.HBM),
        scratch_shapes=[pltpu.VMEM((rows, d), xt.dtype), pltpu.SemaphoreType.DMA((4,))],
        compiler_params=pltpu.CompilerParams(vmem_limit_bytes=VMEM_LIMIT),
        cost_estimate=pl.CostEstimate(flops=0, bytes_accessed=2 * xt.size * 4, transcendentals=0),
        name="ads_out",
    )(xt)


def move(x, steps, flip):
    blocks, cycles = lax.axis_size("blk"), lax.axis_size("pair")
    route = []
    for b in range(blocks):
        for p in range(cycles):
            to = (b + steps) % blocks, p ^ (cycles // 2 if flip else 0)
            route.append((b * cycles + p, to[0] * cycles + to[1]))
    return lax.ppermute(x, AXES, route)


def local(users, user_moms, ads, ad_moms, pos_user, pos_ad, neg_ad):
    nu, d = users.shape
    na = ads.shape[0]
    rounds, groups, n = neg_ad.shape[2:]
    edges = pos_user.shape[3]
    indices = (pos_user, pos_ad, neg_ad)

    def shape(*dims, dtype=F32):
        return jax.ShapeDtypeStruct(dims, dtype)

    table_u, table_a = shape(nu, d), shape(d, na)
    part_g, part_a = shape(nu, na, dtype=BF16), shape(d, na, dtype=BF16)
    index_scratch = [
        pltpu.VMEM((rounds, edges), jnp.int32),
        pltpu.VMEM((rounds, edges), jnp.int32),
        pltpu.VMEM((rounds, groups, n), jnp.int32),
    ]
    sems = pltpu.SemaphoreType.DMA((3,))
    prep_shapes = [shape(groups, nu, na, dtype=BF16), shape(groups, nu, 128), shape(groups, 8, na)]
    prep_scratch = [pltpu.VMEM(s.shape, s.dtype) for s in prep_shapes]
    product = 3 * nu * na * d

    u, um, at, amt, *g = call(
        first_round_kernel,
        (*indices, users, ads, user_moms, ad_moms),
        [table_u, table_u, table_a, table_a, part_g, part_g, part_a, part_a],
        [*index_scratch, *prep_scratch, *[pltpu.VMEM((nu, d), F32)] * 2, *[pltpu.VMEM((na, d), F32)] * 2, sems, pltpu.SemaphoreType.DMA((4,))],
        hbm=7, macs=5 * product, name="round_first",
    )
    for rnd in range(1, rounds):
        flip = rnd == rounds // 2
        at = move(at, 1, flip)
        amt = move(amt, 1, flip)
        u, um, *prep = call(
            functools.partial(users_kernel, rnd),
            (u, um, *g, *indices),
            [table_u, table_u, *prep_shapes],
            [*index_scratch, sems], hbm=3, macs=product, name="users_prepare",
        )
        u, um, ga = call(
            embedding_kernel, (u, um, at, *prep), [table_u, table_u, table_a], macs=3 * product, name="group_first",
        )
        at, amt, *g = call(
            moment_kernel, (u, at, amt, ga, *prep), [table_a, table_a, part_g, part_g, part_a, part_a],
            macs=2 * product, name="group_second",
        )
    a = finish(move(at, 1 - rounds, True))
    am = finish(move(amt, 1 - rounds, True))
    u, um = call(
        last_users_kernel, (u, um, *g), [pltpu.HBM((nu, d), F32)] * 2,
        [pltpu.VMEM((nu, d), F32)] * 2 + [pltpu.SemaphoreType.DMA((2,))], macs=product, name="users_last", out_place=pltpu.HBM,
    )
    return u, um, a, am


def solution(mesh):
    rows = P(AXES, None)
    return jax.shard_map(
        local,
        mesh=mesh,
        in_specs=(rows, rows, rows, rows, P("blk", None, None, None), P("blk", None, None, None), P("blk", None, None, None, None)),
        out_specs=(rows, rows, rows, rows),
        check_vma=False,
    )
```

```python
import functools

import jax
import jax.numpy as jnp
from jax import lax
from jax.experimental import pallas as pl
from jax.experimental.pallas import tpu as pltpu
from jax.sharding import PartitionSpec as P

LEARN_RATE = 0.1
EPS = 1e-08
F32 = jnp.float32
BF16 = jnp.bfloat16
AXES = ("blk", "pair")
VMEM_LIMIT = 28 * 1024 * 1024


def dot(a, b, ca, cb):
    return lax.dot_general(a, b, (((ca,), (cb,)), ((), ())), preferred_element_type=F32)


def split(x):
    hi = x.astype(BF16)
    return hi, (x - hi.astype(F32)).astype(BF16)


def dot3(a, b, ca, cb):
    (ah, al), (bh, bl) = a, b
    return dot(ah, bh, ca, cb) + (dot(ah, bl, ca, cb) + dot(al, bh, ca, cb))


def adagrad(row, mom, grad):
    mom = mom + grad * grad
    return row - LEARN_RATE * grad / (jnp.sqrt(mom) + EPS), mom


def onehot(idx, count):
    rows = lax.broadcasted_iota(jnp.int32, (count, idx.shape[1]), 0)
    return jnp.where(rows == idx, F32(1), F32(0)).astype(BF16)


def prepare(group, pu, pa, ng, users, ads, mh_ref, cu_ref, cn_ref):
    n = ng.shape[1]
    hot_u = onehot(pu, users)
    hot_a = onehot(pa, ads)
    mh_ref[group] = (0.5 * dot(hot_u, hot_a, 1, 1)).astype(BF16)
    ones = jnp.ones((pu.shape[1], 128), BF16)
    cu_ref[group] = dot(hot_u, ones, 1, 0) * F32(0.5 / n**0.5)
    cn_ref[group] = dot(jnp.ones((8, n), BF16), onehot(ng, ads), 1, 1)


def gradient_matrix(u_hl, at_hl, mh, cu, cn):
    s = dot3(u_hl, at_hl, 1, 0)
    t = jnp.tanh(0.5 * s)
    w = jnp.concatenate([cu] * (s.shape[1] // 128), axis=1) * cn
    m = mh.astype(F32)
    return split((w + m) * t + (w - m))


BLOCK = 256


def group_pass(group, u_read, users, at_hl, prep, gu_out, g_out=None):
    mh_ref, cu_ref, cn_ref = prep
    cn = cn_ref[group, 0:1, :]
    ga = None
    for r in range(0, users, BLOCK):
        rows = pl.ds(r, BLOCK)
        u_hl = split(u_read(rows))
        g_hl = gradient_matrix(u_hl, at_hl, mh_ref[group, rows, :], cu_ref[group, rows, :], cn)
        part = dot3(u_hl, g_hl, 0, 0)
        ga = part if ga is None else ga + part
        if g_out is None:
            gu_out(rows, dot3(g_hl, at_hl, 1, 1))
        else:
            g_out[0][rows, :], g_out[1][rows, :] = g_hl
    return ga


def reader(ref):
    return lambda rows: ref[rows, :]


def picker(odd, even_ref, odd_ref):
    return lambda rows: jnp.where(odd, odd_ref[rows, :], even_ref[rows, :])


def update_users(u_read, um_read, uo_ref, umo_ref):
    def put(rows, grad):
        uo_ref[rows, :], umo_ref[rows, :] = adagrad(u_read(rows), um_read(rows), grad)

    return put


def on_odd_core():
    return lax.rem(lax.axis_index("blk"), 2) == 1


def fetch_indices(pu_hbm, pa_hbm, ng_hbm, pu, pa, ng, sems, away=False):
    cycle = lax.axis_index("pair")
    if away:
        count = lax.axis_size("pair")
        cycle = lax.rem(cycle + jnp.where(on_odd_core(), count // 2, 0), count)
    copies = [
        pltpu.make_async_copy(src.at[0, cycle], dst, sems.at[k])
        for k, (src, dst) in enumerate(((pu_hbm, pu), (pa_hbm, pa), (ng_hbm, ng)))
    ]
    for c in copies:
        c.start()
    return copies


def prepare_round(rnd, pu, pa, ng, users, ads, prep):
    groups = ng.shape[1]
    edges = pu.shape[1] // groups
    for g in range(groups):
        cols = pl.ds(g * edges, edges)
        prepare(g, pu[rnd : rnd + 1, cols], pa[rnd : rnd + 1, cols], ng[rnd, g : g + 1, :], users, ads, *prep)


def second_group(u_ref, at1, amt1, ato_ref, amto_ref, prep, gh_ref, gl_ref, ah_ref, al_ref):
    at_hl = split(at1)
    ah_ref[...], al_ref[...] = at_hl
    ga = group_pass(1, reader(u_ref), u_ref.shape[0], at_hl, prep, None, (gh_ref, gl_ref))
    ato_ref[...], amto_ref[...] = adagrad(at1, amt1, ga)


def first_round_kernel(
    pu_hbm, pa_hbm, ng_hbm, u_hbm, a_hbm, um_hbm, am_hbm,
    uo_ref, umo_ref, ato_ref, amto_ref, gh_ref, gl_ref, ah_ref, al_ref,
    pu, pa, ng, mh, cu, cn, u_ref, um_ref, a_ref, am_ref, sems, table_sems,
):
    copies = fetch_indices(pu_hbm, pa_hbm, ng_hbm, pu, pa, ng, sems)
    tables = [
        pltpu.make_async_copy(src, dst, table_sems.at[k])
        for k, (src, dst) in enumerate(
            ((u_hbm, u_ref), (a_hbm, a_ref), (um_hbm, um_ref), (am_hbm, am_ref))
        )
    ]
    for c in tables:
        c.start()
    for c in copies:
        c.wait()
    prep = (mh, cu, cn)
    prepare_round(0, pu, pa, ng, u_ref.shape[0], a_ref.shape[0], prep)
    for c in tables:
        c.wait()
    at = a_ref[...].T
    amt = am_ref[...].T
    put = update_users(reader(u_ref), reader(um_ref), uo_ref, umo_ref)
    ga = group_pass(0, reader(u_ref), u_ref.shape[0], split(at), prep, put)
    at1, amt1 = adagrad(at, amt, ga)
    second_group(uo_ref, at1, amt1, ato_ref, amto_ref, prep, gh_ref, gl_ref, ah_ref, al_ref)


def embedding_kernel(u_ref, um_ref, at_ref, mh, cu, cn, *refs):
    uo_ref, umo_ref, ga_ref = refs[-3:]
    u_read = reader(u_ref)
    put = update_users(u_read, reader(um_ref), uo_ref, umo_ref)
    ga_ref[...] = group_pass(0, u_read, u_ref.shape[0], split(at_ref[...]), (mh, cu, cn), put)


def moment_kernel(
    u_ref, at_ref, amt_ref, ga_ref, mh, cu, cn,
    ato_ref, amto_ref, gh_ref, gl_ref, ah_ref, al_ref,
):
    at1, amt1 = adagrad(at_ref[...], amt_ref[...], ga_ref[...])
    second_group(u_ref, at1, amt1, ato_ref, amto_ref, (mh, cu, cn), gh_ref, gl_ref, ah_ref, al_ref)


def moment_pair_kernel(u_ref, at_ref, amt_ref, ga_ref, mh, cu, cn, ads_ref, *parts):
    moment_kernel(u_ref, at_ref, amt_ref, ga_ref, mh, cu, cn, ads_ref.at[0], ads_ref.at[1], *parts)


def embedding_pick_kernel(ue_ref, ume_ref, users_ref, ads_ref, ato_ref, mh, cu, cn, un_ref, umn_ref, ga_ref):
    odd = on_odd_core()
    u_read = picker(odd, ue_ref, users_ref.at[0])
    put = update_users(u_read, picker(odd, ume_ref, users_ref.at[1]), un_ref, umn_ref)
    at = jnp.where(odd, ato_ref[...], ads_ref[0])
    ga_ref[...] = group_pass(0, u_read, ue_ref.shape[0], split(at), (mh, cu, cn), put)


def moment_pick_kernel(
    u_ref, ads_ref, ato_ref, amto_ref, ga_ref, mh, cu, cn,
    atn_ref, amtn_ref, gh_ref, gl_ref, ah_ref, al_ref,
):
    odd = on_odd_core()
    at = jnp.where(odd, ato_ref[...], ads_ref[0])
    amt = jnp.where(odd, amto_ref[...], ads_ref[1])
    at1, amt1 = adagrad(at, amt, ga_ref[...])
    second_group(u_ref, at1, amt1, atn_ref, amtn_ref, (mh, cu, cn), gh_ref, gl_ref, ah_ref, al_ref)


def gradient_kernel(u_ref, at_ref, mh, cu, cn, gu_ref, ga_ref):
    def put(rows, grad):
        gu_ref[rows, :] = grad

    ga_ref[...] = group_pass(0, reader(u_ref), u_ref.shape[0], split(at_ref[...]), (mh, cu, cn), put)


def both_moments_kernel(
    u_ref, um_ref, at_ref, amt_ref, gu_ref, ga_ref, mh, cu, cn,
    uo_ref, umo_ref, ato_ref, amto_ref, gh_ref, gl_ref, ah_ref, al_ref,
):
    uo_ref[...], umo_ref[...] = adagrad(u_ref[...], um_ref[...], gu_ref[...])
    at1, amt1 = adagrad(at_ref[...], amt_ref[...], ga_ref[...])
    second_group(uo_ref, at1, amt1, ato_ref, amto_ref, (mh, cu, cn), gh_ref, gl_ref, ah_ref, al_ref)


def users_kernel(u_ref, um_ref, gh_ref, gl_ref, ah_ref, al_ref, uo_ref, umo_ref):
    put = update_users(reader(u_ref), reader(um_ref), uo_ref, umo_ref)
    at_hl = ah_ref[...], al_ref[...]
    for r in range(0, u_ref.shape[0], BLOCK):
        rows = pl.ds(r, BLOCK)
        put(rows, dot3((gh_ref[rows, :], gl_ref[rows, :]), at_hl, 1, 1))


def users_pair_kernel(u_ref, um_ref, gh_ref, gl_ref, ah_ref, al_ref, users_ref):
    users_kernel(u_ref, um_ref, gh_ref, gl_ref, ah_ref, al_ref, users_ref.at[0], users_ref.at[1])


def prepare_kernel(rnd, away, after_ref, pu_hbm, pa_hbm, ng_hbm, mh, cu, cn, pu, pa, ng, sems):
    for c in (copies := fetch_indices(pu_hbm, pa_hbm, ng_hbm, pu, pa, ng, sems, away)):
        c.wait()
    prepare_round(rnd, pu, pa, ng, mh.shape[1], mh.shape[2], (mh, cu, cn))


def last_users_kernel(u_ref, um_ref, gh_ref, gl_ref, ah_ref, al_ref, uo_hbm, umo_hbm, uo_ref, umo_ref, sems):
    users_kernel(u_ref, um_ref, gh_ref, gl_ref, ah_ref, al_ref, uo_ref, umo_ref)
    copies = [
        pltpu.make_async_copy(uo_ref, uo_hbm, sems.at[0]),
        pltpu.make_async_copy(umo_ref, umo_hbm, sems.at[1]),
    ]
    for c in copies:
        c.start()
    for c in copies:
        c.wait()


def call(kernel, ins, outs, scratch=(), hbm=0, name=None, out_place=pltpu.VMEM):
    vmem = pl.BlockSpec(memory_space=pltpu.VMEM)
    split_at = len(ins) - hbm
    far = [pltpu.with_memory_space_constraint(x, pltpu.HBM) for x in ins[split_at:]]
    return pl.pallas_call(
        kernel,
        out_shape=outs,
        in_specs=[vmem] * split_at + [pl.BlockSpec(memory_space=pltpu.HBM)] * hbm,
        out_specs=[pl.BlockSpec(memory_space=out_place)] * len(outs),
        scratch_shapes=list(scratch),
        compiler_params=pltpu.CompilerParams(vmem_limit_bytes=VMEM_LIMIT),
        cost_estimate=pl.CostEstimate(flops=1, bytes_accessed=1, transcendentals=0),
        name=name,
    )(*ins[:split_at], *far)


def finish_kernel(xt_ref, out_hbm, x_ref, sems):
    count = sems.shape[0]
    size = x_ref.shape[0] // count
    copies = []
    for k in range(count):
        rows = pl.ds(k * size, size)
        x_ref[rows, :] = xt_ref[:, rows].T
        copies.append(pltpu.make_async_copy(x_ref.at[rows, :], out_hbm.at[rows, :], sems.at[k]))
        copies[-1].start()
    for c in copies:
        c.wait()


def finish(xt):
    d, rows = xt.shape
    return pl.pallas_call(
        finish_kernel,
        out_shape=pltpu.HBM((rows, d), xt.dtype),
        in_specs=[pl.BlockSpec(memory_space=pltpu.VMEM)],
        out_specs=pl.BlockSpec(memory_space=pltpu.HBM),
        scratch_shapes=[pltpu.VMEM((rows, d), xt.dtype), pltpu.SemaphoreType.DMA((4,))],
        compiler_params=pltpu.CompilerParams(vmem_limit_bytes=VMEM_LIMIT),
        cost_estimate=pl.CostEstimate(flops=0, bytes_accessed=2 * xt.size * 4, transcendentals=0),
        name="ads_out",
    )(xt)


def move(arrays, even, odd):
    blocks, cycles = lax.axis_size("blk"), lax.axis_size("pair")
    route = []
    for b in range(blocks):
        for p in range(cycles):
            steps, flip = odd if b % 2 else even
            to = (b + steps) % blocks, p ^ (cycles // 2 if flip else 0)
            route.append((b * cycles + p, to[0] * cycles + to[1]))
    return tuple(lax.ppermute(x, AXES, route) for x in arrays)


def local(users, user_moms, ads, ad_moments, pos_user, pos_ad, neg_ad):
    nu, d = users.shape
    na = ads.shape[0]
    rounds, groups, n = neg_ad.shape[2:]
    edges = pos_user.shape[3]
    indices = (pos_user, pos_ad, neg_ad)

    def shape(*dims, dtype=F32):
        return jax.ShapeDtypeStruct(dims, dtype)

    table_u, table_a = shape(nu, d), shape(d, na)
    parts = [shape(nu, na, dtype=BF16)] * 2 + [shape(d, na, dtype=BF16)] * 2
    index_scratch = [
        pltpu.VMEM((rounds, edges), jnp.int32),
        pltpu.VMEM((rounds, edges), jnp.int32),
        pltpu.VMEM((rounds, groups, n), jnp.int32),
    ]
    sems = pltpu.SemaphoreType.DMA((3,))
    prep_shapes = [shape(groups, nu, na, dtype=BF16), shape(groups, nu, 128), shape(groups, 8, na)]
    prep_scratch = [pltpu.VMEM(s.shape, s.dtype) for s in prep_shapes]

    def prepare_for(rnd, away, after):
        return call(
            functools.partial(prepare_kernel, rnd, away), (after, *indices), prep_shapes,
            [*index_scratch, sems], hbm=3, name="counts",
        )

    def first_group(u, um, at, prep, *after):
        return call(embedding_kernel, (u, um, at, *prep, *after), [table_u, table_u, table_a], name="group_first")

    def second_group_of(u, at, amt, ga, prep):
        at, amt, *g = call(moment_kernel, (u, at, amt, ga, *prep), [table_a, table_a, *parts], name="group_second")
        return (at, amt), g

    def update(u, um, g):
        return call(users_kernel, (u, um, *g), [table_u, table_u], name="users_update")

    u, um, at, amt, *g = call(
        first_round_kernel,
        (*indices, users, ads, user_moms, ad_moments),
        [table_u, table_u, table_a, table_a, *parts],
        [*index_scratch, *prep_scratch, *[pltpu.VMEM((nu, d), F32)] * 2, *[pltpu.VMEM((na, d), F32)] * 2, sems, pltpu.SemaphoreType.DMA((4,))],
        hbm=7, name="round_first",
    )
    near = move((at, amt), (1, False), (-1, False))
    far = move((at, amt), (1, False), (1, False))
    u, um = update(u, um, g)
    prep = prepare_for(1, False, um)

    u_early, um_early, ga = first_group(u, um, near[0], prep)
    ads_early, *g = call(
        moment_pair_kernel, (u_early, *near, ga, *prep), [shape(2, d, na), *parts], name="group_second_pair",
    )
    (ads_early,) = move((ads_early,), (1, False), (1, True))
    (after,) = call(users_pair_kernel, (u_early, um_early, *g), [shape(2, nu, d)], name="users_update_pair")
    (users_early,) = move((after,), (0, False), (0, True))

    u, um, ga = first_group(u, um, far[0], prep, after)
    ads_late, g = second_group_of(u, *far, ga, prep)
    ads_late = move(ads_late, (1, False), (-1, False))
    u, um = update(u, um, g)
    prep = prepare_for(2, True, um)

    u, um, ga = call(
        embedding_pick_kernel, (u, um, users_early, ads_early, ads_late[0], *prep), [table_u, table_u, table_a],
        name="group_first_pick",
    )
    at, amt, *g = call(
        moment_pick_kernel, (u, ads_early, *ads_late, ga, *prep),
        [table_a, table_a, *parts], name="group_second_pick",
    )
    at, amt = move((at, amt), (1, False), (1, True))
    u, um = update(u, um, g)
    after = um
    u, um = move((u, um), (0, False), (0, True))
    prep = prepare_for(3, False, after)

    gu, ga = call(gradient_kernel, (u, at, *prep), [table_u, table_a], name="group_first_gradients")
    u, um, at, amt, *g = call(
        both_moments_kernel, (u, um, at, amt, gu, ga, *prep), [table_u, table_u, table_a, table_a, *parts],
        name="group_second_both",
    )
    at, amt = move((at, amt), (1 - rounds, True), (1 - rounds, True))
    u, um = call(
        last_users_kernel, (u, um, *g), [pltpu.HBM((nu, d), F32)] * 2,
        [pltpu.VMEM((nu, d), F32)] * 2 + [pltpu.SemaphoreType.DMA((2,))], name="users_last", out_place=pltpu.HBM,
    )
    return u, um, finish(at), finish(amt)


def solution(mesh):
    rows = P(AXES, None)
    return jax.shard_map(
        local,
        mesh=mesh,
        in_specs=(rows, rows, rows, rows, P("blk", None, None, None), P("blk", None, None, None), P("blk", None, None, None, None)),
        out_specs=(rows, rows, rows, rows),
        check_vma=False,
    )
```

```python
import functools

import jax
import jax.numpy as jnp
from jax import lax
from jax.experimental import pallas as pl
from jax.experimental.pallas import tpu as pltpu
from jax.sharding import PartitionSpec as P

LEARN_RATE = 0.1
EPS = 1e-08
F32 = jnp.float32
BF16 = jnp.bfloat16
LANES = 128
PARTS_OUT = 4
AXES = ("blk", "pair")
VMEM_LIMIT = 28 * 1024 * 1024


def dot(a, b, ca, cb):
    return lax.dot_general(a, b, (((ca,), (cb,)), ((), ())), preferred_element_type=F32)


def split(x):
    hi = x.astype(BF16)
    return hi, (x - hi.astype(F32)).astype(BF16)


def dot3(a, b, ca, cb):
    (ah, al), (bh, bl) = a, b
    return dot(ah, bh, ca, cb) + (dot(ah, bl, ca, cb) + dot(al, bh, ca, cb))


def adagrad(row, mom, grad):
    mom = mom + grad * grad
    return row - LEARN_RATE * grad / (jnp.sqrt(mom) + EPS), mom


def onehot(idx, count):
    rows = lax.broadcasted_iota(jnp.int32, (count, idx.shape[1]), 0)
    return jnp.where(rows == idx, F32(1), F32(0)).astype(BF16)


def prepare(group, pu, pa, ng, users, ads, mh_ref, cu_ref, cn_ref):
    n = ng.shape[1]
    hot_u = onehot(pu, users)
    hot_a = onehot(pa, ads)
    mh_ref[group] = (0.5 * dot(hot_u, hot_a, 1, 1)).astype(BF16)
    ones = jnp.ones((pu.shape[1], 128), BF16)
    cu_ref[group] = dot(hot_u, ones, 1, 0) * F32(0.5 / n**0.5)
    hi = lax.shift_right_logical(ng, LANES.bit_length() - 1)
    counts = dot(onehot(hi, 8), onehot(ng - hi * LANES, LANES), 1, 1)
    for k in range(ads // LANES):
        cols = pl.ds(k * LANES, LANES)
        cn_ref[group, :, cols] = jnp.broadcast_to(counts[k : k + 1, :], (8, LANES))


def gradient_matrix(u_hl, at_hl, mh, cu, cn):
    s = dot3(u_hl, at_hl, 1, 0)
    t = jnp.tanh(0.5 * s)
    w = jnp.concatenate([cu] * (s.shape[1] // 128), axis=1) * cn
    m = mh.astype(F32)
    return split((w + m) * t + (w - m))


BLOCK = 256


def group_pass(group, u_read, users, at_hl, prep, gu_out, g_out=None):
    mh_ref, cu_ref, cn_ref = prep
    cn = cn_ref[group, 0:1, :]
    ga = None
    for r in range(0, users, BLOCK):
        rows = pl.ds(r, BLOCK)
        u_hl = split(u_read(rows))
        g_hl = gradient_matrix(u_hl, at_hl, mh_ref[group, rows, :], cu_ref[group, rows, :], cn)
        part = dot3(u_hl, g_hl, 0, 0)
        ga = part if ga is None else ga + part
        if g_out is None:
            gu_out(rows, dot3(g_hl, at_hl, 1, 1))
        else:
            g_out[0][rows, :], g_out[1][rows, :] = g_hl
    return ga


def reader(ref):
    return lambda rows: ref[rows, :]


def picker(odd, even_ref, odd_ref):
    return lambda rows: jnp.where(odd, odd_ref[rows, :], even_ref[rows, :])


def update_users(u_read, um_read, uo_ref, umo_ref):
    def put(rows, grad):
        uo_ref[rows, :], umo_ref[rows, :] = adagrad(u_read(rows), um_read(rows), grad)

    return put


def on_odd_core():
    return lax.rem(lax.axis_index("blk"), 2) == 1


def fetch_indices(pu_hbm, pa_hbm, ng_hbm, pu, pa, ng, sems, away=False):
    cycle = lax.axis_index("pair")
    if away:
        count = lax.axis_size("pair")
        cycle = lax.rem(cycle + jnp.where(on_odd_core(), count // 2, 0), count)
    copies = [
        pltpu.make_async_copy(src.at[0, cycle], dst, sems.at[k])
        for k, (src, dst) in enumerate(((pu_hbm, pu), (pa_hbm, pa), (ng_hbm, ng)))
    ]
    for c in copies:
        c.start()
    return copies


def pack_lists(rnd, pu, pa, ng, lists_ref):
    lists_ref[...] = jnp.zeros_like(lists_ref)
    lists_ref[0:1, pl.ds(0, pu.shape[1])] = pu[rnd : rnd + 1, :]
    lists_ref[1:2, pl.ds(0, pa.shape[1])] = pa[rnd : rnd + 1, :]
    lists_ref[pl.ds(2, ng.shape[1]), pl.ds(0, ng.shape[2])] = ng[rnd]


def prepare_round(rnd, pu, pa, ng, users, ads, prep):
    groups = ng.shape[1]
    edges = pu.shape[1] // groups
    for g in range(groups):
        cols = pl.ds(g * edges, edges)
        prepare(g, pu[rnd : rnd + 1, cols], pa[rnd : rnd + 1, cols], ng[rnd, g : g + 1, :], users, ads, *prep)


def second_group(u_ref, at1, amt1, ato_ref, amto_ref, prep, gh_ref, gl_ref, ah_ref, al_ref):
    at_hl = split(at1)
    ah_ref[...], al_ref[...] = at_hl
    ga = group_pass(1, reader(u_ref), u_ref.shape[0], at_hl, prep, None, (gh_ref, gl_ref))
    ato_ref[...], amto_ref[...] = adagrad(at1, amt1, ga)


def first_round_kernel(
    pu_hbm, pa_hbm, ng_hbm, u_hbm, a_hbm, um_hbm, am_hbm,
    uo_ref, umo_ref, ato_ref, amto_ref, gh_ref, gl_ref, ah_ref, al_ref,
    pu, pa, ng, mh, cu, cn, u_ref, um_ref, a_ref, am_ref, sems, table_sems,
):
    copies = fetch_indices(pu_hbm, pa_hbm, ng_hbm, pu, pa, ng, sems)
    tables = [
        pltpu.make_async_copy(src, dst, table_sems.at[k])
        for k, (src, dst) in enumerate(
            ((u_hbm, u_ref), (a_hbm, a_ref), (um_hbm, um_ref), (am_hbm, am_ref))
        )
    ]
    for c in tables:
        c.start()
    for c in copies:
        c.wait()
    prep = (mh, cu, cn)
    prepare_round(0, pu, pa, ng, u_ref.shape[0], a_ref.shape[0], prep)
    for c in tables:
        c.wait()
    at = a_ref[...].T
    amt = am_ref[...].T
    put = update_users(reader(u_ref), reader(um_ref), uo_ref, umo_ref)
    ga = group_pass(0, reader(u_ref), u_ref.shape[0], split(at), prep, put)
    at1, amt1 = adagrad(at, amt, ga)
    second_group(uo_ref, at1, amt1, ato_ref, amto_ref, prep, gh_ref, gl_ref, ah_ref, al_ref)


def embedding_kernel(u_ref, um_ref, at_ref, mh, cu, cn, *refs):
    uo_ref, umo_ref, ga_ref = refs[-3:]
    u_read = reader(u_ref)
    put = update_users(u_read, reader(um_ref), uo_ref, umo_ref)
    ga_ref[...] = group_pass(0, u_read, u_ref.shape[0], split(at_ref[...]), (mh, cu, cn), put)


def moment_kernel(
    u_ref, at_ref, amt_ref, ga_ref, mh, cu, cn,
    ato_ref, amto_ref, gh_ref, gl_ref, ah_ref, al_ref,
):
    at1, amt1 = adagrad(at_ref[...], amt_ref[...], ga_ref[...])
    second_group(u_ref, at1, amt1, ato_ref, amto_ref, (mh, cu, cn), gh_ref, gl_ref, ah_ref, al_ref)


def early_kernel(u_ref, um_ref, at_ref, amt_ref, ga_ref, mh, cu, cn, ads_ref, users_ref):
    at1, amt1 = adagrad(at_ref[...], amt_ref[...], ga_ref[...])
    put = update_users(reader(u_ref), reader(um_ref), users_ref.at[0], users_ref.at[1])
    ga = group_pass(1, reader(u_ref), u_ref.shape[0], split(at1), (mh, cu, cn), put)
    ads_ref[0], ads_ref[1] = adagrad(at1, amt1, ga)


def embedding_pick_kernel(ue_ref, ume_ref, users_ref, ads_ref, ato_ref, mh, cu, cn, un_ref, umn_ref, ga_ref):
    odd = on_odd_core()
    u_read = picker(odd, ue_ref, users_ref.at[0])
    put = update_users(u_read, picker(odd, ume_ref, users_ref.at[1]), un_ref, umn_ref)
    at = jnp.where(odd, ato_ref[...], ads_ref[0])
    ga_ref[...] = group_pass(0, u_read, ue_ref.shape[0], split(at), (mh, cu, cn), put)


def moment_pick_kernel(
    u_ref, um_ref, ads_ref, ato_ref, amto_ref, ga_ref, mh, cu, cn,
    un_ref, umn_ref, atn_ref, amtn_ref,
):
    odd = on_odd_core()
    at = jnp.where(odd, ato_ref[...], ads_ref[0])
    amt = jnp.where(odd, amto_ref[...], ads_ref[1])
    at1, amt1 = adagrad(at, amt, ga_ref[...])
    put = update_users(reader(u_ref), reader(um_ref), un_ref, umn_ref)
    ga = group_pass(1, reader(u_ref), u_ref.shape[0], split(at1), (mh, cu, cn), put)
    atn_ref[...], amtn_ref[...] = adagrad(at1, amt1, ga)


def gradient_kernel(u_ref, at_ref, mh, cu, cn, gu_ref, ga_ref):
    def put(rows, grad):
        gu_ref[rows, :] = grad

    ga_ref[...] = group_pass(0, reader(u_ref), u_ref.shape[0], split(at_ref[...]), (mh, cu, cn), put)


def both_moments_kernel(
    u_ref, um_ref, at_ref, amt_ref, gu_ref, ga_ref, mh, cu, cn,
    uo_ref, umo_ref, ato_ref, amto_ref, u1_ref, um1_ref,
):
    u1_ref[...], um1_ref[...] = adagrad(u_ref[...], um_ref[...], gu_ref[...])
    at1, amt1 = adagrad(at_ref[...], amt_ref[...], ga_ref[...])
    put = update_users(reader(u1_ref), reader(um1_ref), uo_ref, umo_ref)
    ga = group_pass(1, reader(u1_ref), u_ref.shape[0], split(at1), (mh, cu, cn), put)
    ato_ref[...], amto_ref[...] = adagrad(at1, amt1, ga)


def users_kernel(u_ref, um_ref, gh_ref, gl_ref, ah_ref, al_ref, uo_ref, umo_ref):
    put = update_users(reader(u_ref), reader(um_ref), uo_ref, umo_ref)
    at_hl = ah_ref[...], al_ref[...]
    for r in range(0, u_ref.shape[0], BLOCK):
        rows = pl.ds(r, BLOCK)
        put(rows, dot3((gh_ref[rows, :], gl_ref[rows, :]), at_hl, 1, 1))


def prepare_kernel(rnd, away, pack, after_ref, pu_hbm, pa_hbm, ng_hbm, mh, cu, cn, *refs):
    *lists, pu, pa, ng, sems = refs
    for c in (copies := fetch_indices(pu_hbm, pa_hbm, ng_hbm, pu, pa, ng, sems, away)):
        c.wait()
    prepare_round(rnd, pu, pa, ng, mh.shape[1], mh.shape[2], (mh, cu, cn))
    if lists:
        pack_lists(pack, pu, pa, ng, *lists)


def prepare_packed_kernel(edges, n, after_ref, lists_ref, mh, cu, cn):
    groups, users, ads = mh.shape
    size = edges // groups
    for g in range(groups):
        cols = pl.ds(g * size, size)
        negs = lists_ref[2 + g : 3 + g, pl.ds(0, n)]
        prepare(g, lists_ref[0:1, cols], lists_ref[1:2, cols], negs, users, ads, mh, cu, cn)


def call(kernel, ins, outs, scratch=(), hbm=0, name=None, out_place=pltpu.VMEM):
    vmem = pl.BlockSpec(memory_space=pltpu.VMEM)
    split_at = len(ins) - hbm
    far = [pltpu.with_memory_space_constraint(x, pltpu.HBM) for x in ins[split_at:]]
    return pl.pallas_call(
        kernel,
        out_shape=outs,
        in_specs=[vmem] * split_at + [pl.BlockSpec(memory_space=pltpu.HBM)] * hbm,
        out_specs=[pl.BlockSpec(memory_space=out_place)] * len(outs),
        scratch_shapes=list(scratch),
        compiler_params=pltpu.CompilerParams(vmem_limit_bytes=VMEM_LIMIT),
        cost_estimate=pl.CostEstimate(flops=1, bytes_accessed=1, transcendentals=0),
        name=name,
    )(*ins[:split_at], *far)


def turn_out(xt_ref, out_hbm, x_ref, sems):
    size = x_ref.shape[0] // PARTS_OUT
    copies = []
    for k in range(PARTS_OUT):
        rows = pl.ds(k * size, size)
        x_ref[rows, :] = xt_ref[:, rows].T
        copies.append(pltpu.make_async_copy(x_ref.at[rows, :], out_hbm.at[rows, :], sems.at[k]))
        copies[-1].start()
    return copies


def ads_out_kernel(xt_ref, out_hbm, x_ref, sems):
    for c in turn_out(xt_ref, out_hbm, x_ref, sems):
        c.wait()


def last_kernel(u_ref, um_ref, xt_ref, u_hbm, um_hbm, x_hbm, x_ref, sems, user_sems):
    copies = [
        pltpu.make_async_copy(u_ref, u_hbm, user_sems.at[0]),
        pltpu.make_async_copy(um_ref, um_hbm, user_sems.at[1]),
    ]
    for c in copies:
        c.start()
    for c in copies + turn_out(xt_ref, x_hbm, x_ref, sems):
        c.wait()


def move(arrays, *kinds):
    blocks, cycles = lax.axis_size("blk"), lax.axis_size("pair")
    route = []
    for b in range(blocks):
        for p in range(cycles):
            steps, flip = kinds[b % len(kinds)]
            to = (b + steps) % blocks, p ^ (cycles // 2 if flip else 0)
            route.append((b * cycles + p, to[0] * cycles + to[1]))
    return tuple(lax.ppermute(x, AXES, route) for x in arrays)


def local(users, user_moms, ads, ad_moments, pos_user, pos_ad, neg_ad):
    nu, d = users.shape
    na = ads.shape[0]
    rounds, groups, n = neg_ad.shape[2:]
    edges = pos_user.shape[3]
    indices = (pos_user, pos_ad, neg_ad)

    def shape(*dims, dtype=F32):
        return jax.ShapeDtypeStruct(dims, dtype)

    table_u, table_a = shape(nu, d), shape(d, na)
    parts = [shape(nu, na, dtype=BF16)] * 2 + [shape(d, na, dtype=BF16)] * 2
    index_scratch = [
        pltpu.VMEM((rounds, edges), jnp.int32),
        pltpu.VMEM((rounds, edges), jnp.int32),
        pltpu.VMEM((rounds, groups, n), jnp.int32),
    ]
    sems = pltpu.SemaphoreType.DMA((3,))
    prep_shapes = [shape(groups, nu, na, dtype=BF16), shape(groups, nu, 128), shape(groups, 8, na)]
    prep_scratch = [pltpu.VMEM(s.shape, s.dtype) for s in prep_shapes]

    def prepare_for(rnd, away, after, pack=None):
        lists = [] if pack is None else [shape(8, max(edges, n), dtype=jnp.int32)]
        return call(
            functools.partial(prepare_kernel, rnd, away, pack), (after, *indices), prep_shapes + lists,
            [*index_scratch, sems], hbm=3, name="counts",
        )

    def first_group(u, um, at, prep, *after):
        return call(embedding_kernel, (u, um, at, *prep, *after), [table_u, table_u, table_a], name="group_first")

    def update(u, um, g):
        return call(users_kernel, (u, um, *g), [table_u, table_u], name="users_update")

    stay, away = (0, False), (0, True)
    u, um, at, amt, *g = call(
        first_round_kernel,
        (*indices, users, ads, user_moms, ad_moments),
        [table_u, table_u, table_a, table_a, *parts],
        [*index_scratch, *prep_scratch, *[pltpu.VMEM((nu, d), F32)] * 2, *[pltpu.VMEM((na, d), F32)] * 2, sems, pltpu.SemaphoreType.DMA((4,))],
        hbm=7, name="round_first",
    )
    near = move((at, amt), (1, False), (-1, False))
    far = move((at, amt), (1, False), (1, False))
    u, um = update(u, um, g)
    *prep, lists = prepare_for(1, False, um, rounds - 1)

    (lists,) = move((lists,), (-4, False), stay, stay, stay)

    u_early, um_early, ga = first_group(u, um, near[0], prep)
    ads_early, after = call(
        early_kernel, (u_early, um_early, *near, ga, *prep), [shape(2, d, na), shape(2, nu, d)], name="group_second_early",
    )
    (ads_early,) = move((ads_early,), (1, False), (1, True))
    (users_early,) = move((after,), stay, away)

    u, um, ga = first_group(u, um, far[0], prep, after)
    at, amt, *g = call(moment_kernel, (u, *far, ga, *prep), [table_a, table_a, *parts], name="group_second")
    ads_late = move((at, amt), (1, False), (-1, False))
    u, um = update(u, um, g)
    prep = prepare_for(2, True, um)

    u, um, ga = call(
        embedding_pick_kernel, (u, um, users_early, ads_early, ads_late[0], *prep), [table_u, table_u, table_a],
        name="group_first_pick",
    )
    u, um, at, amt = call(
        moment_pick_kernel, (u, um, ads_early, *ads_late, ga, *prep),
        [table_u, table_u, table_a, table_a], name="group_second_pick",
    )
    after = um
    at, amt = move((at, amt), (1, False), (1, True), (1, False), (-3, True))
    u, um = move((u, um), (-4, False), away, stay, away)
    prep = call(functools.partial(prepare_packed_kernel, edges, n), (after, lists), prep_shapes, name="counts_moved")
    gu, ga = call(gradient_kernel, (u, at, *prep), [table_u, table_a], name="group_first_gradients")
    u, um, at, amt = call(
        both_moments_kernel, (u, um, at, amt, gu, ga, *prep), [table_u, table_u, table_a, table_a],
        [pltpu.VMEM((nu, d), F32)] * 2, name="group_second_both",
    )
    at, amt = move((at, amt), (1, True), (-3, True), (-3, True), (-3, True))
    u, um = move((u, um), (4, False), stay, stay, stay)
    upright = pltpu.HBM((na, d), F32)
    turn_scratch = [pltpu.VMEM((na, d), F32), pltpu.SemaphoreType.DMA((PARTS_OUT,))]
    (a,) = call(ads_out_kernel, (at,), [upright], turn_scratch, name="ads_out", out_place=pltpu.HBM)
    u, um, am = call(
        last_kernel, (u, um, amt), [pltpu.HBM((nu, d), F32)] * 2 + [upright],
        [*turn_scratch, pltpu.SemaphoreType.DMA((2,))], name="last_out", out_place=pltpu.HBM,
    )
    return u, um, a, am


def solution(mesh):
    rows = P(AXES, None)
    return jax.shard_map(
        local,
        mesh=mesh,
        in_specs=(rows, rows, rows, rows, P("blk", None, None, None), P("blk", None, None, None), P("blk", None, None, None, None)),
        out_specs=(rows, rows, rows, rows),
        check_vma=False,
    )
```

```python
import functools

import jax
import jax.numpy as jnp
from jax import lax
from jax.experimental import pallas as pl
from jax.experimental.pallas import tpu as pltpu
from jax.sharding import PartitionSpec as P

LEARN_RATE = 0.1
EPS = 1e-08
F32 = jnp.float32
BF16 = jnp.bfloat16
LANES = 128
PARTS_OUT = 4
AXES = ("blk", "pair")
VMEM_LIMIT = 28 * 1024 * 1024


def dot(a, b, ca, cb):
    return lax.dot_general(a, b, (((ca,), (cb,)), ((), ())), preferred_element_type=F32)


def split(x):
    hi = x.astype(BF16)
    return hi, (x - hi.astype(F32)).astype(BF16)


def dot3(a, b, ca, cb):
    (ah, al), (bh, bl) = a, b
    return dot(ah, bh, ca, cb) + (dot(ah, bl, ca, cb) + dot(al, bh, ca, cb))


def adagrad(row, mom, grad):
    mom = mom + grad * grad
    return row - LEARN_RATE * grad / (jnp.sqrt(mom) + EPS), mom


def onehot(idx, count):
    rows = lax.broadcasted_iota(jnp.int32, (count, idx.shape[1]), 0)
    return jnp.where(rows == idx, F32(1), F32(0)).astype(BF16)


def prepare(group, pu, pa, ng, users, ads, mh_ref, cu_ref, cn_ref):
    n = ng.shape[1]
    hot_u = onehot(pu, users)
    hot_a = onehot(pa, ads)
    mh_ref[group] = (0.5 * dot(hot_u, hot_a, 1, 1)).astype(BF16)
    ones = jnp.ones((pu.shape[1], 128), BF16)
    cu_ref[group] = dot(hot_u, ones, 1, 0) * F32(0.5 / n**0.5)
    hi = lax.shift_right_logical(ng, LANES.bit_length() - 1)
    counts = dot(onehot(hi, 8), onehot(ng - hi * LANES, LANES), 1, 1)
    for k in range(ads // LANES):
        cols = pl.ds(k * LANES, LANES)
        cn_ref[group, :, cols] = jnp.broadcast_to(counts[k : k + 1, :], (8, LANES))


def gradient_matrix(u_hl, at_hl, mh, cu, cn):
    s = dot3(u_hl, at_hl, 1, 0)
    t = jnp.tanh(0.5 * s)
    w = jnp.concatenate([cu] * (s.shape[1] // 128), axis=1) * cn
    m = mh.astype(F32)
    return split((w + m) * t + (w - m))


BLOCK = 256


def group_pass(group, u_read, users, at_hl, prep, gu_out, g_out=None):
    mh_ref, cu_ref, cn_ref = prep
    cn = cn_ref[group, 0:1, :]
    ga = None
    for r in range(0, users, BLOCK):
        rows = pl.ds(r, BLOCK)
        u_hl = split(u_read(rows))
        g_hl = gradient_matrix(u_hl, at_hl, mh_ref[group, rows, :], cu_ref[group, rows, :], cn)
        part = dot3(u_hl, g_hl, 0, 0)
        ga = part if ga is None else ga + part
        if g_out is None:
            gu_out(rows, dot3(g_hl, at_hl, 1, 1))
        else:
            g_out[0][rows, :], g_out[1][rows, :] = g_hl
    return ga


def reader(ref):
    return lambda rows: ref[rows, :]


def picker(odd, even_ref, odd_ref):
    return lambda rows: jnp.where(odd, odd_ref[rows, :], even_ref[rows, :])


def update_users(u_read, um_read, uo_ref, umo_ref):
    def put(rows, grad):
        uo_ref[rows, :], umo_ref[rows, :] = adagrad(u_read(rows), um_read(rows), grad)

    return put


def on_odd_core():
    return lax.rem(lax.axis_index("blk"), 2) == 1


def fetch_indices(pu_hbm, pa_hbm, ng_hbm, pu, pa, ng, sems, away=False):
    cycle = lax.axis_index("pair")
    if away:
        count = lax.axis_size("pair")
        cycle = lax.rem(cycle + jnp.where(on_odd_core(), count // 2, 0), count)
    copies = [
        pltpu.make_async_copy(src.at[0, cycle], dst, sems.at[k])
        for k, (src, dst) in enumerate(((pu_hbm, pu), (pa_hbm, pa), (ng_hbm, ng)))
    ]
    for c in copies:
        c.start()
    return copies


def pack_lists(rnd, pu, pa, ng, lists_ref):
    lists_ref[...] = jnp.zeros_like(lists_ref)
    lists_ref[0:1, pl.ds(0, pu.shape[1])] = pu[rnd : rnd + 1, :]
    lists_ref[1:2, pl.ds(0, pa.shape[1])] = pa[rnd : rnd + 1, :]
    lists_ref[pl.ds(2, ng.shape[1]), pl.ds(0, ng.shape[2])] = ng[rnd]


def prepare_round(rnd, pu, pa, ng, users, ads, prep):
    groups = ng.shape[1]
    edges = pu.shape[1] // groups
    for g in range(groups):
        cols = pl.ds(g * edges, edges)
        prepare(g, pu[rnd : rnd + 1, cols], pa[rnd : rnd + 1, cols], ng[rnd, g : g + 1, :], users, ads, *prep)


def second_group(u_ref, at1, amt1, ato_ref, amto_ref, prep, gh_ref, gl_ref, ah_ref, al_ref):
    at_hl = split(at1)
    ah_ref[...], al_ref[...] = at_hl
    ga = group_pass(1, reader(u_ref), u_ref.shape[0], at_hl, prep, None, (gh_ref, gl_ref))
    ato_ref[...], amto_ref[...] = adagrad(at1, amt1, ga)


def first_round_kernel(
    pu_hbm, pa_hbm, ng_hbm, u_hbm, a_hbm, um_hbm, am_hbm,
    uo_ref, umo_ref, ads_ref, gh_ref, gl_ref, ah_ref, al_ref,
    pu, pa, ng, mh, cu, cn, u_ref, um_ref, a_ref, am_ref, sems, table_sems,
):
    copies = fetch_indices(pu_hbm, pa_hbm, ng_hbm, pu, pa, ng, sems)
    tables = [
        pltpu.make_async_copy(src, dst, table_sems.at[k])
        for k, (src, dst) in enumerate(
            ((u_hbm, u_ref), (a_hbm, a_ref), (um_hbm, um_ref), (am_hbm, am_ref))
        )
    ]
    for c in tables:
        c.start()
    for c in copies:
        c.wait()
    prep = (mh, cu, cn)
    prepare_round(0, pu, pa, ng, u_ref.shape[0], a_ref.shape[0], prep)
    for c in tables:
        c.wait()
    at = a_ref[...].T
    amt = am_ref[...].T
    put = update_users(reader(u_ref), reader(um_ref), uo_ref, umo_ref)
    ga = group_pass(0, reader(u_ref), u_ref.shape[0], split(at), prep, put)
    at1, amt1 = adagrad(at, amt, ga)
    second_group(uo_ref, at1, amt1, ads_ref.at[0], ads_ref.at[1], prep, gh_ref, gl_ref, ah_ref, al_ref)


def meeting(u_read, um_read, at, amt, prep, u1_ref, um1_ref, uo_ref, umo_ref):
    users = u1_ref.shape[0]
    ga = group_pass(0, u_read, users, split(at), prep, update_users(u_read, um_read, u1_ref, um1_ref))
    at1, amt1 = adagrad(at, amt, ga)
    u_read = reader(u1_ref)
    ga = group_pass(1, u_read, users, split(at1), prep, update_users(u_read, reader(um1_ref), uo_ref, umo_ref))
    return adagrad(at1, amt1, ga)


def early_kernel(u_ref, um_ref, near_ref, mh, cu, cn, ads_ref, users_ref, u1_ref, um1_ref):
    ads_ref[0], ads_ref[1] = meeting(
        reader(u_ref), reader(um_ref), near_ref[0], near_ref[1], (mh, cu, cn),
        u1_ref, um1_ref, users_ref.at[0], users_ref.at[1],
    )


def late_kernel(
    u_ref, um_ref, far_ref, mh, cu, cn, after_ref,
    u1_ref, um1_ref, ato_ref, amto_ref, gh_ref, gl_ref, ah_ref, al_ref,
):
    prep = (mh, cu, cn)
    at = far_ref[0]
    u_read = reader(u_ref)
    put = update_users(u_read, reader(um_ref), u1_ref, um1_ref)
    ga = group_pass(0, u_read, u_ref.shape[0], split(at), prep, put)
    at1, amt1 = adagrad(at, far_ref[1], ga)
    second_group(u1_ref, at1, amt1, ato_ref, amto_ref, prep, gh_ref, gl_ref, ah_ref, al_ref)


def pick_kernel(
    ue_ref, ume_ref, users_ref, ads_ref, ato_ref, amto_ref, mh, cu, cn,
    un_ref, umn_ref, atn_ref, amtn_ref, u1_ref, um1_ref,
):
    odd = on_odd_core()
    at = jnp.where(odd, ato_ref[...], ads_ref[0])
    amt = jnp.where(odd, amto_ref[...], ads_ref[1])
    u_read, um_read = picker(odd, ue_ref, users_ref.at[0]), picker(odd, ume_ref, users_ref.at[1])
    atn_ref[...], amtn_ref[...] = meeting(
        u_read, um_read, at, amt, (mh, cu, cn), u1_ref, um1_ref, un_ref, umn_ref
    )


def gradient_kernel(u_ref, at_ref, mh, cu, cn, gu_ref, ga_ref):
    def put(rows, grad):
        gu_ref[rows, :] = grad

    ga_ref[...] = group_pass(0, reader(u_ref), u_ref.shape[0], split(at_ref[...]), (mh, cu, cn), put)


def both_moments_kernel(
    u_ref, um_ref, at_ref, amt_ref, gu_ref, ga_ref, mh, cu, cn,
    uo_ref, umo_ref, ads_ref, u1_ref, um1_ref,
):
    u1_ref[...], um1_ref[...] = adagrad(u_ref[...], um_ref[...], gu_ref[...])
    at1, amt1 = adagrad(at_ref[...], amt_ref[...], ga_ref[...])
    put = update_users(reader(u1_ref), reader(um1_ref), uo_ref, umo_ref)
    ga = group_pass(1, reader(u1_ref), u_ref.shape[0], split(at1), (mh, cu, cn), put)
    ads_ref[0], ads_ref[1] = adagrad(at1, amt1, ga)


def users_kernel(u_ref, um_ref, gh_ref, gl_ref, ah_ref, al_ref, uo_ref, umo_ref):
    put = update_users(reader(u_ref), reader(um_ref), uo_ref, umo_ref)
    at_hl = ah_ref[...], al_ref[...]
    for r in range(0, u_ref.shape[0], BLOCK):
        rows = pl.ds(r, BLOCK)
        put(rows, dot3((gh_ref[rows, :], gl_ref[rows, :]), at_hl, 1, 1))


def prepare_kernel(rnd, pack, after_ref, pu_hbm, pa_hbm, ng_hbm, mh, cu, cn, lists_ref, pu, pa, ng, sems):
    for c in (copies := fetch_indices(pu_hbm, pa_hbm, ng_hbm, pu, pa, ng, sems)):
        c.wait()
    prepare_round(rnd, pu, pa, ng, mh.shape[1], mh.shape[2], (mh, cu, cn))
    pack_lists(pack, pu, pa, ng, lists_ref)


def prepare_both_kernel(
    rnd, after_ref, lists_ref, pu_hbm, pa_hbm, ng_hbm, mh, cu, cn, mh2, cu2, cn2, pu, pa, ng, sems,
):
    copies = fetch_indices(pu_hbm, pa_hbm, ng_hbm, pu, pa, ng, sems, away=True)
    groups, users, ads = mh.shape
    n = ng_hbm.shape[-1]
    size = pu_hbm.shape[-1] // groups
    for g in range(groups):
        cols = pl.ds(g * size, size)
        negs = lists_ref[2 + g : 3 + g, pl.ds(0, n)]
        prepare(g, lists_ref[0:1, cols], lists_ref[1:2, cols], negs, users, ads, mh2, cu2, cn2)
    for c in copies:
        c.wait()
    prepare_round(rnd, pu, pa, ng, users, ads, (mh, cu, cn))


def call(kernel, ins, outs, scratch=(), hbm=0, name=None, out_place=pltpu.VMEM):
    vmem = pl.BlockSpec(memory_space=pltpu.VMEM)
    split_at = len(ins) - hbm
    far = [pltpu.with_memory_space_constraint(x, pltpu.HBM) for x in ins[split_at:]]
    return pl.pallas_call(
        kernel,
        out_shape=outs,
        in_specs=[vmem] * split_at + [pl.BlockSpec(memory_space=pltpu.HBM)] * hbm,
        out_specs=[pl.BlockSpec(memory_space=out_place)] * len(outs),
        scratch_shapes=list(scratch),
        compiler_params=pltpu.CompilerParams(vmem_limit_bytes=VMEM_LIMIT),
        cost_estimate=pl.CostEstimate(flops=1, bytes_accessed=1, transcendentals=0),
        name=name,
    )(*ins[:split_at], *far)


def last_kernel(u_ref, um_ref, ads_ref, u_hbm, um_hbm, a_hbm, am_hbm, turned, sems, user_sems):
    copies = [
        pltpu.make_async_copy(u_ref, u_hbm, user_sems.at[0]),
        pltpu.make_async_copy(um_ref, um_hbm, user_sems.at[1]),
    ]
    for c in copies:
        c.start()
    size = turned.shape[1] // PARTS_OUT
    for t, out_hbm in enumerate((a_hbm, am_hbm)):
        for k in range(PARTS_OUT):
            rows = pl.ds(k * size, size)
            turned[t, rows, :] = ads_ref[t, :, rows].T
            copies.append(pltpu.make_async_copy(turned.at[t, rows, :], out_hbm.at[rows, :], sems.at[t * PARTS_OUT + k]))
            copies[-1].start()
    for c in copies:
        c.wait()


def move(arrays, *kinds):
    blocks, cycles = lax.axis_size("blk"), lax.axis_size("pair")
    route = []
    for b in range(blocks):
        for p in range(cycles):
            steps, flip = kinds[b % len(kinds)]
            to = (b + steps) % blocks, p ^ (cycles // 2 if flip else 0)
            route.append((b * cycles + p, to[0] * cycles + to[1]))
    return tuple(lax.ppermute(x, AXES, route) for x in arrays)


def local(users, user_moms, ads, ad_moments, pos_user, pos_ad, neg_ad):
    nu, d = users.shape
    na = ads.shape[0]
    rounds, groups, n = neg_ad.shape[2:]
    edges = pos_user.shape[3]
    indices = (pos_user, pos_ad, neg_ad)

    def shape(*dims, dtype=F32):
        return jax.ShapeDtypeStruct(dims, dtype)

    table_u, table_a = shape(nu, d), shape(d, na)
    parts = [shape(nu, na, dtype=BF16)] * 2 + [shape(d, na, dtype=BF16)] * 2
    index_scratch = [
        pltpu.VMEM((rounds, edges), jnp.int32),
        pltpu.VMEM((rounds, edges), jnp.int32),
        pltpu.VMEM((rounds, groups, n), jnp.int32),
    ]
    sems = pltpu.SemaphoreType.DMA((3,))
    prep_shapes = [shape(groups, nu, na, dtype=BF16), shape(groups, nu, 128), shape(groups, 8, na)]
    prep_scratch = [pltpu.VMEM(s.shape, s.dtype) for s in prep_shapes]

    def update(u, um, g):
        return call(users_kernel, (u, um, *g), [table_u, table_u], name="users_update")

    stay, away = (0, False), (0, True)
    both_u, both_a = shape(2, nu, d), shape(2, d, na)
    users_scratch = [pltpu.VMEM((nu, d), F32)] * 2
    u, um, ads_now, *g = call(
        first_round_kernel,
        (*indices, users, ads, user_moms, ad_moments),
        [table_u, table_u, both_a, *parts],
        [*index_scratch, *prep_scratch, *users_scratch, *[pltpu.VMEM((na, d), F32)] * 2, sems, pltpu.SemaphoreType.DMA((4,))],
        hbm=7, name="round_first",
    )
    (near,) = move((ads_now,), (1, False), (-1, False))
    (far,) = move((ads_now,), (1, False), (1, False))
    u, um = update(u, um, g)
    *prep, lists = call(
        functools.partial(prepare_kernel, 1, rounds - 1), (um, *indices),
        prep_shapes + [shape(8, max(edges, n), dtype=jnp.int32)], [*index_scratch, sems], hbm=3, name="counts_1",
    )
    (lists,) = move((lists,), (-4, False), stay, stay, stay)

    ads_early, after = call(early_kernel, (u, um, near, *prep), [both_a, both_u], users_scratch, name="round_early")
    (ads_early,) = move((ads_early,), (1, False), (1, True))
    (users_early,) = move((after,), stay, away)

    u, um, at, amt, *g = call(
        late_kernel, (u, um, far, *prep, after), [table_u, table_u, table_a, table_a, *parts], name="round_late",
    )
    ads_late = move((at, amt), (1, False), (-1, False))
    u, um = update(u, um, g)
    preps = call(
        functools.partial(prepare_both_kernel, 2), (um, lists, *indices), prep_shapes * 2, [*index_scratch, sems], hbm=3,
        name="counts_23",
    )
    prep, prep_last = preps[: len(prep_shapes)], preps[len(prep_shapes) :]

    u, um, at, amt = call(
        pick_kernel, (u, um, users_early, ads_early, *ads_late, *prep), [table_u, table_u, table_a, table_a],
        users_scratch, name="round_pick",
    )
    at, amt = move((at, amt), (1, False), (1, True), (1, False), (-3, True))
    u, um = move((u, um), (-4, False), away, stay, away)
    gu, ga = call(gradient_kernel, (u, at, *prep_last), [table_u, table_a], name="round_last_gradients")
    u, um, ads_now = call(
        both_moments_kernel, (u, um, at, amt, gu, ga, *prep_last), [table_u, table_u, both_a], users_scratch,
        name="round_last",
    )
    (ads_now,) = move((ads_now,), (1, True), (-3, True), (-3, True), (-3, True))
    u, um = move((u, um), (4, False), stay, stay, stay)
    return call(
        last_kernel, (u, um, ads_now), [pltpu.HBM((nu, d), F32)] * 2 + [pltpu.HBM((na, d), F32)] * 2,
        [pltpu.VMEM((2, na, d), F32), pltpu.SemaphoreType.DMA((2 * PARTS_OUT,)), pltpu.SemaphoreType.DMA((2,))],
        name="last_out", out_place=pltpu.HBM,
    )


def solution(mesh):
    rows = P(AXES, None)
    return jax.shard_map(
        local,
        mesh=mesh,
        in_specs=(rows, rows, rows, rows, P("blk", None, None, None), P("blk", None, None, None), P("blk", None, None, None, None)),
        out_specs=(rows, rows, rows, rows),
        check_vma=False,
    )
```

```python
import functools

import jax
import jax.numpy as jnp
from jax import lax
from jax.experimental import pallas as pl
from jax.experimental.pallas import tpu as pltpu
from jax.sharding import PartitionSpec as P

LEARN_RATE = 0.1
EPS = 1e-08
F32 = jnp.float32
BF16 = jnp.bfloat16
LANES = 128
PARTS_OUT = 4
AXES = ("blk", "pair")
VMEM_LIMIT = 28 * 1024 * 1024


def dot(a, b, ca, cb):
    return lax.dot_general(a, b, (((ca,), (cb,)), ((), ())), preferred_element_type=F32)


def split(x):
    hi = x.astype(BF16)
    return hi, (x - hi.astype(F32)).astype(BF16)


def dot3(a, b, ca, cb):
    (ah, al), (bh, bl) = a, b
    return dot(jnp.concatenate([ah, al, ah], axis=ca), jnp.concatenate([bh, bh, bl], axis=cb), ca, cb)


def adagrad(row, mom, grad):
    mom = mom + grad * grad
    return row - LEARN_RATE * grad / (jnp.sqrt(mom) + EPS), mom


def onehot(idx, count):
    rows = lax.broadcasted_iota(jnp.int32, (count, idx.shape[1]), 0)
    return jnp.where(rows == idx, F32(1), F32(0)).astype(BF16)


def prepare(group, pu, pa, ng, users, ads, mh_ref, cu_ref, cn_ref):
    n = ng.shape[1]
    hot_u = onehot(pu, users)
    hot_a = onehot(pa, ads)
    mh_ref[group] = (0.5 * dot(hot_u, hot_a, 1, 1)).astype(BF16)
    ones = jnp.ones((pu.shape[1], 128), BF16)
    cu_ref[group] = dot(hot_u, ones, 1, 0) * F32(0.5 / n**0.5)
    hi = lax.shift_right_logical(ng, LANES.bit_length() - 1)
    counts = dot(onehot(hi, 8), onehot(ng - hi * LANES, LANES), 1, 1)
    for k in range(ads // LANES):
        cols = pl.ds(k * LANES, LANES)
        cn_ref[group, :, cols] = jnp.broadcast_to(counts[k : k + 1, :], (8, LANES))


def gradient_matrix(s, mh, cu, cn):
    t = jnp.tanh(0.5 * s)
    w = jnp.concatenate([cu] * (s.shape[1] // 128), axis=1) * cn
    m = mh.astype(F32)
    return split((w + m) * t + (w - m))


BLOCK = 256


def group_pass(group, u_read, users, at_hl, prep, gu_out, g_out=None):
    mh_ref, cu_ref, cn_ref = prep
    cn = cn_ref[group, 0:1, :]
    blocks = [pl.ds(r, BLOCK) for r in range(0, users, BLOCK)]
    u_hl = [split(u_read(rows)) for rows in blocks]
    scores = [dot3(u, at_hl, 1, 0) for u in u_hl]
    ga = None
    for rows, u, s in zip(blocks, u_hl, scores):
        g_hl = gradient_matrix(s, mh_ref[group, rows, :], cu_ref[group, rows, :], cn)
        if g_out is None:
            gu_out(rows, dot3(g_hl, at_hl, 1, 1))
        else:
            g_out[0][rows, :], g_out[1][rows, :] = g_hl
        part = dot3(u, g_hl, 0, 0)
        ga = part if ga is None else ga + part
    return ga


def reader(ref):
    return lambda rows: ref[rows, :]


def picker(odd, even_ref, odd_ref):
    return lambda rows: jnp.where(odd, odd_ref[rows, :], even_ref[rows, :])


def update_users(u_read, um_read, uo_ref, umo_ref):
    def put(rows, grad):
        uo_ref[rows, :], umo_ref[rows, :] = adagrad(u_read(rows), um_read(rows), grad)

    return put


def on_odd_core():
    return lax.rem(lax.axis_index("blk"), 2) == 1


def fetch_indices(pu_hbm, pa_hbm, ng_hbm, pu, pa, ng, sems, away=False):
    cycle = lax.axis_index("pair")
    if away:
        count = lax.axis_size("pair")
        cycle = lax.rem(cycle + jnp.where(on_odd_core(), count // 2, 0), count)
    copies = [
        pltpu.make_async_copy(src.at[0, cycle], dst, sems.at[k])
        for k, (src, dst) in enumerate(((pu_hbm, pu), (pa_hbm, pa), (ng_hbm, ng)))
    ]
    for c in copies:
        c.start()
    return copies


def pack_lists(rnd, pu, pa, ng, lists_ref):
    lists_ref[...] = jnp.zeros_like(lists_ref)
    lists_ref[0:1, pl.ds(0, pu.shape[1])] = pu[rnd : rnd + 1, :]
    lists_ref[1:2, pl.ds(0, pa.shape[1])] = pa[rnd : rnd + 1, :]
    lists_ref[pl.ds(2, ng.shape[1]), pl.ds(0, ng.shape[2])] = ng[rnd]


def prepare_round(rnd, pu, pa, ng, users, ads, prep):
    groups = ng.shape[1]
    edges = pu.shape[1] // groups
    for g in range(groups):
        cols = pl.ds(g * edges, edges)
        prepare(g, pu[rnd : rnd + 1, cols], pa[rnd : rnd + 1, cols], ng[rnd, g : g + 1, :], users, ads, *prep)


def second_group(u_ref, at1, amt1, ato_ref, amto_ref, prep, gh_ref, gl_ref, ah_ref, al_ref):
    at_hl = split(at1)
    ah_ref[...], al_ref[...] = at_hl
    ga = group_pass(1, reader(u_ref), u_ref.shape[0], at_hl, prep, None, (gh_ref, gl_ref))
    ato_ref[...], amto_ref[...] = adagrad(at1, amt1, ga)


def first_round_kernel(
    pu_hbm, pa_hbm, ng_hbm, u_hbm, a_hbm, um_hbm, am_hbm,
    uo_ref, umo_ref, ads_ref, gh_ref, gl_ref, ah_ref, al_ref,
    pu, pa, ng, mh, cu, cn, u_ref, um_ref, a_ref, am_ref, sems, table_sems,
):
    copies = fetch_indices(pu_hbm, pa_hbm, ng_hbm, pu, pa, ng, sems)
    tables = [
        pltpu.make_async_copy(src, dst, table_sems.at[k])
        for k, (src, dst) in enumerate(
            ((u_hbm, u_ref), (a_hbm, a_ref), (um_hbm, um_ref), (am_hbm, am_ref))
        )
    ]
    for c in tables:
        c.start()
    for c in copies:
        c.wait()
    prep = (mh, cu, cn)
    prepare_round(0, pu, pa, ng, u_ref.shape[0], a_ref.shape[0], prep)
    for c in tables:
        c.wait()
    at = a_ref[...].T
    amt = am_ref[...].T
    put = update_users(reader(u_ref), reader(um_ref), uo_ref, umo_ref)
    ga = group_pass(0, reader(u_ref), u_ref.shape[0], split(at), prep, put)
    at1, amt1 = adagrad(at, amt, ga)
    second_group(uo_ref, at1, amt1, ads_ref.at[0], ads_ref.at[1], prep, gh_ref, gl_ref, ah_ref, al_ref)


def meeting(u_read, um_read, at, amt, prep, u1_ref, um1_ref, uo_ref, umo_ref):
    users = u1_ref.shape[0]
    ga = group_pass(0, u_read, users, split(at), prep, update_users(u_read, um_read, u1_ref, um1_ref))
    at1, amt1 = adagrad(at, amt, ga)
    u_read = reader(u1_ref)
    ga = group_pass(1, u_read, users, split(at1), prep, update_users(u_read, reader(um1_ref), uo_ref, umo_ref))
    return adagrad(at1, amt1, ga)


def early_kernel(u_ref, um_ref, near_ref, mh, cu, cn, ads_ref, users_ref, u1_ref, um1_ref):
    ads_ref[0], ads_ref[1] = meeting(
        reader(u_ref), reader(um_ref), near_ref[0], near_ref[1], (mh, cu, cn),
        u1_ref, um1_ref, users_ref.at[0], users_ref.at[1],
    )


def late_kernel(
    u_ref, um_ref, far_ref, mh, cu, cn, after_ref, lists_ref,
    u1_ref, um1_ref, ato_ref, amto_ref, gh_ref, gl_ref, ah_ref, al_ref,
):
    prep = (mh, cu, cn)
    at = far_ref[0]
    u_read = reader(u_ref)
    put = update_users(u_read, reader(um_ref), u1_ref, um1_ref)
    ga = group_pass(0, u_read, u_ref.shape[0], split(at), prep, put)
    at1, amt1 = adagrad(at, far_ref[1], ga)
    second_group(u1_ref, at1, amt1, ato_ref, amto_ref, prep, gh_ref, gl_ref, ah_ref, al_ref)


def pick_kernel(
    ue_ref, ume_ref, users_ref, ads_ref, ato_ref, amto_ref, mh, cu, cn,
    un_ref, umn_ref, atn_ref, amtn_ref, u1_ref, um1_ref,
):
    odd = on_odd_core()
    at = jnp.where(odd, ato_ref[...], ads_ref[0])
    amt = jnp.where(odd, amto_ref[...], ads_ref[1])
    u_read, um_read = picker(odd, ue_ref, users_ref.at[0]), picker(odd, ume_ref, users_ref.at[1])
    atn_ref[...], amtn_ref[...] = meeting(
        u_read, um_read, at, amt, (mh, cu, cn), u1_ref, um1_ref, un_ref, umn_ref
    )


def gradient_kernel(u_ref, at_ref, mh, cu, cn, gu_ref, ga_ref):
    def put(rows, grad):
        gu_ref[rows, :] = grad

    ga_ref[...] = group_pass(0, reader(u_ref), u_ref.shape[0], split(at_ref[...]), (mh, cu, cn), put)


def both_moments_kernel(
    u_ref, um_ref, at_ref, amt_ref, gu_ref, ga_ref, mh, cu, cn,
    uo_ref, umo_ref, ads_ref, u1_ref, um1_ref,
):
    u1_ref[...], um1_ref[...] = adagrad(u_ref[...], um_ref[...], gu_ref[...])
    at1, amt1 = adagrad(at_ref[...], amt_ref[...], ga_ref[...])
    put = update_users(reader(u1_ref), reader(um1_ref), uo_ref, umo_ref)
    ga = group_pass(1, reader(u1_ref), u_ref.shape[0], split(at1), (mh, cu, cn), put)
    ads_ref[0], ads_ref[1] = adagrad(at1, amt1, ga)


def users_kernel(u_ref, um_ref, gh_ref, gl_ref, ah_ref, al_ref, uo_ref, umo_ref):
    put = update_users(reader(u_ref), reader(um_ref), uo_ref, umo_ref)
    at_hl = ah_ref[...], al_ref[...]
    for r in range(0, u_ref.shape[0], BLOCK):
        rows = pl.ds(r, BLOCK)
        put(rows, dot3((gh_ref[rows, :], gl_ref[rows, :]), at_hl, 1, 1))


def prepare_kernel(rnd, pack, after_ref, pu_hbm, pa_hbm, ng_hbm, mh, cu, cn, lists_ref, pu, pa, ng, sems):
    for c in (copies := fetch_indices(pu_hbm, pa_hbm, ng_hbm, pu, pa, ng, sems)):
        c.wait()
    prepare_round(rnd, pu, pa, ng, mh.shape[1], mh.shape[2], (mh, cu, cn))
    pack_lists(pack, pu, pa, ng, lists_ref)


def prepare_both_kernel(
    rnd, after_ref, lists_ref, pu_hbm, pa_hbm, ng_hbm, mh, cu, cn, mh2, cu2, cn2, pu, pa, ng, sems,
):
    copies = fetch_indices(pu_hbm, pa_hbm, ng_hbm, pu, pa, ng, sems, away=True)
    groups, users, ads = mh.shape
    n = ng_hbm.shape[-1]
    size = pu_hbm.shape[-1] // groups
    for g in range(groups):
        cols = pl.ds(g * size, size)
        negs = lists_ref[2 + g : 3 + g, pl.ds(0, n)]
        prepare(g, lists_ref[0:1, cols], lists_ref[1:2, cols], negs, users, ads, mh2, cu2, cn2)
    for c in copies:
        c.wait()
    prepare_round(rnd, pu, pa, ng, users, ads, (mh, cu, cn))


def call(kernel, ins, outs, scratch=(), hbm=0, name=None, out_place=pltpu.VMEM):
    vmem = pl.BlockSpec(memory_space=pltpu.VMEM)
    split_at = len(ins) - hbm
    far = [pltpu.with_memory_space_constraint(x, pltpu.HBM) for x in ins[split_at:]]
    return pl.pallas_call(
        kernel,
        out_shape=outs,
        in_specs=[vmem] * split_at + [pl.BlockSpec(memory_space=pltpu.HBM)] * hbm,
        out_specs=[pl.BlockSpec(memory_space=out_place)] * len(outs),
        scratch_shapes=list(scratch),
        compiler_params=pltpu.CompilerParams(vmem_limit_bytes=VMEM_LIMIT),
        cost_estimate=pl.CostEstimate(flops=1, bytes_accessed=1, transcendentals=0),
        name=name,
    )(*ins[:split_at], *far)


def last_kernel(u_ref, um_ref, ads_ref, u_hbm, um_hbm, a_hbm, am_hbm, turned, sems, user_sems):
    copies = [
        pltpu.make_async_copy(u_ref, u_hbm, user_sems.at[0]),
        pltpu.make_async_copy(um_ref, um_hbm, user_sems.at[1]),
    ]
    for c in copies:
        c.start()
    size = turned.shape[1] // PARTS_OUT
    for t, out_hbm in enumerate((a_hbm, am_hbm)):
        for k in range(PARTS_OUT):
            rows = pl.ds(k * size, size)
            turned[t, rows, :] = ads_ref[t, :, rows].T
            copies.append(pltpu.make_async_copy(turned.at[t, rows, :], out_hbm.at[rows, :], sems.at[t * PARTS_OUT + k]))
            copies[-1].start()
    for c in copies:
        c.wait()


def move(arrays, *kinds):
    blocks, cycles = lax.axis_size("blk"), lax.axis_size("pair")
    route = []
    for b in range(blocks):
        for p in range(cycles):
            steps, flip = kinds[b % len(kinds)]
            to = (b + steps) % blocks, p ^ (cycles // 2 if flip else 0)
            route.append((b * cycles + p, to[0] * cycles + to[1]))
    return tuple(lax.ppermute(x, AXES, route) for x in arrays)


def local(users, user_moms, ads, ad_moments, pos_user, pos_ad, neg_ad):
    nu, d = users.shape
    na = ads.shape[0]
    rounds, groups, n = neg_ad.shape[2:]
    edges = pos_user.shape[3]
    indices = (pos_user, pos_ad, neg_ad)

    def shape(*dims, dtype=F32):
        return jax.ShapeDtypeStruct(dims, dtype)

    table_u, table_a = shape(nu, d), shape(d, na)
    parts = [shape(nu, na, dtype=BF16)] * 2 + [shape(d, na, dtype=BF16)] * 2
    index_scratch = [
        pltpu.VMEM((rounds, edges), jnp.int32),
        pltpu.VMEM((rounds, edges), jnp.int32),
        pltpu.VMEM((rounds, groups, n), jnp.int32),
    ]
    sems = pltpu.SemaphoreType.DMA((3,))
    prep_shapes = [shape(groups, nu, na, dtype=BF16), shape(groups, nu, 128), shape(groups, 8, na)]
    prep_scratch = [pltpu.VMEM(s.shape, s.dtype) for s in prep_shapes]

    def update(u, um, g):
        return call(users_kernel, (u, um, *g), [table_u, table_u], name="users_update")

    stay, away = (0, False), (0, True)
    both_u, both_a = shape(2, nu, d), shape(2, d, na)
    users_scratch = [pltpu.VMEM((nu, d), F32)] * 2
    u, um, ads_now, *g = call(
        first_round_kernel,
        (*indices, users, ads, user_moms, ad_moments),
        [table_u, table_u, both_a, *parts],
        [*index_scratch, *prep_scratch, *users_scratch, *[pltpu.VMEM((na, d), F32)] * 2, sems, pltpu.SemaphoreType.DMA((4,))],
        hbm=7, name="round_first",
    )
    (near,) = move((ads_now,), (1, False), (-1, False))
    (far,) = move((ads_now,), (1, False), (1, False))
    u, um = update(u, um, g)
    *prep, lists = call(
        functools.partial(prepare_kernel, 1, rounds - 1), (um, *indices),
        prep_shapes + [shape(8, max(edges, n), dtype=jnp.int32)], [*index_scratch, sems], hbm=3, name="counts_1",
    )
    (lists,) = move((lists,), (-4, False), stay, stay, stay)

    ads_early, after = call(early_kernel, (u, um, near, *prep), [both_a, both_u], users_scratch, name="round_early")
    (ads_early,) = move((ads_early,), (1, False), (1, True))
    (users_early,) = move((after,), stay, away)

    u, um, at, amt, *g = call(
        late_kernel, (u, um, far, *prep, after, lists), [table_u, table_u, table_a, table_a, *parts], name="round_late",
    )
    ads_late = move((at, amt), (1, False), (-1, False))
    u, um = update(u, um, g)
    preps = call(
        functools.partial(prepare_both_kernel, 2), (um, lists, *indices), prep_shapes * 2, [*index_scratch, sems], hbm=3,
        name="counts_23",
    )
    prep, prep_last = preps[: len(prep_shapes)], preps[len(prep_shapes) :]

    u, um, at, amt = call(
        pick_kernel, (u, um, users_early, ads_early, *ads_late, *prep), [table_u, table_u, table_a, table_a],
        users_scratch, name="round_pick",
    )
    at, amt = move((at, amt), (1, False), (1, True), (1, False), (-3, True))
    u, um = move((u, um), (-4, False), away, stay, away)
    gu, ga = call(gradient_kernel, (u, at, *prep_last), [table_u, table_a], name="round_last_gradients")
    u, um, ads_now = call(
        both_moments_kernel, (u, um, at, amt, gu, ga, *prep_last), [table_u, table_u, both_a], users_scratch,
        name="round_last",
    )
    (ads_now,) = move((ads_now,), (1, True), (-3, True), (-3, True), (-3, True))
    u, um = move((u, um), (4, False), stay, stay, stay)
    return call(
        last_kernel, (u, um, ads_now), [pltpu.HBM((nu, d), F32)] * 2 + [pltpu.HBM((na, d), F32)] * 2,
        [pltpu.VMEM((2, na, d), F32), pltpu.SemaphoreType.DMA((2 * PARTS_OUT,)), pltpu.SemaphoreType.DMA((2,))],
        name="last_out", out_place=pltpu.HBM,
    )


def solution(mesh):
    rows = P(AXES, None)
    return jax.shard_map(
        local,
        mesh=mesh,
        in_specs=(rows, rows, rows, rows, P("blk", None, None, None), P("blk", None, None, None), P("blk", None, None, None, None)),
        out_specs=(rows, rows, rows, rows),
        check_vma=False,
    )
```

```python
import functools

import jax
import jax.numpy as jnp
from jax import lax
from jax.experimental import pallas as pl
from jax.experimental.pallas import tpu as pltpu
from jax.sharding import PartitionSpec as P

LEARN_RATE = 0.1
EPS = 1e-08
F32 = jnp.float32
BF16 = jnp.bfloat16
LANES = 128
PARTS_OUT = 4
AXES = ("blk", "pair")
VMEM_LIMIT = 28 * 1024 * 1024


def dot(a, b, ca, cb):
    return lax.dot_general(a, b, (((ca,), (cb,)), ((), ())), preferred_element_type=F32)


def split(x):
    hi = x.astype(BF16)
    return hi, (x - hi.astype(F32)).astype(BF16)


def dot3(a, b, ca, cb):
    (ah, al), (bh, bl) = a, b
    return dot(jnp.concatenate([ah, al, ah], axis=ca), jnp.concatenate([bh, bh, bl], axis=cb), ca, cb)


def adagrad(row, mom, grad):
    mom = mom + grad * grad
    return row - LEARN_RATE * grad / (jnp.sqrt(mom) + EPS), mom


def onehot(idx, count):
    rows = lax.broadcasted_iota(jnp.int32, (count, idx.shape[1]), 0)
    return jnp.where(rows == idx, F32(1), F32(0)).astype(BF16)


def prepare(group, pu, pa, ng, users, ads, mh_ref, cu_ref, cn_ref):
    n = ng.shape[1]
    hot_u = onehot(pu, users)
    hot_a = onehot(pa, ads)
    mh_ref[group] = (0.5 * dot(hot_u, hot_a, 1, 1)).astype(BF16)
    ones = jnp.ones((pu.shape[1], 128), BF16)
    cu_ref[group] = dot(hot_u, ones, 1, 0) * F32(0.5 / n**0.5)
    hi = lax.shift_right_logical(ng, LANES.bit_length() - 1)
    counts = dot(onehot(hi, 8), onehot(ng - hi * LANES, LANES), 1, 1)
    for k in range(ads // LANES):
        cols = pl.ds(k * LANES, LANES)
        cn_ref[group, :, cols] = jnp.broadcast_to(counts[k : k + 1, :], (8, LANES))


def gradient_matrix(s, mh, cu, cn):
    t = jnp.tanh(0.5 * s)
    w = jnp.concatenate([cu] * (s.shape[1] // 128), axis=1) * cn
    m = mh.astype(F32)
    return split((w + m) * t + (w - m))


BLOCK = 256


def group_pass(group, u_read, users, at_hl, prep, gu_out, g_out=None):
    mh_ref, cu_ref, cn_ref = prep
    cn = cn_ref[group, 0:1, :]
    blocks = [pl.ds(r, BLOCK) for r in range(0, users, BLOCK)]
    u_hl = [split(u_read(rows)) for rows in blocks]
    scores = [dot3(u, at_hl, 1, 0) for u in u_hl]
    ga = None
    for rows, u, s in zip(blocks, u_hl, scores):
        g_hl = gradient_matrix(s, mh_ref[group, rows, :], cu_ref[group, rows, :], cn)
        if g_out is None:
            gu_out(rows, dot3(g_hl, at_hl, 1, 1))
        else:
            g_out[0][rows, :], g_out[1][rows, :] = g_hl
        part = dot3(u, g_hl, 0, 0)
        ga = part if ga is None else ga + part
    return ga


def reader(ref):
    return lambda rows: ref[rows, :]


def picker(odd, even_ref, odd_ref):
    return lambda rows: jnp.where(odd, odd_ref[rows, :], even_ref[rows, :])


def update_users(u_read, um_read, uo_ref, umo_ref):
    def put(rows, grad):
        uo_ref[rows, :], umo_ref[rows, :] = adagrad(u_read(rows), um_read(rows), grad)

    return put


def on_odd_core():
    return lax.rem(lax.axis_index("blk"), 2) == 1


def fetch_indices(pu_hbm, pa_hbm, ng_hbm, pu, pa, ng, sems, away=False):
    cycle = lax.axis_index("pair")
    if away:
        count = lax.axis_size("pair")
        cycle = lax.rem(cycle + jnp.where(on_odd_core(), count // 2, 0), count)
    copies = [
        pltpu.make_async_copy(src.at[0, cycle], dst, sems.at[k])
        for k, (src, dst) in enumerate(((pu_hbm, pu), (pa_hbm, pa), (ng_hbm, ng)))
    ]
    for c in copies:
        c.start()
    return copies


def pack_lists(rnd, pu, pa, ng, lists_ref):
    lists_ref[...] = jnp.zeros_like(lists_ref)
    lists_ref[0:1, pl.ds(0, pu.shape[1])] = pu[rnd : rnd + 1, :]
    lists_ref[1:2, pl.ds(0, pa.shape[1])] = pa[rnd : rnd + 1, :]
    lists_ref[pl.ds(2, ng.shape[1]), pl.ds(0, ng.shape[2])] = ng[rnd]


def prepare_round(rnd, pu, pa, ng, users, ads, prep):
    groups = ng.shape[1]
    edges = pu.shape[1] // groups
    for g in range(groups):
        cols = pl.ds(g * edges, edges)
        prepare(g, pu[rnd : rnd + 1, cols], pa[rnd : rnd + 1, cols], ng[rnd, g : g + 1, :], users, ads, *prep)


def second_group(u_ref, at1, amt1, ato_ref, amto_ref, prep, gh_ref, gl_ref, ah_ref, al_ref):
    at_hl = split(at1)
    ah_ref[...], al_ref[...] = at_hl
    ga = group_pass(1, reader(u_ref), u_ref.shape[0], at_hl, prep, None, (gh_ref, gl_ref))
    ato_ref[...], amto_ref[...] = adagrad(at1, amt1, ga)


def first_round_kernel(
    pu_hbm, pa_hbm, ng_hbm, u_hbm, a_hbm, um_hbm, am_hbm,
    uo_ref, umo_ref, ads_ref, gh_ref, gl_ref, ah_ref, al_ref, pu, pa, ng,
    mh, cu, cn, u_ref, um_ref, a_ref, am_ref, sems, table_sems,
):
    copies = fetch_indices(pu_hbm, pa_hbm, ng_hbm, pu, pa, ng, sems)
    tables = [
        pltpu.make_async_copy(src, dst, table_sems.at[k])
        for k, (src, dst) in enumerate(
            ((u_hbm, u_ref), (a_hbm, a_ref), (um_hbm, um_ref), (am_hbm, am_ref))
        )
    ]
    for c in tables:
        c.start()
    for c in copies:
        c.wait()
    prep = (mh, cu, cn)
    prepare_round(0, pu, pa, ng, u_ref.shape[0], a_ref.shape[0], prep)
    for c in tables:
        c.wait()
    at = a_ref[...].T
    amt = am_ref[...].T
    put = update_users(reader(u_ref), reader(um_ref), uo_ref, umo_ref)
    ga = group_pass(0, reader(u_ref), u_ref.shape[0], split(at), prep, put)
    at1, amt1 = adagrad(at, amt, ga)
    second_group(uo_ref, at1, amt1, ads_ref.at[0], ads_ref.at[1], prep, gh_ref, gl_ref, ah_ref, al_ref)


def meeting(u_read, um_read, at, amt, prep, u1_ref, um1_ref, uo_ref, umo_ref):
    users = u1_ref.shape[0]
    ga = group_pass(0, u_read, users, split(at), prep, update_users(u_read, um_read, u1_ref, um1_ref))
    at1, amt1 = adagrad(at, amt, ga)
    u_read = reader(u1_ref)
    ga = group_pass(1, u_read, users, split(at1), prep, update_users(u_read, reader(um1_ref), uo_ref, umo_ref))
    return adagrad(at1, amt1, ga)


def early_kernel(u_ref, um_ref, near_ref, mh, cu, cn, ads_ref, users_ref, u1_ref, um1_ref):
    ads_ref[0], ads_ref[1] = meeting(
        reader(u_ref), reader(um_ref), near_ref[0], near_ref[1], (mh, cu, cn),
        u1_ref, um1_ref, users_ref.at[0], users_ref.at[1],
    )


def late_kernel(
    u_ref, um_ref, far_ref, mh, cu, cn, after_ref, lists_ref,
    u1_ref, um1_ref, ato_ref, amto_ref, gh_ref, gl_ref, ah_ref, al_ref,
):
    prep = (mh, cu, cn)
    at = far_ref[0]
    u_read = reader(u_ref)
    put = update_users(u_read, reader(um_ref), u1_ref, um1_ref)
    ga = group_pass(0, u_read, u_ref.shape[0], split(at), prep, put)
    at1, amt1 = adagrad(at, far_ref[1], ga)
    second_group(u1_ref, at1, amt1, ato_ref, amto_ref, prep, gh_ref, gl_ref, ah_ref, al_ref)


def pick_kernel(
    ue_ref, ume_ref, users_ref, ads_ref, ato_ref, amto_ref, mh, cu, cn,
    ads_out_ref, users_out_ref, u1_ref, um1_ref,
):
    odd = on_odd_core()
    at = jnp.where(odd, ato_ref[...], ads_ref[0])
    amt = jnp.where(odd, amto_ref[...], ads_ref[1])
    u_read, um_read = picker(odd, ue_ref, users_ref.at[0]), picker(odd, ume_ref, users_ref.at[1])
    ads_out_ref[0], ads_out_ref[1] = meeting(
        u_read, um_read, at, amt, (mh, cu, cn), u1_ref, um1_ref, users_out_ref.at[0], users_out_ref.at[1]
    )


def whole_kernel(users_ref, ads_ref, mh, cu, cn, ads_out_ref, users_out_ref, u1_ref, um1_ref):
    u_read, um_read = reader(users_ref.at[0]), reader(users_ref.at[1])
    ads_out_ref[0], ads_out_ref[1] = meeting(
        u_read, um_read, ads_ref[0], ads_ref[1], (mh, cu, cn), u1_ref, um1_ref,
        users_out_ref.at[0], users_out_ref.at[1],
    )


def users_kernel(u_ref, um_ref, gh_ref, gl_ref, ah_ref, al_ref, uo_ref, umo_ref):
    put = update_users(reader(u_ref), reader(um_ref), uo_ref, umo_ref)
    at_hl = ah_ref[...], al_ref[...]
    for r in range(0, u_ref.shape[0], BLOCK):
        rows = pl.ds(r, BLOCK)
        put(rows, dot3((gh_ref[rows, :], gl_ref[rows, :]), at_hl, 1, 1))


def prepare_kernel(rnd, pack, after_ref, pu, pa, ng, mh, cu, cn, lists_ref):
    prepare_round(rnd, pu, pa, ng, mh.shape[1], mh.shape[2], (mh, cu, cn))
    pack_lists(pack, pu, pa, ng, lists_ref)


def prepare_both_kernel(
    rnd, after_ref, lists_ref, pu_hbm, pa_hbm, ng_hbm, mh, cu, cn, mh2, cu2, cn2, pu, pa, ng, sems,
):
    copies = fetch_indices(pu_hbm, pa_hbm, ng_hbm, pu, pa, ng, sems, away=True)
    groups, users, ads = mh.shape
    n = ng_hbm.shape[-1]
    size = pu_hbm.shape[-1] // groups
    for g in range(groups):
        cols = pl.ds(g * size, size)
        negs = lists_ref[2 + g : 3 + g, pl.ds(0, n)]
        prepare(g, lists_ref[0:1, cols], lists_ref[1:2, cols], negs, users, ads, mh2, cu2, cn2)
    for c in copies:
        c.wait()
    prepare_round(rnd, pu, pa, ng, users, ads, (mh, cu, cn))


def call(kernel, ins, outs, scratch=(), hbm=0, name=None, out_place=pltpu.VMEM):
    vmem = pl.BlockSpec(memory_space=pltpu.VMEM)
    split_at = len(ins) - hbm
    far = [pltpu.with_memory_space_constraint(x, pltpu.HBM) for x in ins[split_at:]]
    return pl.pallas_call(
        kernel,
        out_shape=outs,
        in_specs=[vmem] * split_at + [pl.BlockSpec(memory_space=pltpu.HBM)] * hbm,
        out_specs=[pl.BlockSpec(memory_space=out_place)] * len(outs),
        scratch_shapes=list(scratch),
        compiler_params=pltpu.CompilerParams(vmem_limit_bytes=VMEM_LIMIT),
        cost_estimate=pl.CostEstimate(flops=1, bytes_accessed=1, transcendentals=0),
        name=name,
    )(*ins[:split_at], *far)


def last_kernel(ads_ref, users_ref, u_hbm, um_hbm, a_hbm, am_hbm, turned, sems, user_sems):
    copies = [
        pltpu.make_async_copy(users_ref.at[0], u_hbm, user_sems.at[0]),
        pltpu.make_async_copy(users_ref.at[1], um_hbm, user_sems.at[1]),
    ]
    for c in copies:
        c.start()
    size = turned.shape[1] // PARTS_OUT
    for t, out_hbm in enumerate((a_hbm, am_hbm)):
        for k in range(PARTS_OUT):
            rows = pl.ds(k * size, size)
            turned[t, rows, :] = ads_ref[t, :, rows].T
            copies.append(pltpu.make_async_copy(turned.at[t, rows, :], out_hbm.at[rows, :], sems.at[t * PARTS_OUT + k]))
            copies[-1].start()
    for c in copies:
        c.wait()


def move(arrays, *kinds):
    blocks, cycles = lax.axis_size("blk"), lax.axis_size("pair")
    route = []
    for b in range(blocks):
        for p in range(cycles):
            steps, flip = kinds[b % len(kinds)]
            to = (b + steps) % blocks, p ^ (cycles // 2 if flip else 0)
            route.append((b * cycles + p, to[0] * cycles + to[1]))
    return tuple(lax.ppermute(x, AXES, route) for x in arrays)


def local(users, user_moms, ads, ad_moments, pos_user, pos_ad, neg_ad):
    nu, d = users.shape
    na = ads.shape[0]
    rounds, groups, n = neg_ad.shape[2:]
    edges = pos_user.shape[3]
    indices = (pos_user, pos_ad, neg_ad)

    def shape(*dims, dtype=F32):
        return jax.ShapeDtypeStruct(dims, dtype)

    table_u, table_a = shape(nu, d), shape(d, na)
    parts = [shape(nu, na, dtype=BF16)] * 2 + [shape(d, na, dtype=BF16)] * 2
    index_scratch = [
        pltpu.VMEM((rounds, edges), jnp.int32),
        pltpu.VMEM((rounds, edges), jnp.int32),
        pltpu.VMEM((rounds, groups, n), jnp.int32),
    ]
    sems = pltpu.SemaphoreType.DMA((3,))
    prep_shapes = [shape(groups, nu, na, dtype=BF16), shape(groups, nu, 128), shape(groups, 8, na)]
    prep_scratch = [pltpu.VMEM(s.shape, s.dtype) for s in prep_shapes]

    def update(u, um, g):
        return call(users_kernel, (u, um, *g), [table_u, table_u], name="users_update")

    stay, away = (0, False), (0, True)
    both_u, both_a = shape(2, nu, d), shape(2, d, na)
    users_scratch = [pltpu.VMEM((nu, d), F32)] * 2
    own_lists = [shape(rounds, edges, dtype=jnp.int32)] * 2 + [shape(rounds, groups, n, dtype=jnp.int32)]
    u, um, ads_now, *rest = call(
        first_round_kernel,
        (*indices, users, ads, user_moms, ad_moments),
        [table_u, table_u, both_a, *parts, *own_lists],
        [*prep_scratch, *users_scratch, *[pltpu.VMEM((na, d), F32)] * 2, sems, pltpu.SemaphoreType.DMA((4,))],
        hbm=7, name="round_first",
    )
    g, own_lists = rest[: len(parts)], rest[len(parts) :]
    (near,) = move((ads_now,), (1, False), (-1, False))
    (far,) = move((ads_now,), (1, False), (1, False))
    u, um = update(u, um, g)
    *prep, lists = call(
        functools.partial(prepare_kernel, 1, rounds - 1), (um, *own_lists),
        prep_shapes + [shape(8, max(edges, n), dtype=jnp.int32)], name="counts_1",
    )
    (lists,) = move((lists,), (-4, False), stay, stay, stay)

    ads_early, after = call(early_kernel, (u, um, near, *prep), [both_a, both_u], users_scratch, name="round_early")
    (ads_early,) = move((ads_early,), (1, False), (1, True))
    (users_early,) = move((after,), stay, away)

    u, um, at, amt, *g = call(
        late_kernel, (u, um, far, *prep, after, lists), [table_u, table_u, table_a, table_a, *parts], name="round_late",
    )
    ads_late = move((at, amt), (1, False), (-1, False))
    u, um = update(u, um, g)
    preps = call(
        functools.partial(prepare_both_kernel, 2), (um, lists, *indices), prep_shapes * 2, [*index_scratch, sems], hbm=3,
        name="counts_23",
    )
    prep, prep_last = preps[: len(prep_shapes)], preps[len(prep_shapes) :]

    ads_now, users_now = call(
        pick_kernel, (u, um, users_early, ads_early, *ads_late, *prep), [both_a, both_u], users_scratch, name="round_pick",
    )
    (users_now,) = move((users_now,), (-4, False), away, stay, away)
    (ads_now,) = move((ads_now,), (1, False), (1, True), (1, False), (-3, True))
    ads_now, users_now = call(
        whole_kernel, (users_now, ads_now, *prep_last), [both_a, both_u], users_scratch, name="round_last",
    )
    (users_now,) = move((users_now,), (4, False), stay, stay, stay)
    (ads_now,) = move((ads_now,), (1, True), (-3, True), (-3, True), (-3, True))
    return call(
        last_kernel, (ads_now, users_now), [pltpu.HBM((nu, d), F32)] * 2 + [pltpu.HBM((na, d), F32)] * 2,
        [pltpu.VMEM((2, na, d), F32), pltpu.SemaphoreType.DMA((2 * PARTS_OUT,)), pltpu.SemaphoreType.DMA((2,))],
        name="last_out", out_place=pltpu.HBM,
    )


def solution(mesh):
    rows = P(AXES, None)
    return jax.shard_map(
        local,
        mesh=mesh,
        in_specs=(rows, rows, rows, rows, P("blk", None, None, None), P("blk", None, None, None), P("blk", None, None, None, None)),
        out_specs=(rows, rows, rows, rows),
        check_vma=False,
    )
```

```python
import functools

import jax
import jax.numpy as jnp
from jax import lax
from jax.experimental import pallas as pl
from jax.experimental.pallas import tpu as pltpu
from jax.sharding import PartitionSpec as P

LEARN_RATE = 0.1
EPS = 1e-08
F32 = jnp.float32
BF16 = jnp.bfloat16
LANES = 128
PARTS_OUT = 4
AXES = ("blk", "pair")
VMEM_LIMIT = 28 * 1024 * 1024


def dot(a, b, ca, cb):
    return lax.dot_general(a, b, (((ca,), (cb,)), ((), ())), preferred_element_type=F32)


def split(x):
    hi = x.astype(BF16)
    return hi, (x - hi.astype(F32)).astype(BF16)


def dot3(a, b, ca, cb):
    (ah, al), (bh, bl) = a, b
    return dot(jnp.concatenate([ah, al, ah], axis=ca), jnp.concatenate([bh, bh, bl], axis=cb), ca, cb)


def adagrad(row, mom, grad):
    mom = mom + grad * grad
    return row - LEARN_RATE * grad / (jnp.sqrt(mom) + EPS), mom


def onehot(idx, count):
    rows = lax.broadcasted_iota(jnp.int32, (count, idx.shape[1]), 0)
    return jnp.where(rows == idx, F32(1), F32(0)).astype(BF16)


def prepare(group, pu, pa, ng, users, ads, mh_ref, cu_ref, cn_ref):
    n = ng.shape[1]
    hot_u = onehot(pu, users)
    hot_a = onehot(pa, ads)
    mh_ref[group] = (0.5 * dot(hot_u, hot_a, 1, 1)).astype(BF16)
    ones = jnp.ones((pu.shape[1], 128), BF16)
    cu_ref[group] = dot(hot_u, ones, 1, 0) * F32(0.5 / n**0.5)
    hi = lax.shift_right_logical(ng, LANES.bit_length() - 1)
    counts = dot(onehot(hi, 8), onehot(ng - hi * LANES, LANES), 1, 1)
    for k in range(ads // LANES):
        cols = pl.ds(k * LANES, LANES)
        cn_ref[group, :, cols] = jnp.broadcast_to(counts[k : k + 1, :], (8, LANES))


def gradient_matrix(s, mh, cu, cn):
    t = jnp.tanh(0.5 * s)
    w = jnp.concatenate([cu] * (s.shape[1] // 128), axis=1) * cn
    m = mh.astype(F32)
    return split((w + m) * t + (w - m))


BLOCK = 256


def group_pass(group, u_read, users, at_hl, prep, gu_out, g_out=None):
    mh_ref, cu_ref, cn_ref = prep
    cn = cn_ref[group, 0:1, :]
    blocks = [pl.ds(r, BLOCK) for r in range(0, users, BLOCK)]
    u_hl = [split(u_read(rows)) for rows in blocks]
    scores = [dot3(u, at_hl, 1, 0) for u in u_hl]
    ga = None
    for rows, u, s in zip(blocks, u_hl, scores):
        g_hl = gradient_matrix(s, mh_ref[group, rows, :], cu_ref[group, rows, :], cn)
        if g_out is None:
            gu_out(rows, dot3(g_hl, at_hl, 1, 1))
        else:
            g_out[0][rows, :], g_out[1][rows, :] = g_hl
        part = dot3(u, g_hl, 0, 0)
        ga = part if ga is None else ga + part
    return ga


def reader(ref):
    return lambda rows: ref[rows, :]


def picker(odd, even_ref, odd_ref):
    return lambda rows: jnp.where(odd, odd_ref[rows, :], even_ref[rows, :])


def update_users(u_read, um_read, uo_ref, umo_ref):
    def put(rows, grad):
        uo_ref[rows, :], umo_ref[rows, :] = adagrad(u_read(rows), um_read(rows), grad)

    return put


def on_odd_core():
    return lax.rem(lax.axis_index("blk"), 2) == 1


def fetch_indices(pu_hbm, pa_hbm, ng_hbm, pu, pa, ng, sems, away=False):
    cycle = lax.axis_index("pair")
    if away:
        count = lax.axis_size("pair")
        cycle = lax.rem(cycle + jnp.where(on_odd_core(), count // 2, 0), count)
    copies = [
        pltpu.make_async_copy(src.at[0, cycle], dst, sems.at[k])
        for k, (src, dst) in enumerate(((pu_hbm, pu), (pa_hbm, pa), (ng_hbm, ng)))
    ]
    for c in copies:
        c.start()
    return copies


def pack_lists(rnd, pu, pa, ng, lists_ref):
    lists_ref[...] = jnp.zeros_like(lists_ref)
    lists_ref[0:1, pl.ds(0, pu.shape[1])] = pu[rnd : rnd + 1, :]
    lists_ref[1:2, pl.ds(0, pa.shape[1])] = pa[rnd : rnd + 1, :]
    lists_ref[pl.ds(2, ng.shape[1]), pl.ds(0, ng.shape[2])] = ng[rnd]


def prepare_round(rnd, pu, pa, ng, users, ads, prep):
    groups = ng.shape[1]
    edges = pu.shape[1] // groups
    for g in range(groups):
        cols = pl.ds(g * edges, edges)
        prepare(g, pu[rnd : rnd + 1, cols], pa[rnd : rnd + 1, cols], ng[rnd, g : g + 1, :], users, ads, *prep)


def second_group(u_ref, at1, amt1, prep, gh_ref, gl_ref, ah_ref, al_ref):
    at_hl = split(at1)
    ah_ref[...], al_ref[...] = at_hl
    ga = group_pass(1, reader(u_ref), u_ref.shape[0], at_hl, prep, None, (gh_ref, gl_ref))
    return adagrad(at1, amt1, ga)


def first_round_kernel(
    pu_hbm, pa_hbm, ng_hbm, u_hbm, a_hbm, um_hbm, am_hbm,
    uo_ref, umo_ref, ads_ref, gh_ref, gl_ref, ah_ref, al_ref, pu, pa, ng,
    mh, cu, cn, u_ref, um_ref, a_ref, am_ref, sems, table_sems,
):
    copies = fetch_indices(pu_hbm, pa_hbm, ng_hbm, pu, pa, ng, sems)
    tables = [
        pltpu.make_async_copy(src, dst, table_sems.at[k])
        for k, (src, dst) in enumerate(
            ((u_hbm, u_ref), (a_hbm, a_ref), (um_hbm, um_ref), (am_hbm, am_ref))
        )
    ]
    for c in tables:
        c.start()
    for c in copies:
        c.wait()
    prep = (mh, cu, cn)
    prepare_round(0, pu, pa, ng, u_ref.shape[0], a_ref.shape[0], prep)
    for c in tables:
        c.wait()
    at = a_ref[...].T
    amt = am_ref[...].T
    put = update_users(reader(u_ref), reader(um_ref), uo_ref, umo_ref)
    ga = group_pass(0, reader(u_ref), u_ref.shape[0], split(at), prep, put)
    at1, amt1 = adagrad(at, amt, ga)
    ads_ref[0], ads_ref[1] = second_group(uo_ref, at1, amt1, prep, gh_ref, gl_ref, ah_ref, al_ref)


def meeting(u_read, um_read, at, amt, prep, u1_ref, um1_ref, uo_ref, umo_ref):
    users = u1_ref.shape[0]
    ga = group_pass(0, u_read, users, split(at), prep, update_users(u_read, um_read, u1_ref, um1_ref))
    at1, amt1 = adagrad(at, amt, ga)
    u_read = reader(u1_ref)
    ga = group_pass(1, u_read, users, split(at1), prep, update_users(u_read, reader(um1_ref), uo_ref, umo_ref))
    return adagrad(at1, amt1, ga)


def early_kernel(u_ref, um_ref, near_ref, mh, cu, cn, ads_ref, users_ref, u1_ref, um1_ref):
    ads_ref[0], ads_ref[1] = meeting(
        reader(u_ref), reader(um_ref), near_ref[0], near_ref[1], (mh, cu, cn),
        u1_ref, um1_ref, users_ref.at[0], users_ref.at[1],
    )


def late_kernel(
    u_ref, um_ref, far_ref, mh, cu, cn, after_ref, lists_ref,
    u1_ref, um1_ref, ato_ref, amto_ref, gh_ref, gl_ref, ah_ref, al_ref,
):
    prep = (mh, cu, cn)
    at = far_ref[0]
    u_read = reader(u_ref)
    put = update_users(u_read, reader(um_ref), u1_ref, um1_ref)
    ga = group_pass(0, u_read, u_ref.shape[0], split(at), prep, put)
    at1, amt1 = adagrad(at, far_ref[1], ga)
    ato_ref[...], amto_ref[...] = second_group(u1_ref, at1, amt1, prep, gh_ref, gl_ref, ah_ref, al_ref)


def pick_kernel(
    ue_ref, ume_ref, users_ref, ads_ref, ato_ref, amto_ref, mh, cu, cn,
    un_ref, umn_ref, atn_ref, amtn_ref, u1_ref, um1_ref,
):
    odd = on_odd_core()
    at = jnp.where(odd, ato_ref[...], ads_ref[0])
    amt = jnp.where(odd, amto_ref[...], ads_ref[1])
    u_read, um_read = picker(odd, ue_ref, users_ref.at[0]), picker(odd, ume_ref, users_ref.at[1])
    atn_ref[...], amtn_ref[...] = meeting(
        u_read, um_read, at, amt, (mh, cu, cn), u1_ref, um1_ref, un_ref, umn_ref
    )


def gradient_kernel(u_ref, at_ref, mh, cu, cn, gu_ref, ga_ref):
    def put(rows, grad):
        gu_ref[rows, :] = grad

    ga_ref[...] = group_pass(0, reader(u_ref), u_ref.shape[0], split(at_ref[...]), (mh, cu, cn), put)


def last_end_kernel(
    u_ref, um_ref, at_ref, amt_ref, gu_ref, ga_ref, mh, cu, cn, ads_ref, users_ref, u1_ref, um1_ref,
):
    u1_ref[...], um1_ref[...] = adagrad(u_ref[...], um_ref[...], gu_ref[...])
    at1, amt1 = adagrad(at_ref[...], amt_ref[...], ga_ref[...])
    put = update_users(reader(u1_ref), reader(um1_ref), users_ref.at[0], users_ref.at[1])
    ga = group_pass(1, reader(u1_ref), u1_ref.shape[0], split(at1), (mh, cu, cn), put)
    ads_ref[0], ads_ref[1] = adagrad(at1, amt1, ga)


def users_kernel(u_ref, um_ref, gh_ref, gl_ref, ah_ref, al_ref, uo_ref, umo_ref):
    put = update_users(reader(u_ref), reader(um_ref), uo_ref, umo_ref)
    at_hl = ah_ref[...], al_ref[...]
    for r in range(0, u_ref.shape[0], BLOCK):
        rows = pl.ds(r, BLOCK)
        put(rows, dot3((gh_ref[rows, :], gl_ref[rows, :]), at_hl, 1, 1))


def prepare_kernel(rnd, pack, after_ref, pu, pa, ng, mh, cu, cn, lists_ref):
    prepare_round(rnd, pu, pa, ng, mh.shape[1], mh.shape[2], (mh, cu, cn))
    pack_lists(pack, pu, pa, ng, lists_ref)


def prepare_both_kernel(
    rnd, after_ref, lists_ref, pu_hbm, pa_hbm, ng_hbm, mh, cu, cn, mh2, cu2, cn2, pu, pa, ng, sems,
):
    copies = fetch_indices(pu_hbm, pa_hbm, ng_hbm, pu, pa, ng, sems, away=True)
    groups, users, ads = mh.shape
    n = ng_hbm.shape[-1]
    size = pu_hbm.shape[-1] // groups
    for g in range(groups):
        cols = pl.ds(g * size, size)
        negs = lists_ref[2 + g : 3 + g, pl.ds(0, n)]
        prepare(g, lists_ref[0:1, cols], lists_ref[1:2, cols], negs, users, ads, mh2, cu2, cn2)
    for c in copies:
        c.wait()
    prepare_round(rnd, pu, pa, ng, users, ads, (mh, cu, cn))


def call(kernel, ins, outs, scratch=(), hbm=0, name=None, out_place=pltpu.VMEM):
    vmem = pl.BlockSpec(memory_space=pltpu.VMEM)
    split_at = len(ins) - hbm
    far = [pltpu.with_memory_space_constraint(x, pltpu.HBM) for x in ins[split_at:]]
    return pl.pallas_call(
        kernel,
        out_shape=outs,
        in_specs=[vmem] * split_at + [pl.BlockSpec(memory_space=pltpu.HBM)] * hbm,
        out_specs=[pl.BlockSpec(memory_space=out_place)] * len(outs),
        scratch_shapes=list(scratch),
        compiler_params=pltpu.CompilerParams(vmem_limit_bytes=VMEM_LIMIT),
        cost_estimate=pl.CostEstimate(flops=1, bytes_accessed=1, transcendentals=0),
        name=name,
    )(*ins[:split_at], *far)


def last_kernel(users_ref, ads_ref, u_hbm, um_hbm, a_hbm, am_hbm, turned, sems, user_sems):
    copies = [
        pltpu.make_async_copy(users_ref.at[0], u_hbm, user_sems.at[0]),
        pltpu.make_async_copy(users_ref.at[1], um_hbm, user_sems.at[1]),
    ]
    for c in copies:
        c.start()
    size = turned.shape[1] // PARTS_OUT
    for t, out_hbm in enumerate((a_hbm, am_hbm)):
        for k in range(PARTS_OUT):
            rows = pl.ds(k * size, size)
            turned[t, rows, :] = ads_ref[t, :, rows].T
            copies.append(pltpu.make_async_copy(turned.at[t, rows, :], out_hbm.at[rows, :], sems.at[t * PARTS_OUT + k]))
            copies[-1].start()
    for c in copies:
        c.wait()


def move(arrays, *kinds):
    blocks, cycles = lax.axis_size("blk"), lax.axis_size("pair")
    route = []
    for b in range(blocks):
        for p in range(cycles):
            steps, flip = kinds[b % len(kinds)]
            to = (b + steps) % blocks, p ^ (cycles // 2 if flip else 0)
            route.append((b * cycles + p, to[0] * cycles + to[1]))
    return tuple(lax.ppermute(x, AXES, route) for x in arrays)


def local(users, user_moms, ads, ad_moments, pos_user, pos_ad, neg_ad):
    nu, d = users.shape
    na = ads.shape[0]
    rounds, groups, n = neg_ad.shape[2:]
    edges = pos_user.shape[3]
    indices = (pos_user, pos_ad, neg_ad)

    def shape(*dims, dtype=F32):
        return jax.ShapeDtypeStruct(dims, dtype)

    table_u, table_a = shape(nu, d), shape(d, na)
    parts = [shape(nu, na, dtype=BF16)] * 2 + [shape(d, na, dtype=BF16)] * 2
    index_scratch = [
        pltpu.VMEM((rounds, edges), jnp.int32),
        pltpu.VMEM((rounds, edges), jnp.int32),
        pltpu.VMEM((rounds, groups, n), jnp.int32),
    ]
    sems = pltpu.SemaphoreType.DMA((3,))
    prep_shapes = [shape(groups, nu, na, dtype=BF16), shape(groups, nu, 128), shape(groups, 8, na)]
    prep_scratch = [pltpu.VMEM(s.shape, s.dtype) for s in prep_shapes]

    def update(u, um, g):
        return call(users_kernel, (u, um, *g), [table_u, table_u], name="users_update")

    stay, away = (0, False), (0, True)
    both_u, both_a = shape(2, nu, d), shape(2, d, na)
    users_scratch = [pltpu.VMEM((nu, d), F32)] * 2
    own_lists = [shape(rounds, edges, dtype=jnp.int32)] * 2 + [shape(rounds, groups, n, dtype=jnp.int32)]
    u, um, ads_now, *rest = call(
        first_round_kernel,
        (*indices, users, ads, user_moms, ad_moments),
        [table_u, table_u, both_a, *parts, *own_lists],
        [*prep_scratch, *users_scratch, *[pltpu.VMEM((na, d), F32)] * 2, sems, pltpu.SemaphoreType.DMA((4,))],
        hbm=7, name="round_first",
    )
    g, own_lists = rest[: len(parts)], rest[len(parts) :]
    (near,) = move((ads_now,), (1, False), (-1, False))
    (far,) = move((ads_now,), (1, False), (1, False))
    u, um = update(u, um, g)
    *prep, lists = call(
        functools.partial(prepare_kernel, 1, rounds - 1), (um, *own_lists),
        prep_shapes + [shape(8, max(edges, n), dtype=jnp.int32)], name="counts_1",
    )
    (lists,) = move((lists,), (-4, False), stay, stay, stay)

    ads_early, after = call(early_kernel, (u, um, near, *prep), [both_a, both_u], users_scratch, name="round_early")
    (ads_early,) = move((ads_early,), (1, False), (1, True))
    (users_early,) = move((after,), stay, away)

    u, um, at, amt, *g = call(
        late_kernel, (u, um, far, *prep, after, lists), [table_u, table_u, table_a, table_a, *parts], name="round_late",
    )
    ads_late = move((at, amt), (1, False), (-1, False))
    u, um = update(u, um, g)
    preps = call(
        functools.partial(prepare_both_kernel, 2), (um, lists, *indices), prep_shapes * 2, [*index_scratch, sems], hbm=3,
        name="counts_23",
    )
    prep, prep_last = preps[: len(prep_shapes)], preps[len(prep_shapes) :]

    u, um, at, amt = call(
        pick_kernel, (u, um, users_early, ads_early, *ads_late, *prep), [table_u, table_u, table_a, table_a],
        users_scratch, name="round_pick",
    )
    u, um = move((u, um), (-4, False), away, stay, away)
    at, amt = move((at, amt), (1, False), (1, True), (1, False), (-3, True))
    gu, ga = call(gradient_kernel, (u, at, *prep_last), [table_u, table_a], name="round_last_gradients")
    ads_now, users_now = call(
        last_end_kernel, (u, um, at, amt, gu, ga, *prep_last), [both_a, both_u], users_scratch, name="round_last_end",
    )
    (users_now,) = move((users_now,), (4, False), stay, stay, stay)
    (ads_now,) = move((ads_now,), (1, True), (-3, True), (-3, True), (-3, True))
    return call(
        last_kernel, (users_now, ads_now), [pltpu.HBM((nu, d), F32)] * 2 + [pltpu.HBM((na, d), F32)] * 2,
        [pltpu.VMEM((2, na, d), F32), pltpu.SemaphoreType.DMA((2 * PARTS_OUT,)), pltpu.SemaphoreType.DMA((2,))],
        name="last_out", out_place=pltpu.HBM,
    )


def solution(mesh):
    rows = P(AXES, None)
    return jax.shard_map(
        local,
        mesh=mesh,
        in_specs=(rows, rows, rows, rows, P("blk", None, None, None), P("blk", None, None, None), P("blk", None, None, None, None)),
        out_specs=(rows, rows, rows, rows),
        check_vma=False,
    )
```

```python
import functools

import jax
import jax.numpy as jnp
from jax import lax
from jax.experimental import pallas as pl
from jax.experimental.pallas import tpu as pltpu
from jax.sharding import PartitionSpec as P

LEARN_RATE = 0.1
EPS = 1e-08
F32 = jnp.float32
BF16 = jnp.bfloat16
LANES = 128
PARTS_OUT = 4
AXES = ("blk", "pair")
VMEM_LIMIT = 28 * 1024 * 1024


def dot(a, b, ca, cb):
    return lax.dot_general(a, b, (((ca,), (cb,)), ((), ())), preferred_element_type=F32)


def split(x):
    hi = x.astype(BF16)
    return hi, (x - hi.astype(F32)).astype(BF16)


def dot3(a, b, ca, cb):
    (ah, al), (bh, bl) = a, b
    return dot(jnp.concatenate([ah, al, ah], axis=ca), jnp.concatenate([bh, bh, bl], axis=cb), ca, cb)


def adagrad(row, mom, grad):
    mom = mom + grad * grad
    return row - LEARN_RATE * grad / (jnp.sqrt(mom) + EPS), mom


def onehot(idx, count):
    rows = lax.broadcasted_iota(jnp.int32, (count, idx.shape[1]), 0)
    return jnp.where(rows == idx, F32(1), F32(0)).astype(BF16)


def prepare(group, pu, pa, ng, users, ads, mh_ref, cu_ref, cn_ref):
    n = ng.shape[1]
    hot_u = onehot(pu, users)
    hot_a = onehot(pa, ads)
    mh_ref[group] = (0.5 * dot(hot_u, hot_a, 1, 1)).astype(BF16)
    ones = jnp.ones((pu.shape[1], 128), BF16)
    cu_ref[group] = dot(hot_u, ones, 1, 0) * F32(0.5 / n**0.5)
    hi = lax.shift_right_logical(ng, LANES.bit_length() - 1)
    counts = dot(onehot(hi, 8), onehot(ng - hi * LANES, LANES), 1, 1)
    for k in range(ads // LANES):
        cols = pl.ds(k * LANES, LANES)
        cn_ref[group, :, cols] = jnp.broadcast_to(counts[k : k + 1, :], (8, LANES))


def gradient_matrix(s, mh, cu, cn):
    t = jnp.tanh(0.5 * s)
    w = jnp.concatenate([cu] * (s.shape[1] // 128), axis=1) * cn
    m = mh.astype(F32)
    return split((w + m) * t + (w - m))


BLOCK = 256


def group_pass(group, u_read, users, at_hl, prep, gu_out, g_out=None):
    mh_ref, cu_ref, cn_ref = prep
    cn = cn_ref[group, 0:1, :]
    blocks = [pl.ds(r, BLOCK) for r in range(0, users, BLOCK)]
    u_hl = [split(u_read(rows)) for rows in blocks]
    scores = [dot3(u, at_hl, 1, 0) for u in u_hl]
    ga = None
    for rows, u, s in zip(blocks, u_hl, scores):
        g_hl = gradient_matrix(s, mh_ref[group, rows, :], cu_ref[group, rows, :], cn)
        if g_out is None:
            gu_out(rows, dot3(g_hl, at_hl, 1, 1))
        else:
            g_out[0][rows, :], g_out[1][rows, :] = g_hl
        part = dot3(u, g_hl, 0, 0)
        ga = part if ga is None else ga + part
    return ga


def reader(ref):
    return lambda rows: ref[rows, :]


def picker(odd, even_ref, odd_ref):
    return lambda rows: jnp.where(odd, odd_ref[rows, :], even_ref[rows, :])


def update_users(u_read, um_read, uo_ref, umo_ref):
    def put(rows, grad):
        uo_ref[rows, :], umo_ref[rows, :] = adagrad(u_read(rows), um_read(rows), grad)

    return put


def on_odd_core():
    return lax.rem(lax.axis_index("blk"), 2) == 1


def fetch_indices(pu_hbm, pa_hbm, ng_hbm, pu, pa, ng, sems, away=False):
    cycle = lax.axis_index("pair")
    if away:
        count = lax.axis_size("pair")
        cycle = lax.rem(cycle + jnp.where(on_odd_core(), count // 2, 0), count)
    copies = [
        pltpu.make_async_copy(src.at[0, cycle], dst, sems.at[k])
        for k, (src, dst) in enumerate(((pu_hbm, pu), (pa_hbm, pa), (ng_hbm, ng)))
    ]
    for c in copies:
        c.start()
    return copies


def pack_lists(rnd, pu, pa, ng, lists_ref):
    lists_ref[...] = jnp.zeros_like(lists_ref)
    lists_ref[0:1, pl.ds(0, pu.shape[1])] = pu[rnd : rnd + 1, :]
    lists_ref[1:2, pl.ds(0, pa.shape[1])] = pa[rnd : rnd + 1, :]
    lists_ref[pl.ds(2, ng.shape[1]), pl.ds(0, ng.shape[2])] = ng[rnd]


def prepare_round(rnd, pu, pa, ng, users, ads, prep):
    groups = ng.shape[1]
    edges = pu.shape[1] // groups
    for g in range(groups):
        cols = pl.ds(g * edges, edges)
        prepare(g, pu[rnd : rnd + 1, cols], pa[rnd : rnd + 1, cols], ng[rnd, g : g + 1, :], users, ads, *prep)


def second_group(u_ref, at1, amt1, prep, gh_ref, gl_ref, ah_ref, al_ref):
    at_hl = split(at1)
    ah_ref[...], al_ref[...] = at_hl
    ga = group_pass(1, reader(u_ref), u_ref.shape[0], at_hl, prep, None, (gh_ref, gl_ref))
    return adagrad(at1, amt1, ga)


def first_round_kernel(
    pu_hbm, pa_hbm, ng_hbm, u_hbm, a_hbm, um_hbm, am_hbm,
    uo_ref, umo_ref, ads_ref, gh_ref, gl_ref, ah_ref, al_ref, pu, pa, ng,
    mh, cu, cn, u_ref, um_ref, a_ref, am_ref, sems, table_sems,
):
    copies = fetch_indices(pu_hbm, pa_hbm, ng_hbm, pu, pa, ng, sems)
    tables = [
        pltpu.make_async_copy(src, dst, table_sems.at[k])
        for k, (src, dst) in enumerate(
            ((u_hbm, u_ref), (a_hbm, a_ref), (um_hbm, um_ref), (am_hbm, am_ref))
        )
    ]
    for c in tables:
        c.start()
    for c in copies:
        c.wait()
    prep = (mh, cu, cn)
    prepare_round(0, pu, pa, ng, u_ref.shape[0], a_ref.shape[0], prep)
    for c in tables:
        c.wait()
    at = a_ref[...].T
    amt = am_ref[...].T
    put = update_users(reader(u_ref), reader(um_ref), uo_ref, umo_ref)
    ga = group_pass(0, reader(u_ref), u_ref.shape[0], split(at), prep, put)
    at1, amt1 = adagrad(at, amt, ga)
    ads_ref[0], ads_ref[1] = second_group(uo_ref, at1, amt1, prep, gh_ref, gl_ref, ah_ref, al_ref)


def meeting(u_read, um_read, at, amt, prep, u1_ref, um1_ref, uo_ref, umo_ref):
    users = u1_ref.shape[0]
    ga = group_pass(0, u_read, users, split(at), prep, update_users(u_read, um_read, u1_ref, um1_ref))
    at1, amt1 = adagrad(at, amt, ga)
    u_read = reader(u1_ref)
    ga = group_pass(1, u_read, users, split(at1), prep, update_users(u_read, reader(um1_ref), uo_ref, umo_ref))
    return adagrad(at1, amt1, ga)


def early_kernel(u_ref, um_ref, near_ref, mh, cu, cn, ads_ref, users_ref, u1_ref, um1_ref):
    ads_ref[0], ads_ref[1] = meeting(
        reader(u_ref), reader(um_ref), near_ref[0], near_ref[1], (mh, cu, cn),
        u1_ref, um1_ref, users_ref.at[0], users_ref.at[1],
    )


def late_kernel(
    u_ref, um_ref, far_ref, mh, cu, cn, after_ref, lists_ref,
    u1_ref, um1_ref, ato_ref, amto_ref, gh_ref, gl_ref, ah_ref, al_ref,
):
    prep = (mh, cu, cn)
    at = far_ref[0]
    u_read = reader(u_ref)
    put = update_users(u_read, reader(um_ref), u1_ref, um1_ref)
    ga = group_pass(0, u_read, u_ref.shape[0], split(at), prep, put)
    at1, amt1 = adagrad(at, far_ref[1], ga)
    ato_ref[...], amto_ref[...] = second_group(u1_ref, at1, amt1, prep, gh_ref, gl_ref, ah_ref, al_ref)


def pick_kernel(
    ue_ref, ume_ref, users_ref, ads_ref, ato_ref, amto_ref, mh, cu, cn,
    un_ref, umn_ref, atn_ref, amtn_ref, u1_ref, um1_ref,
):
    odd = on_odd_core()
    at = jnp.where(odd, ato_ref[...], ads_ref[0])
    amt = jnp.where(odd, amto_ref[...], ads_ref[1])
    u_read, um_read = picker(odd, ue_ref, users_ref.at[0]), picker(odd, ume_ref, users_ref.at[1])
    atn_ref[...], amtn_ref[...] = meeting(
        u_read, um_read, at, amt, (mh, cu, cn), u1_ref, um1_ref, un_ref, umn_ref
    )


def gradient_kernel(u_ref, at_ref, mh, cu, cn, gu_ref, ga_ref):
    def put(rows, grad):
        gu_ref[rows, :] = grad

    ga_ref[...] = group_pass(0, reader(u_ref), u_ref.shape[0], split(at_ref[...]), (mh, cu, cn), put)


def last_end_kernel(
    u_ref, um_ref, at_ref, amt_ref, gu_ref, ga_ref, mh, cu, cn, ads_ref, users_ref, u1_ref, um1_ref,
):
    u1_ref[...], um1_ref[...] = adagrad(u_ref[...], um_ref[...], gu_ref[...])
    at1, amt1 = adagrad(at_ref[...], amt_ref[...], ga_ref[...])
    put = update_users(reader(u1_ref), reader(um1_ref), users_ref.at[0], users_ref.at[1])
    ga = group_pass(1, reader(u1_ref), u1_ref.shape[0], split(at1), (mh, cu, cn), put)
    ads_ref[0], ads_ref[1] = adagrad(at1, amt1, ga)


def users_kernel(u_ref, um_ref, gh_ref, gl_ref, ah_ref, al_ref, uo_ref, umo_ref):
    put = update_users(reader(u_ref), reader(um_ref), uo_ref, umo_ref)
    at_hl = ah_ref[...], al_ref[...]
    for r in range(0, u_ref.shape[0], BLOCK):
        rows = pl.ds(r, BLOCK)
        put(rows, dot3((gh_ref[rows, :], gl_ref[rows, :]), at_hl, 1, 1))


def prepare_kernel(rnd, pack, after_ref, pu, pa, ng, mh, cu, cn, lists_ref):
    prepare_round(rnd, pu, pa, ng, mh.shape[1], mh.shape[2], (mh, cu, cn))
    pack_lists(pack, pu, pa, ng, lists_ref)


def prepare_both_kernel(
    rnd, after_ref, lists_ref, pu_hbm, pa_hbm, ng_hbm, mh, cu, cn, mh2, cu2, cn2, pu, pa, ng, sems,
):
    copies = fetch_indices(pu_hbm, pa_hbm, ng_hbm, pu, pa, ng, sems, away=True)
    groups, users, ads = mh.shape
    n = ng_hbm.shape[-1]
    size = pu_hbm.shape[-1] // groups
    for g in range(groups):
        cols = pl.ds(g * size, size)
        negs = lists_ref[2 + g : 3 + g, pl.ds(0, n)]
        prepare(g, lists_ref[0:1, cols], lists_ref[1:2, cols], negs, users, ads, mh2, cu2, cn2)
    for c in copies:
        c.wait()
    prepare_round(rnd, pu, pa, ng, users, ads, (mh, cu, cn))


def call(kernel, ins, outs, scratch=(), hbm=0, name=None, out_place=pltpu.VMEM):
    vmem = pl.BlockSpec(memory_space=pltpu.VMEM)
    split_at = len(ins) - hbm
    far = [pltpu.with_memory_space_constraint(x, pltpu.HBM) for x in ins[split_at:]]
    return pl.pallas_call(
        kernel,
        out_shape=outs,
        in_specs=[vmem] * split_at + [pl.BlockSpec(memory_space=pltpu.HBM)] * hbm,
        out_specs=[pl.BlockSpec(memory_space=out_place)] * len(outs),
        scratch_shapes=list(scratch),
        compiler_params=pltpu.CompilerParams(vmem_limit_bytes=VMEM_LIMIT),
        cost_estimate=pl.CostEstimate(flops=1, bytes_accessed=1, transcendentals=0),
        name=name,
    )(*ins[:split_at], *far)


def users_out_kernel(users_ref, after_hbm, u_hbm, um_hbm, sems):
    size = users_ref.shape[1] // PARTS_OUT
    copies = []
    for t, out_hbm in enumerate((u_hbm, um_hbm)):
        for k in range(PARTS_OUT):
            rows = pl.ds(k * size, size)
            copies.append(pltpu.make_async_copy(users_ref.at[t, rows, :], out_hbm.at[rows, :], sems.at[t * PARTS_OUT + k]))
    for c in copies:
        c.start()
    for c in copies:
        c.wait()


def ads_out_kernel(ads_ref, a_hbm, am_hbm, turned, sems):
    size = turned.shape[1] // PARTS_OUT
    copies = []
    for t, out_hbm in enumerate((a_hbm, am_hbm)):
        for k in range(PARTS_OUT):
            rows = pl.ds(k * size, size)
            turned[t, rows, :] = ads_ref[t, :, rows].T
            copies.append(pltpu.make_async_copy(turned.at[t, rows, :], out_hbm.at[rows, :], sems.at[t * PARTS_OUT + k]))
            copies[-1].start()
    for c in copies:
        c.wait()


def move(arrays, *kinds):
    blocks, cycles = lax.axis_size("blk"), lax.axis_size("pair")
    route = []
    for b in range(blocks):
        for p in range(cycles):
            steps, flip = kinds[b % len(kinds)]
            to = (b + steps) % blocks, p ^ (cycles // 2 if flip else 0)
            route.append((b * cycles + p, to[0] * cycles + to[1]))
    return tuple(lax.ppermute(x, AXES, route) for x in arrays)


def local(users, user_moms, ads, ad_moments, pos_user, pos_ad, neg_ad):
    nu, d = users.shape
    na = ads.shape[0]
    rounds, groups, n = neg_ad.shape[2:]
    edges = pos_user.shape[3]
    indices = (pos_user, pos_ad, neg_ad)

    def shape(*dims, dtype=F32):
        return jax.ShapeDtypeStruct(dims, dtype)

    table_u, table_a = shape(nu, d), shape(d, na)
    parts = [shape(nu, na, dtype=BF16)] * 2 + [shape(d, na, dtype=BF16)] * 2
    index_scratch = [
        pltpu.VMEM((rounds, edges), jnp.int32),
        pltpu.VMEM((rounds, edges), jnp.int32),
        pltpu.VMEM((rounds, groups, n), jnp.int32),
    ]
    sems = pltpu.SemaphoreType.DMA((3,))
    prep_shapes = [shape(groups, nu, na, dtype=BF16), shape(groups, nu, 128), shape(groups, 8, na)]
    prep_scratch = [pltpu.VMEM(s.shape, s.dtype) for s in prep_shapes]

    def update(u, um, g):
        return call(users_kernel, (u, um, *g), [table_u, table_u], name="users_update")

    stay, away = (0, False), (0, True)
    both_u, both_a = shape(2, nu, d), shape(2, d, na)
    users_scratch = [pltpu.VMEM((nu, d), F32)] * 2
    own_lists = [shape(rounds, edges, dtype=jnp.int32)] * 2 + [shape(rounds, groups, n, dtype=jnp.int32)]
    u, um, ads_now, *rest = call(
        first_round_kernel,
        (*indices, users, ads, user_moms, ad_moments),
        [table_u, table_u, both_a, *parts, *own_lists],
        [*prep_scratch, *users_scratch, *[pltpu.VMEM((na, d), F32)] * 2, sems, pltpu.SemaphoreType.DMA((4,))],
        hbm=7, name="round_first",
    )
    g, own_lists = rest[: len(parts)], rest[len(parts) :]
    (near,) = move((ads_now,), (1, False), (-1, False))
    (far,) = move((ads_now,), (1, False), (1, False))
    u, um = update(u, um, g)
    *prep, lists = call(
        functools.partial(prepare_kernel, 1, rounds - 1), (um, *own_lists),
        prep_shapes + [shape(8, max(edges, n), dtype=jnp.int32)], name="counts_1",
    )
    (lists,) = move((lists,), (-4, False), stay, stay, stay)

    ads_early, after = call(early_kernel, (u, um, near, *prep), [both_a, both_u], users_scratch, name="round_early")
    (ads_early,) = move((ads_early,), (1, False), (1, True))
    (users_early,) = move((after,), stay, away)

    u, um, at, amt, *g = call(
        late_kernel, (u, um, far, *prep, after, lists), [table_u, table_u, table_a, table_a, *parts], name="round_late",
    )
    ads_late = move((at, amt), (1, False), (-1, False))
    u, um = update(u, um, g)
    preps = call(
        functools.partial(prepare_both_kernel, 2), (um, lists, *indices), prep_shapes * 2, [*index_scratch, sems], hbm=3,
        name="counts_23",
    )
    prep, prep_last = preps[: len(prep_shapes)], preps[len(prep_shapes) :]

    u, um, at, amt = call(
        pick_kernel, (u, um, users_early, ads_early, *ads_late, *prep), [table_u, table_u, table_a, table_a],
        users_scratch, name="round_pick",
    )
    u, um = move((u, um), (-4, False), away, stay, away)
    at, amt = move((at, amt), (1, False), (1, True), (1, False), (-3, True))
    gu, ga = call(gradient_kernel, (u, at, *prep_last), [table_u, table_a], name="round_last_gradients")
    ads_now, users_now = call(
        last_end_kernel, (u, um, at, amt, gu, ga, *prep_last), [both_a, both_u], users_scratch, name="round_last_end",
    )
    (ads_now,) = move((ads_now,), (1, True), (-3, True), (-3, True), (-3, True))
    (users_now,) = move((users_now,), (4, False), stay, stay, stay)
    out_sems = pltpu.SemaphoreType.DMA((2 * PARTS_OUT,))
    a, am = call(
        ads_out_kernel, (ads_now,), [pltpu.HBM((na, d), F32)] * 2, [pltpu.VMEM((2, na, d), F32), out_sems],
        name="ads_out", out_place=pltpu.HBM,
    )
    u, um = call(
        users_out_kernel, (users_now, am), [pltpu.HBM((nu, d), F32)] * 2, [out_sems], hbm=1, name="users_out", out_place=pltpu.HBM,
    )
    return u, um, a, am


def solution(mesh):
    rows = P(AXES, None)
    return jax.shard_map(
        local,
        mesh=mesh,
        in_specs=(rows, rows, rows, rows, P("blk", None, None, None), P("blk", None, None, None), P("blk", None, None, None, None)),
        out_specs=(rows, rows, rows, rows),
        check_vma=False,
    )
```

```python
import functools

import jax
import jax.numpy as jnp
from jax import lax
from jax.experimental import pallas as pl
from jax.experimental.pallas import tpu as pltpu
from jax.sharding import PartitionSpec as P

LEARN_RATE = 0.1
EPS = 1e-08
F32 = jnp.float32
BF16 = jnp.bfloat16
LANES = 128
PARTS_OUT = 4
AXES = ("blk", "pair")
VMEM_LIMIT = 28 * 1024 * 1024


def dot(a, b, ca, cb):
    return lax.dot_general(a, b, (((ca,), (cb,)), ((), ())), preferred_element_type=F32)


def split(x):
    hi = x.astype(BF16)
    return hi, (x - hi.astype(F32)).astype(BF16)


def dot3(a, b, ca, cb):
    (ah, al), (bh, bl) = a, b
    return dot(jnp.concatenate([ah, al, ah], axis=ca), jnp.concatenate([bh, bh, bl], axis=cb), ca, cb)


def adagrad(row, mom, grad):
    mom = mom + grad * grad
    return row - LEARN_RATE * grad / (jnp.sqrt(mom) + EPS), mom


def onehot(idx, count):
    rows = lax.broadcasted_iota(jnp.int32, (count, idx.shape[1]), 0)
    return jnp.where(rows == idx, F32(1), F32(0)).astype(BF16)


def prepare(group, pu, pa, ng, users, ads, mh_ref, cu_ref, cn_ref):
    n = ng.shape[1]
    hot_u = onehot(pu, users)
    hot_a = onehot(pa, ads)
    mh_ref[group] = (0.5 * dot(hot_u, hot_a, 1, 1)).astype(BF16)
    ones = jnp.ones((pu.shape[1], 128), BF16)
    cu_ref[group] = dot(hot_u, ones, 1, 0) * F32(0.5 / n**0.5)
    hi = lax.shift_right_logical(ng, LANES.bit_length() - 1)
    counts = dot(onehot(hi, 8), onehot(ng - hi * LANES, LANES), 1, 1)
    for k in range(ads // LANES):
        cols = pl.ds(k * LANES, LANES)
        cn_ref[group, :, cols] = jnp.broadcast_to(counts[k : k + 1, :], (8, LANES))


def gradient_matrix(s, mh, cu, cn):
    t = jnp.tanh(0.5 * s)
    w = jnp.concatenate([cu] * (s.shape[1] // 128), axis=1) * cn
    m = mh.astype(F32)
    return split((w + m) * t + (w - m))


BLOCK = 256


def group_pass(group, u_read, users, at_hl, prep, gu_out, g_out=None):
    mh_ref, cu_ref, cn_ref = prep
    cn = cn_ref[group, 0:1, :]
    blocks = [pl.ds(r, BLOCK) for r in range(0, users, BLOCK)]
    u_hl = [split(u_read(rows)) for rows in blocks]
    scores = [dot3(u, at_hl, 1, 0) for u in u_hl]
    ga = None
    for rows, u, s in zip(blocks, u_hl, scores):
        g_hl = gradient_matrix(s, mh_ref[group, rows, :], cu_ref[group, rows, :], cn)
        if g_out is None:
            gu_out(rows, dot3(g_hl, at_hl, 1, 1))
        else:
            g_out[0][rows, :], g_out[1][rows, :] = g_hl
        part = dot3(u, g_hl, 0, 0)
        ga = part if ga is None else ga + part
    return ga


def reader(ref):
    return lambda rows: ref[rows, :]


def picker(odd, even_ref, odd_ref):
    return lambda rows: jnp.where(odd, odd_ref[rows, :], even_ref[rows, :])


def update_users(u_read, um_read, uo_ref, umo_ref):
    def put(rows, grad):
        uo_ref[rows, :], umo_ref[rows, :] = adagrad(u_read(rows), um_read(rows), grad)

    return put


def on_odd_core():
    return lax.rem(lax.axis_index("blk"), 2) == 1


def fetch_indices(pu_hbm, pa_hbm, ng_hbm, pu, pa, ng, sems, away=False):
    cycle = lax.axis_index("pair")
    if away:
        count = lax.axis_size("pair")
        cycle = lax.rem(cycle + jnp.where(on_odd_core(), count // 2, 0), count)
    copies = [
        pltpu.make_async_copy(src.at[0, cycle], dst, sems.at[k])
        for k, (src, dst) in enumerate(((pu_hbm, pu), (pa_hbm, pa), (ng_hbm, ng)))
    ]
    for c in copies:
        c.start()
    return copies


def pack_lists(rnd, pu, pa, ng, lists_ref):
    lists_ref[...] = jnp.zeros_like(lists_ref)
    lists_ref[0:1, pl.ds(0, pu.shape[1])] = pu[rnd : rnd + 1, :]
    lists_ref[1:2, pl.ds(0, pa.shape[1])] = pa[rnd : rnd + 1, :]
    lists_ref[pl.ds(2, ng.shape[1]), pl.ds(0, ng.shape[2])] = ng[rnd]


def prepare_round(rnd, pu, pa, ng, users, ads, prep):
    groups = ng.shape[1]
    edges = pu.shape[1] // groups
    for g in range(groups):
        cols = pl.ds(g * edges, edges)
        prepare(g, pu[rnd : rnd + 1, cols], pa[rnd : rnd + 1, cols], ng[rnd, g : g + 1, :], users, ads, *prep)


def second_group(u_ref, at1, amt1, prep, gh_ref, gl_ref, ah_ref, al_ref):
    at_hl = split(at1)
    ah_ref[...], al_ref[...] = at_hl
    ga = group_pass(1, reader(u_ref), u_ref.shape[0], at_hl, prep, None, (gh_ref, gl_ref))
    return adagrad(at1, amt1, ga)


def first_round_kernel(
    pu_hbm, pa_hbm, ng_hbm, u_hbm, a_hbm, um_hbm, am_hbm,
    uo_ref, umo_ref, ads_ref, gh_ref, gl_ref, ah_ref, al_ref, pu, pa, ng,
    mh, cu, cn, u_ref, um_ref, a_ref, am_ref, sems, table_sems,
):
    copies = fetch_indices(pu_hbm, pa_hbm, ng_hbm, pu, pa, ng, sems)
    tables = [
        pltpu.make_async_copy(src, dst, table_sems.at[k])
        for k, (src, dst) in enumerate(
            ((u_hbm, u_ref), (a_hbm, a_ref), (um_hbm, um_ref), (am_hbm, am_ref))
        )
    ]
    for c in tables:
        c.start()
    for c in copies:
        c.wait()
    prep = (mh, cu, cn)
    prepare_round(0, pu, pa, ng, u_ref.shape[0], a_ref.shape[0], prep)
    for c in tables:
        c.wait()
    at = a_ref[...].T
    amt = am_ref[...].T
    put = update_users(reader(u_ref), reader(um_ref), uo_ref, umo_ref)
    ga = group_pass(0, reader(u_ref), u_ref.shape[0], split(at), prep, put)
    at1, amt1 = adagrad(at, amt, ga)
    ads_ref[0], ads_ref[1] = second_group(uo_ref, at1, amt1, prep, gh_ref, gl_ref, ah_ref, al_ref)


def meeting(u_read, um_read, at, amt, prep, u1_ref, um1_ref, uo_ref, umo_ref):
    users = u1_ref.shape[0]
    ga = group_pass(0, u_read, users, split(at), prep, update_users(u_read, um_read, u1_ref, um1_ref))
    at1, amt1 = adagrad(at, amt, ga)
    u_read = reader(u1_ref)
    ga = group_pass(1, u_read, users, split(at1), prep, update_users(u_read, reader(um1_ref), uo_ref, umo_ref))
    return adagrad(at1, amt1, ga)


def early_kernel(u_ref, um_ref, near_ref, mh, cu, cn, ads_ref, users_ref, u1_ref, um1_ref):
    ads_ref[0], ads_ref[1] = meeting(
        reader(u_ref), reader(um_ref), near_ref[0], near_ref[1], (mh, cu, cn),
        u1_ref, um1_ref, users_ref.at[0], users_ref.at[1],
    )


def late_kernel(
    u_ref, um_ref, far_ref, mh, cu, cn, after_ref, lists_ref,
    u1_ref, um1_ref, ato_ref, amto_ref, gh_ref, gl_ref, ah_ref, al_ref,
):
    prep = (mh, cu, cn)
    at = far_ref[0]
    u_read = reader(u_ref)
    put = update_users(u_read, reader(um_ref), u1_ref, um1_ref)
    ga = group_pass(0, u_read, u_ref.shape[0], split(at), prep, put)
    at1, amt1 = adagrad(at, far_ref[1], ga)
    ato_ref[...], amto_ref[...] = second_group(u1_ref, at1, amt1, prep, gh_ref, gl_ref, ah_ref, al_ref)


def pick_kernel(
    ue_ref, ume_ref, users_ref, ads_ref, ato_ref, amto_ref, mh, cu, cn,
    un_ref, umn_ref, atn_ref, amtn_ref, u1_ref, um1_ref,
):
    odd = on_odd_core()
    at = jnp.where(odd, ato_ref[...], ads_ref[0])
    amt = jnp.where(odd, amto_ref[...], ads_ref[1])
    u_read, um_read = picker(odd, ue_ref, users_ref.at[0]), picker(odd, ume_ref, users_ref.at[1])
    atn_ref[...], amtn_ref[...] = meeting(
        u_read, um_read, at, amt, (mh, cu, cn), u1_ref, um1_ref, un_ref, umn_ref
    )


def gradient_kernel(u_ref, at_ref, mh, cu, cn, gu_ref, ga_ref):
    def put(rows, grad):
        gu_ref[rows, :] = grad

    ga_ref[...] = group_pass(0, reader(u_ref), u_ref.shape[0], split(at_ref[...]), (mh, cu, cn), put)


def last_end_kernel(
    u_ref, at_ref, amt_ref, um_ref, gu_ref, ga_ref, mh, cu, cn, ads_ref, users_ref, u1_ref, um1_ref,
):
    u1_ref[...], um1_ref[...] = adagrad(u_ref[...], um_ref[...], gu_ref[...])
    at1, amt1 = adagrad(at_ref[...], amt_ref[...], ga_ref[...])
    put = update_users(reader(u1_ref), reader(um1_ref), users_ref.at[0], users_ref.at[1])
    ga = group_pass(1, reader(u1_ref), u1_ref.shape[0], split(at1), (mh, cu, cn), put)
    ads_ref[0], ads_ref[1] = adagrad(at1, amt1, ga)


def users_kernel(u_ref, um_ref, gh_ref, gl_ref, ah_ref, al_ref, uo_ref, umo_ref):
    put = update_users(reader(u_ref), reader(um_ref), uo_ref, umo_ref)
    at_hl = ah_ref[...], al_ref[...]
    for r in range(0, u_ref.shape[0], BLOCK):
        rows = pl.ds(r, BLOCK)
        put(rows, dot3((gh_ref[rows, :], gl_ref[rows, :]), at_hl, 1, 1))


def prepare_kernel(rnd, pack, after_ref, pu, pa, ng, mh, cu, cn, lists_ref):
    prepare_round(rnd, pu, pa, ng, mh.shape[1], mh.shape[2], (mh, cu, cn))
    pack_lists(pack, pu, pa, ng, lists_ref)


def prepare_both_kernel(
    rnd, after_ref, lists_ref, pu_hbm, pa_hbm, ng_hbm, mh, cu, cn, mh2, cu2, cn2, pu, pa, ng, sems,
):
    copies = fetch_indices(pu_hbm, pa_hbm, ng_hbm, pu, pa, ng, sems, away=True)
    groups, users, ads = mh.shape
    n = ng_hbm.shape[-1]
    size = pu_hbm.shape[-1] // groups
    for g in range(groups):
        cols = pl.ds(g * size, size)
        negs = lists_ref[2 + g : 3 + g, pl.ds(0, n)]
        prepare(g, lists_ref[0:1, cols], lists_ref[1:2, cols], negs, users, ads, mh2, cu2, cn2)
    for c in copies:
        c.wait()
    prepare_round(rnd, pu, pa, ng, users, ads, (mh, cu, cn))


def call(kernel, ins, outs, scratch=(), hbm=0, name=None, out_place=pltpu.VMEM):
    vmem = pl.BlockSpec(memory_space=pltpu.VMEM)
    split_at = len(ins) - hbm
    far = [pltpu.with_memory_space_constraint(x, pltpu.HBM) for x in ins[split_at:]]
    return pl.pallas_call(
        kernel,
        out_shape=outs,
        in_specs=[vmem] * split_at + [pl.BlockSpec(memory_space=pltpu.HBM)] * hbm,
        out_specs=[pl.BlockSpec(memory_space=out_place)] * len(outs),
        scratch_shapes=list(scratch),
        compiler_params=pltpu.CompilerParams(vmem_limit_bytes=VMEM_LIMIT),
        cost_estimate=pl.CostEstimate(flops=1, bytes_accessed=1, transcendentals=0),
        name=name,
    )(*ins[:split_at], *far)


def users_out_kernel(users_ref, after_hbm, u_hbm, um_hbm, sems):
    size = users_ref.shape[1] // PARTS_OUT
    copies = []
    for t, out_hbm in enumerate((u_hbm, um_hbm)):
        for k in range(PARTS_OUT):
            rows = pl.ds(k * size, size)
            copies.append(pltpu.make_async_copy(users_ref.at[t, rows, :], out_hbm.at[rows, :], sems.at[t * PARTS_OUT + k]))
    for c in copies:
        c.start()
    for c in copies:
        c.wait()


def ads_out_kernel(ads_ref, a_hbm, am_hbm, turned, sems):
    size = turned.shape[1] // PARTS_OUT
    copies = []
    for t, out_hbm in enumerate((a_hbm, am_hbm)):
        for k in range(PARTS_OUT):
            rows = pl.ds(k * size, size)
            turned[t, rows, :] = ads_ref[t, :, rows].T
            copies.append(pltpu.make_async_copy(turned.at[t, rows, :], out_hbm.at[rows, :], sems.at[t * PARTS_OUT + k]))
            copies[-1].start()
    for c in copies:
        c.wait()


def move(arrays, *kinds):
    blocks, cycles = lax.axis_size("blk"), lax.axis_size("pair")
    route = []
    for b in range(blocks):
        for p in range(cycles):
            steps, flip = kinds[b % len(kinds)]
            to = (b + steps) % blocks, p ^ (cycles // 2 if flip else 0)
            route.append((b * cycles + p, to[0] * cycles + to[1]))
    return tuple(lax.ppermute(x, AXES, route) for x in arrays)


def local(users, user_moms, ads, ad_moments, pos_user, pos_ad, neg_ad):
    nu, d = users.shape
    na = ads.shape[0]
    rounds, groups, n = neg_ad.shape[2:]
    edges = pos_user.shape[3]
    indices = (pos_user, pos_ad, neg_ad)

    def shape(*dims, dtype=F32):
        return jax.ShapeDtypeStruct(dims, dtype)

    table_u, table_a = shape(nu, d), shape(d, na)
    parts = [shape(nu, na, dtype=BF16)] * 2 + [shape(d, na, dtype=BF16)] * 2
    index_scratch = [
        pltpu.VMEM((rounds, edges), jnp.int32),
        pltpu.VMEM((rounds, edges), jnp.int32),
        pltpu.VMEM((rounds, groups, n), jnp.int32),
    ]
    sems = pltpu.SemaphoreType.DMA((3,))
    prep_shapes = [shape(groups, nu, na, dtype=BF16), shape(groups, nu, 128), shape(groups, 8, na)]
    prep_scratch = [pltpu.VMEM(s.shape, s.dtype) for s in prep_shapes]

    def update(u, um, g):
        return call(users_kernel, (u, um, *g), [table_u, table_u], name="users_update")

    stay, away = (0, False), (0, True)
    both_u, both_a = shape(2, nu, d), shape(2, d, na)
    users_scratch = [pltpu.VMEM((nu, d), F32)] * 2
    own_lists = [shape(rounds, edges, dtype=jnp.int32)] * 2 + [shape(rounds, groups, n, dtype=jnp.int32)]
    u, um, ads_now, *rest = call(
        first_round_kernel,
        (*indices, users, ads, user_moms, ad_moments),
        [table_u, table_u, both_a, *parts, *own_lists],
        [*prep_scratch, *users_scratch, *[pltpu.VMEM((na, d), F32)] * 2, sems, pltpu.SemaphoreType.DMA((4,))],
        hbm=7, name="round_first",
    )
    g, own_lists = rest[: len(parts)], rest[len(parts) :]
    (near,) = move((ads_now,), (1, False), (-1, False))
    (far,) = move((ads_now,), (1, False), (1, False))
    u, um = update(u, um, g)
    *prep, lists = call(
        functools.partial(prepare_kernel, 1, rounds - 1), (um, *own_lists),
        prep_shapes + [shape(8, max(edges, n), dtype=jnp.int32)], name="counts_1",
    )
    (lists,) = move((lists,), (-4, False), stay, stay, stay)

    ads_early, after = call(early_kernel, (u, um, near, *prep), [both_a, both_u], users_scratch, name="round_early")
    (ads_early,) = move((ads_early,), (1, False), (1, True))
    (users_early,) = move((after,), stay, away)

    u, um, at, amt, *g = call(
        late_kernel, (u, um, far, *prep, after, lists), [table_u, table_u, table_a, table_a, *parts], name="round_late",
    )
    ads_late = move((at, amt), (1, False), (-1, False))
    u, um = update(u, um, g)
    preps = call(
        functools.partial(prepare_both_kernel, 2), (um, lists, *indices), prep_shapes * 2, [*index_scratch, sems], hbm=3,
        name="counts_23",
    )
    prep, prep_last = preps[: len(prep_shapes)], preps[len(prep_shapes) :]

    u, um, at, amt = call(
        pick_kernel, (u, um, users_early, ads_early, *ads_late, *prep), [table_u, table_u, table_a, table_a],
        users_scratch, name="round_pick",
    )
    u, um = move((u, um), (-4, False), away, stay, away)
    at, amt = move((at, amt), (1, False), (1, True), (1, False), (-3, True))
    gu, ga = call(gradient_kernel, (u, at, *prep_last), [table_u, table_a], name="round_last_gradients")
    ads_now, users_now = call(
        last_end_kernel, (u, at, amt, um, gu, ga, *prep_last), [both_a, both_u], users_scratch, name="round_last_end",
    )
    (ads_now,) = move((ads_now,), (1, True), (-3, True), (-3, True), (-3, True))
    (users_now,) = move((users_now,), (4, False), stay, stay, stay)
    out_sems = pltpu.SemaphoreType.DMA((2 * PARTS_OUT,))
    a, am = call(
        ads_out_kernel, (ads_now,), [pltpu.HBM((na, d), F32)] * 2, [pltpu.VMEM((2, na, d), F32), out_sems],
        name="ads_out", out_place=pltpu.HBM,
    )
    u, um = call(
        users_out_kernel, (users_now, am), [pltpu.HBM((nu, d), F32)] * 2, [out_sems], hbm=1, name="users_out", out_place=pltpu.HBM,
    )
    return u, um, a, am


def solution(mesh):
    rows = P(AXES, None)
    return jax.shard_map(
        local,
        mesh=mesh,
        in_specs=(rows, rows, rows, rows, P("blk", None, None, None), P("blk", None, None, None), P("blk", None, None, None, None)),
        out_specs=(rows, rows, rows, rows),
        check_vma=False,
    )
```

```python
import functools

import jax
import jax.numpy as jnp
from jax import lax
from jax.experimental import pallas as pl
from jax.experimental.pallas import tpu as pltpu
from jax.sharding import PartitionSpec as P

LEARN_RATE = 0.1
EPS = 1e-08
F32 = jnp.float32
BF16 = jnp.bfloat16
LANES = 128
PARTS_OUT = 4
AXES = ("blk", "pair")
VMEM_LIMIT = 28 * 1024 * 1024


def dot(a, b, ca, cb):
    return lax.dot_general(a, b, (((ca,), (cb,)), ((), ())), preferred_element_type=F32)


def split(x):
    hi = x.astype(BF16)
    return hi, (x - hi.astype(F32)).astype(BF16)


def dot3(a, b, ca, cb):
    (ah, al), (bh, bl) = a, b
    return dot(jnp.concatenate([ah, al, ah], axis=ca), jnp.concatenate([bh, bh, bl], axis=cb), ca, cb)


def adagrad(row, mom, grad):
    mom = mom + grad * grad
    return row - LEARN_RATE * grad / (jnp.sqrt(mom) + EPS), mom


def onehot(idx, count):
    rows = lax.broadcasted_iota(jnp.int32, (count, idx.shape[1]), 0)
    return jnp.where(rows == idx, F32(1), F32(0)).astype(BF16)


def prepare(group, pu, pa, ng, users, ads, mh_ref, cu_ref, cn_ref):
    n = ng.shape[1]
    hot_u = onehot(pu, users)
    hot_a = onehot(pa, ads)
    mh_ref[group] = (0.5 * dot(hot_u, hot_a, 1, 1)).astype(BF16)
    ones = jnp.ones((pu.shape[1], 128), BF16)
    cu_ref[group] = dot(hot_u, ones, 1, 0) * F32(0.5 / n**0.5)
    hi = lax.shift_right_logical(ng, LANES.bit_length() - 1)
    counts = dot(onehot(hi, 8), onehot(ng - hi * LANES, LANES), 1, 1)
    for k in range(ads // LANES):
        cols = pl.ds(k * LANES, LANES)
        cn_ref[group, :, cols] = jnp.broadcast_to(counts[k : k + 1, :], (8, LANES))


def gradient_matrix(s, mh, cu, cn):
    t = jnp.tanh(0.5 * s)
    w = jnp.concatenate([cu] * (s.shape[1] // 128), axis=1) * cn
    m = mh.astype(F32)
    return split((w + m) * t + (w - m))


BLOCK = 256


def group_pass(group, u_read, users, at_hl, prep, gu_out, g_out=None):
    mh_ref, cu_ref, cn_ref = prep
    cn = cn_ref[group, 0:1, :]
    blocks = [pl.ds(r, BLOCK) for r in range(0, users, BLOCK)]
    u_hl = [split(u_read(rows)) for rows in blocks]
    scores = [dot3(u, at_hl, 1, 0) for u in u_hl]
    ga = None
    for rows, u, s in zip(blocks, u_hl, scores):
        g_hl = gradient_matrix(s, mh_ref[group, rows, :], cu_ref[group, rows, :], cn)
        if g_out is None:
            gu_out(rows, dot3(g_hl, at_hl, 1, 1))
        else:
            g_out[0][rows, :], g_out[1][rows, :] = g_hl
        part = dot3(u, g_hl, 0, 0)
        ga = part if ga is None else ga + part
    return ga


def reader(ref):
    return lambda rows: ref[rows, :]


def picker(odd, even_ref, odd_ref):
    return lambda rows: jnp.where(odd, odd_ref[rows, :], even_ref[rows, :])


def update_users(u_read, um_read, uo_ref, umo_ref):
    def put(rows, grad):
        uo_ref[rows, :], umo_ref[rows, :] = adagrad(u_read(rows), um_read(rows), grad)

    return put


def on_odd_core():
    return lax.rem(lax.axis_index("blk"), 2) == 1


def fetch_indices(pu_hbm, pa_hbm, ng_hbm, pu, pa, ng, sems, away=False):
    cycle = lax.axis_index("pair")
    if away:
        count = lax.axis_size("pair")
        cycle = lax.rem(cycle + jnp.where(on_odd_core(), count // 2, 0), count)
    copies = [
        pltpu.make_async_copy(src.at[0, cycle], dst, sems.at[k])
        for k, (src, dst) in enumerate(((pu_hbm, pu), (pa_hbm, pa), (ng_hbm, ng)))
    ]
    for c in copies:
        c.start()
    return copies


def pack_lists(rnd, pu, pa, ng, lists_ref):
    lists_ref[...] = jnp.zeros_like(lists_ref)
    lists_ref[0:1, pl.ds(0, pu.shape[1])] = pu[rnd : rnd + 1, :]
    lists_ref[1:2, pl.ds(0, pa.shape[1])] = pa[rnd : rnd + 1, :]
    lists_ref[pl.ds(2, ng.shape[1]), pl.ds(0, ng.shape[2])] = ng[rnd]


def prepare_round(rnd, pu, pa, ng, users, ads, prep):
    groups = ng.shape[1]
    edges = pu.shape[1] // groups
    for g in range(groups):
        cols = pl.ds(g * edges, edges)
        prepare(g, pu[rnd : rnd + 1, cols], pa[rnd : rnd + 1, cols], ng[rnd, g : g + 1, :], users, ads, *prep)


def second_group(u_ref, at1, amt1, prep, gh_ref, gl_ref, ah_ref, al_ref):
    at_hl = split(at1)
    ah_ref[...], al_ref[...] = at_hl
    ga = group_pass(1, reader(u_ref), u_ref.shape[0], at_hl, prep, None, (gh_ref, gl_ref))
    return adagrad(at1, amt1, ga)


def first_round_kernel(
    pu_hbm, pa_hbm, ng_hbm, u_hbm, a_hbm, um_hbm, am_hbm,
    uo_ref, umo_ref, ads_ref, gh_ref, gl_ref, ah_ref, al_ref, pu, pa, ng,
    mh, cu, cn, u_ref, um_ref, a_ref, am_ref, sems, table_sems,
):
    copies = fetch_indices(pu_hbm, pa_hbm, ng_hbm, pu, pa, ng, sems)
    tables = [
        pltpu.make_async_copy(src, dst, table_sems.at[k])
        for k, (src, dst) in enumerate(
            ((u_hbm, u_ref), (a_hbm, a_ref), (um_hbm, um_ref), (am_hbm, am_ref))
        )
    ]
    for c in tables:
        c.start()
    for c in copies:
        c.wait()
    prep = (mh, cu, cn)
    prepare_round(0, pu, pa, ng, u_ref.shape[0], a_ref.shape[0], prep)
    for c in tables:
        c.wait()
    at = a_ref[...].T
    amt = am_ref[...].T
    put = update_users(reader(u_ref), reader(um_ref), uo_ref, umo_ref)
    ga = group_pass(0, reader(u_ref), u_ref.shape[0], split(at), prep, put)
    at1, amt1 = adagrad(at, amt, ga)
    ads_ref[0], ads_ref[1] = second_group(uo_ref, at1, amt1, prep, gh_ref, gl_ref, ah_ref, al_ref)


def meeting(u_read, um_read, at, amt, prep, u1_ref, um1_ref, uo_ref, umo_ref):
    users = u1_ref.shape[0]
    ga = group_pass(0, u_read, users, split(at), prep, update_users(u_read, um_read, u1_ref, um1_ref))
    at1, amt1 = adagrad(at, amt, ga)
    u_read = reader(u1_ref)
    ga = group_pass(1, u_read, users, split(at1), prep, update_users(u_read, reader(um1_ref), uo_ref, umo_ref))
    return adagrad(at1, amt1, ga)


def early_kernel(u_ref, um_ref, near_ref, mh, cu, cn, ads_ref, users_ref, u1_ref, um1_ref):
    ads_ref[0], ads_ref[1] = meeting(
        reader(u_ref), reader(um_ref), near_ref[0], near_ref[1], (mh, cu, cn),
        u1_ref, um1_ref, users_ref.at[0], users_ref.at[1],
    )


def late_kernel(
    u_ref, um_ref, far_ref, mh, cu, cn, after_ref, lists_ref,
    u1_ref, um1_ref, ato_ref, amto_ref, gh_ref, gl_ref, ah_ref, al_ref,
):
    prep = (mh, cu, cn)
    at = far_ref[0]
    u_read = reader(u_ref)
    put = update_users(u_read, reader(um_ref), u1_ref, um1_ref)
    ga = group_pass(0, u_read, u_ref.shape[0], split(at), prep, put)
    at1, amt1 = adagrad(at, far_ref[1], ga)
    ato_ref[...], amto_ref[...] = second_group(u1_ref, at1, amt1, prep, gh_ref, gl_ref, ah_ref, al_ref)


def pick_kernel(
    ue_ref, ume_ref, users_ref, ads_ref, ato_ref, amto_ref, mh, cu, cn,
    un_ref, umn_ref, atn_ref, amtn_ref, u1_ref, um1_ref,
):
    odd = on_odd_core()
    at = jnp.where(odd, ato_ref[...], ads_ref[0])
    amt = jnp.where(odd, amto_ref[...], ads_ref[1])
    u_read, um_read = picker(odd, ue_ref, users_ref.at[0]), picker(odd, ume_ref, users_ref.at[1])
    atn_ref[...], amtn_ref[...] = meeting(
        u_read, um_read, at, amt, (mh, cu, cn), u1_ref, um1_ref, un_ref, umn_ref
    )


def gradient_kernel(u_ref, at_ref, mh, cu, cn, gu_ref, ga_ref):
    def put(rows, grad):
        gu_ref[rows, :] = grad

    ga_ref[...] = group_pass(0, reader(u_ref), u_ref.shape[0], split(at_ref[...]), (mh, cu, cn), put)


def last_end_kernel(
    u_ref, um_ref, at_ref, amt_ref, gu_ref, ga_ref, mh, cu, cn, ads_ref, uo_ref, umo_ref, u1_ref, um1_ref,
):
    u1_ref[...], um1_ref[...] = adagrad(u_ref[...], um_ref[...], gu_ref[...])
    at1, amt1 = adagrad(at_ref[...], amt_ref[...], ga_ref[...])
    put = update_users(reader(u1_ref), reader(um1_ref), uo_ref, umo_ref)
    ga = group_pass(1, reader(u1_ref), u1_ref.shape[0], split(at1), (mh, cu, cn), put)
    ads_ref[0], ads_ref[1] = adagrad(at1, amt1, ga)


def users_kernel(u_ref, um_ref, gh_ref, gl_ref, ah_ref, al_ref, uo_ref, umo_ref):
    put = update_users(reader(u_ref), reader(um_ref), uo_ref, umo_ref)
    at_hl = ah_ref[...], al_ref[...]
    for r in range(0, u_ref.shape[0], BLOCK):
        rows = pl.ds(r, BLOCK)
        put(rows, dot3((gh_ref[rows, :], gl_ref[rows, :]), at_hl, 1, 1))


def prepare_kernel(rnd, pack, after_ref, pu, pa, ng, mh, cu, cn, lists_ref):
    prepare_round(rnd, pu, pa, ng, mh.shape[1], mh.shape[2], (mh, cu, cn))
    pack_lists(pack, pu, pa, ng, lists_ref)


def prepare_both_kernel(
    rnd, after_ref, lists_ref, pu_hbm, pa_hbm, ng_hbm, mh, cu, cn, mh2, cu2, cn2, pu, pa, ng, sems,
):
    copies = fetch_indices(pu_hbm, pa_hbm, ng_hbm, pu, pa, ng, sems, away=True)
    groups, users, ads = mh.shape
    n = ng_hbm.shape[-1]
    size = pu_hbm.shape[-1] // groups
    for g in range(groups):
        cols = pl.ds(g * size, size)
        negs = lists_ref[2 + g : 3 + g, pl.ds(0, n)]
        prepare(g, lists_ref[0:1, cols], lists_ref[1:2, cols], negs, users, ads, mh2, cu2, cn2)
    for c in copies:
        c.wait()
    prepare_round(rnd, pu, pa, ng, users, ads, (mh, cu, cn))


def call(kernel, ins, outs, scratch=(), hbm=0, name=None, out_place=pltpu.VMEM):
    vmem = pl.BlockSpec(memory_space=pltpu.VMEM)
    split_at = len(ins) - hbm
    far = [pltpu.with_memory_space_constraint(x, pltpu.HBM) for x in ins[split_at:]]
    return pl.pallas_call(
        kernel,
        out_shape=outs,
        in_specs=[vmem] * split_at + [pl.BlockSpec(memory_space=pltpu.HBM)] * hbm,
        out_specs=[pl.BlockSpec(memory_space=out_place)] * len(outs),
        scratch_shapes=list(scratch),
        compiler_params=pltpu.CompilerParams(vmem_limit_bytes=VMEM_LIMIT),
        cost_estimate=pl.CostEstimate(flops=1, bytes_accessed=1, transcendentals=0),
        name=name,
    )(*ins[:split_at], *far)


def users_out_kernel(u_ref, after_hbm, u_hbm, sems):
    size = u_ref.shape[0] // PARTS_OUT
    copies = []
    for k in range(PARTS_OUT):
        rows = pl.ds(k * size, size)
        copies.append(pltpu.make_async_copy(u_ref.at[rows, :], u_hbm.at[rows, :], sems.at[k]))
        copies[-1].start()
    for c in copies:
        c.wait()


def ads_out_kernel(ads_ref, a_hbm, am_hbm, turned, sems):
    size = turned.shape[1] // PARTS_OUT
    copies = []
    for t, out_hbm in enumerate((a_hbm, am_hbm)):
        for k in range(PARTS_OUT):
            rows = pl.ds(k * size, size)
            turned[t, rows, :] = ads_ref[t, :, rows].T
            copies.append(pltpu.make_async_copy(turned.at[t, rows, :], out_hbm.at[rows, :], sems.at[t * PARTS_OUT + k]))
            copies[-1].start()
    for c in copies:
        c.wait()


def move(arrays, *kinds):
    blocks, cycles = lax.axis_size("blk"), lax.axis_size("pair")
    route = []
    for b in range(blocks):
        for p in range(cycles):
            steps, flip = kinds[b % len(kinds)]
            to = (b + steps) % blocks, p ^ (cycles // 2 if flip else 0)
            route.append((b * cycles + p, to[0] * cycles + to[1]))
    return tuple(lax.ppermute(x, AXES, route) for x in arrays)


def local(users, user_moms, ads, ad_moments, pos_user, pos_ad, neg_ad):
    nu, d = users.shape
    na = ads.shape[0]
    rounds, groups, n = neg_ad.shape[2:]
    edges = pos_user.shape[3]
    indices = (pos_user, pos_ad, neg_ad)

    def shape(*dims, dtype=F32):
        return jax.ShapeDtypeStruct(dims, dtype)

    table_u, table_a = shape(nu, d), shape(d, na)
    parts = [shape(nu, na, dtype=BF16)] * 2 + [shape(d, na, dtype=BF16)] * 2
    index_scratch = [
        pltpu.VMEM((rounds, edges), jnp.int32),
        pltpu.VMEM((rounds, edges), jnp.int32),
        pltpu.VMEM((rounds, groups, n), jnp.int32),
    ]
    sems = pltpu.SemaphoreType.DMA((3,))
    prep_shapes = [shape(groups, nu, na, dtype=BF16), shape(groups, nu, 128), shape(groups, 8, na)]
    prep_scratch = [pltpu.VMEM(s.shape, s.dtype) for s in prep_shapes]

    def update(u, um, g):
        return call(users_kernel, (u, um, *g), [table_u, table_u], name="users_update")

    stay, away = (0, False), (0, True)
    both_u, both_a = shape(2, nu, d), shape(2, d, na)
    users_scratch = [pltpu.VMEM((nu, d), F32)] * 2
    own_lists = [shape(rounds, edges, dtype=jnp.int32)] * 2 + [shape(rounds, groups, n, dtype=jnp.int32)]
    u, um, ads_now, *rest = call(
        first_round_kernel,
        (*indices, users, ads, user_moms, ad_moments),
        [table_u, table_u, both_a, *parts, *own_lists],
        [*prep_scratch, *users_scratch, *[pltpu.VMEM((na, d), F32)] * 2, sems, pltpu.SemaphoreType.DMA((4,))],
        hbm=7, name="round_first",
    )
    g, own_lists = rest[: len(parts)], rest[len(parts) :]
    (near,) = move((ads_now,), (1, False), (-1, False))
    (far,) = move((ads_now,), (1, False), (1, False))
    u, um = update(u, um, g)
    *prep, lists = call(
        functools.partial(prepare_kernel, 1, rounds - 1), (um, *own_lists),
        prep_shapes + [shape(8, max(edges, n), dtype=jnp.int32)], name="counts_1",
    )
    (lists,) = move((lists,), (-4, False), stay, stay, stay)

    ads_early, after = call(early_kernel, (u, um, near, *prep), [both_a, both_u], users_scratch, name="round_early")
    (ads_early,) = move((ads_early,), (1, False), (1, True))
    (users_early,) = move((after,), stay, away)

    u, um, at, amt, *g = call(
        late_kernel, (u, um, far, *prep, after, lists), [table_u, table_u, table_a, table_a, *parts], name="round_late",
    )
    ads_late = move((at, amt), (1, False), (-1, False))
    u, um = update(u, um, g)
    preps = call(
        functools.partial(prepare_both_kernel, 2), (um, lists, *indices), prep_shapes * 2, [*index_scratch, sems], hbm=3,
        name="counts_23",
    )
    prep, prep_last = preps[: len(prep_shapes)], preps[len(prep_shapes) :]

    u, um, at, amt = call(
        pick_kernel, (u, um, users_early, ads_early, *ads_late, *prep), [table_u, table_u, table_a, table_a],
        users_scratch, name="round_pick",
    )
    u, um = move((u, um), (-4, False), away, stay, away)
    at, amt = move((at, amt), (1, False), (1, True), (1, False), (-3, True))
    gu, ga = call(gradient_kernel, (u, at, *prep_last), [table_u, table_a], name="round_last_gradients")
    ads_now, u, um = call(
        last_end_kernel, (u, um, at, amt, gu, ga, *prep_last), [both_a, table_u, table_u], users_scratch, name="round_last_end",
    )
    (ads_now,) = move((ads_now,), (1, True), (-3, True), (-3, True), (-3, True))
    u, um = move((u, um), (4, False), stay, stay, stay)
    out_sems = pltpu.SemaphoreType.DMA((2 * PARTS_OUT,))
    a, am = call(
        ads_out_kernel, (ads_now,), [pltpu.HBM((na, d), F32)] * 2, [pltpu.VMEM((2, na, d), F32), out_sems],
        name="ads_out", out_place=pltpu.HBM,
    )
    def users_out(x, after):
        return call(
            users_out_kernel, (x, after), [pltpu.HBM((nu, d), F32)], [pltpu.SemaphoreType.DMA((PARTS_OUT,))], hbm=1,
            name="users_out", out_place=pltpu.HBM,
        )[0]

    u = users_out(u, am)
    um = users_out(um, u)
    return u, um, a, am


def solution(mesh):
    rows = P(AXES, None)
    return jax.shard_map(
        local,
        mesh=mesh,
        in_specs=(rows, rows, rows, rows, P("blk", None, None, None), P("blk", None, None, None), P("blk", None, None, None, None)),
        out_specs=(rows, rows, rows, rows),
        check_vma=False,
    )
```
